128 devices in a mesh: row: 8 (over z, core), height: 16 (over y, x).
Axes of the slice: x: 4, y: 4, z: 4, core: 2. Of those that a mesh axis runs over, the one named last changes fastest.
Arguments:
- heat_source_points: float32 [8, 8, 8, 8, 16, 128], P(None, None, None, 'row', 'height'), may hold values from -6 to 6
- conductivity: float32 [8, 16, 128], P('row', 'height'), may hold values from 0.5 to 8
- solid_element_marks: int32 [8, 16, 128], P('row', 'height'), may hold values 0 or 1
- face_owner: int32 [65536, 1], P(('row', 'height')), may hold values from 0 to 127; in each aligned block of 512 rows (0 to 511, 512 to 1023, ...) at most 16 rows name the same one
- face_element: int32 [65536], P(('row', 'height')), may hold values from 0 to 127
- face_side: int32 [65536], P(('row', 'height')), may hold values from 0 to 5
- owner_element: int32 [65536], P(('row', 'height')), may hold values from 0 to 127
Outputs:
- temperature: float32 [8, 8, 8, 8, 16, 128], P(None, None, None, 'row', 'height')
- residual: float32 [8, 8, 8, 8, 16, 128], P(None, None, None, 'row', 'height')
- interface_load: float32 [128, 8, 16, 128], P(None, 'row', 'height')
The draws below stay inside these ranges and needn't reach their ends.
Inputs may be any that keep to these rules, and one draw needn't show every extreme that they name: `face_owner`: among the 512 faces listed on one device, at most 16 name the same owner device, and some device reaches 16.
All inputs are finite; a program needn't handle non-finite values. No bound on the sum of `solid_element_marks` on one device may be relied on, other than what follows from the above.
Results may differ from the reference program's by a relative error of at most 0.0017.
Values sent between devices are 32-bit elements; how exact they have to be, the bound alone decides.
No kernel may reach another device: no remote copies, remote signals or barrier semaphores. Data moves between devices by JAX's collectives and lax.ppermute only.
A program may use at most 128 MiB of HBM per device.

```python
import math
import jax
import jax.numpy as jnp
import numpy as np
from jax import lax

ELEMENT_POINTS = 8
EXD = 1
EZD = 1
ELEMENTS_AISLE = 128
ITERS = 8
F_DEV = 512
ELEMENTS_ROW_DIR = 8
ELEMENTS_UPWARD = 16
ELEM_DEV = 128
FACES = 65536
CAP = 16
N_HEIGHT = 16
DEVICES = 128


def with_ends(entries, rng, least, largest):
    extent = entries.shape
    index_at = [jax.random.randint(jax.random.fold_in(rng, axis), (), 0, extent[axis]) for axis in range(len(extent))]
    entries = entries.at[tuple(index_at)].set(least)
    longest = extent.index(max(extent))
    index_at[longest] = (index_at[longest] + 1) % extent[longest]
    return entries.at[tuple(index_at)].set(largest)


def block_scale(stream_key, dims, shards, low, largest):
    gain = 1.0
    for dim, shards_of in shards:
        draws = jax.random.uniform(jax.random.fold_in(jax.random.fold_in(stream_key, 6), dim), (shards_of,), jnp.float32, low / len(shards), largest / len(shards))
        gain = gain * jnp.repeat(jnp.exp(draws), dims[dim] // shards_of).reshape((-1,) + (1,) * (len(dims) - 1 - dim))
    return gain


def shared_out(rng, own, number, rows, amount, top, bound, skew):
    ranking = jax.random.permutation(rng, amount)
    crowded, common = shares(amount, rows * top, bound, skew, True), shares(amount, rows * top, bound, skew, False)
    places = jnp.arange(amount)

    def named(lengths, offset_by):
        used = int((lengths > 0).sum())
        fixed = max(1, used // 4)
        shifted = fixed + (places - fixed + offset_by * (used - fixed)) % max(1, amount - fixed)
        return jnp.zeros((amount,), jnp.int32).at[ranking[jnp.where(places < fixed, places, shifted)]].set(jnp.asarray(lengths, jnp.int32))

    lengths = jnp.where(number % 4 == 0, named(crowded, number // 4), named(common, number - number // 4 - 1))
    mixed = jax.random.permutation(jax.random.fold_in(own, 3), amount)
    donor, sink = mixed[0:amount // 2 * 2:2], mixed[1:amount // 2 * 2:2]
    room = jnp.minimum(lengths[donor] - 1, bound - lengths[sink]) // 2
    room = jnp.where((donor == ranking[0]) | (sink == ranking[0]) | (lengths[sink] == 0), 0, jnp.maximum(room, 0))
    shifted = jax.random.randint(jax.random.fold_in(own, 4), (amount // 2,), 0, 1 << 20) % (room + 1)
    lengths = lengths.at[donor].add(-shifted).at[sink].add(shifted)
    labels = jnp.searchsorted(jnp.cumsum(lengths), jnp.arange(rows * top), side="right").astype(jnp.int32)
    grid = labels.reshape(top, rows).T
    grid = grid[jax.random.permutation(jax.random.fold_in(own, 1), rows)]
    offset_by = jax.random.randint(jax.random.fold_in(own, 2), (rows, 1), 0, top)
    return jnp.take_along_axis(grid, (jnp.arange(top)[None, :] + offset_by) % top, axis=1)


def shares(number_of, total, limit, skew, full):
    weights = [(1 << 20) // math.isqrt(standing ** skew) + 1 for standing in range(1, number_of + 1)]
    largest = limit if full else min(limit, max(-(-total // number_of), total * weights[0] // sum(weights)))
    least = 1 if total - largest >= number_of - 1 else 0
    holding, spare = [largest] + [least] * (number_of - 1), total - largest - least * (number_of - 1)
    while spare > 0:
        free = [i for i in range(1, number_of) if holding[i] < largest] or [i for i in range(1, number_of) if holding[i] < limit]
        whole, budget = sum([weights[i] for i in free]), spare
        for i in free:
            addition = min(limit - holding[i], max(1, budget * weights[i] // whole), spare)
            holding[i] = holding[i] + addition
            spare = spare - addition
    return np.array(holding)


def scatter_about(rng, shape, deviation, reach, split=(), held_as=jnp.bfloat16):
    values = deviation * jax.random.normal(rng, shape, jnp.float32)
    if split:
        values = values * block_scale(rng, shape, split, -0.22, 0.18)
    return jnp.clip(values, -reach, reach).astype(held_as)


def setup_inputs(seed: int = 0) -> dict:
    key_list = jax.random.split(jax.random.key(seed), 8)
    heat_source_points = scatter_about(key_list[0], (ELEMENT_POINTS, ELEMENT_POINTS, ELEMENT_POINTS, ELEMENTS_ROW_DIR, ELEMENTS_UPWARD, ELEMENTS_AISLE), 1.0, 6.0, ((3, 8), (4, 16)), jnp.float32)
    conductivity = jnp.clip(jnp.exp(math.log(8.0) - 2.7725887 * jax.random.uniform(key_list[1], (ELEMENTS_ROW_DIR, ELEMENTS_UPWARD, ELEMENTS_AISLE), jnp.float32) ** block_scale(key_list[1], (ELEMENTS_ROW_DIR, ELEMENTS_UPWARD, ELEMENTS_AISLE), ((0, 8), (1, 16)), -0.2, 0.2)), 0.5, 8.0)
    solid_element_marks = with_ends((jax.random.randint(key_list[2], (ELEMENTS_ROW_DIR, ELEMENTS_UPWARD, ELEMENTS_AISLE), 0, 4) < 1).astype(jnp.int32), jax.random.fold_in(key_list[2], 1), 0, 1)
    face_owner_keys = jax.random.split(jax.random.fold_in(key_list[3], 1), FACES // F_DEV)
    face_owner_turns = jax.random.permutation(jax.random.fold_in(key_list[3], 3), FACES // F_DEV)
    face_owner = jax.vmap(lambda own, number: shared_out(jax.random.fold_in(key_list[3], 2), own, number, F_DEV, DEVICES, 1, CAP, 2))(face_owner_keys, face_owner_turns).reshape((FACES, 1))
    face_element = with_ends(jax.random.randint(key_list[4], (FACES,), 0, ELEM_DEV), jax.random.fold_in(key_list[4], 1), 0, ELEM_DEV - 1).astype(jnp.int32)
    face_side = with_ends(jax.random.randint(key_list[5], (FACES,), 0, 6), jax.random.fold_in(key_list[5], 1), 0, 5).astype(jnp.int32)
    owner_element = with_ends(jax.random.randint(key_list[6], (FACES,), 0, ELEM_DEV), jax.random.fold_in(key_list[6], 1), 0, ELEM_DEV - 1).astype(jnp.int32)
    return dict(heat_source_points=heat_source_points, conductivity=conductivity, solid_element_marks=solid_element_marks, face_owner=face_owner, face_element=face_element, face_side=face_side, owner_element=owner_element)


HEAT_AIR = 0.02
HEAT_SOLID = 0.08
GLL_INNER = (-0.8717401485096066, -0.5917001814331423, -0.2092992179024789, 0.2092992179024789, 0.5917001814331423, 0.8717401485096066)
FORWARD_FORMS = ('ai,ijkxzy->ajkxzy', 'aj,ijkxzy->iakxzy', 'ak,ijkxzy->ijaxzy')
BACKWARD_FORMS = ('ai,ajkxzy->ijkxzy', 'aj,iakxzy->ijkxzy', 'ak,ijaxzy->ijkxzy')

def legendre_values(points_in, degree):
    before = points_in * 0.0 + 1.0
    current = points_in * 1.0
    for order_now in range(1, degree):
        following = ((2 * order_now + 1) * points_in * current - order_now * before) / (order_now + 1)
        before = current
        current = following
    return current

def gll_tables():
    poly_order = 7
    gll_nodes = np.array((-1.0,) + GLL_INNER + (1.0,))
    edge_values = legendre_values(gll_nodes, poly_order)
    gll_weights = 2.0 / (poly_order * (poly_order + 1) * edge_values ** 2)
    diff_table = np.zeros((8, 8))
    for row_index in range(8):
        for col_index in range(8):
            if row_index != col_index:
                diff_table[row_index, col_index] = edge_values[row_index] / (edge_values[col_index] * (gll_nodes[row_index] - gll_nodes[col_index]))
    diff_table[0, 0] = -poly_order * (poly_order + 1) / 4.0
    diff_table[7, 7] = poly_order * (poly_order + 1) / 4.0
    return (gll_weights, diff_table)

def operators():
    gll_weights, diff_table = gll_tables()
    weights = jnp.asarray(gll_weights, jnp.float32)
    diff_mat = jnp.asarray(diff_table, jnp.float32)
    mass_points = weights[:, None, None] * weights[None, :, None] * weights[None, None, :]
    stiff_diag = jnp.asarray(np.sum(diff_table ** 2 * gll_weights[:, None], axis=0), jnp.float32)
    return (weights, diff_mat, mass_points[:, :, :, None, None, None], stiff_diag)

def derivative(field_in, diff_mat, direction):
    return jnp.einsum(FORWARD_FORMS[direction], diff_mat, field_in, precision=lax.Precision.HIGHEST)

def local_apply(field_in, conduct, capacity, diff_mat, mass_table):
    stiffness = jnp.zeros_like(field_in)
    for direction in range(3):
        gradient = derivative(field_in, diff_mat, direction)
        stiffness = stiffness + jnp.einsum(BACKWARD_FORMS[direction], diff_mat, mass_table * gradient, precision=lax.Precision.HIGHEST)
    return conduct * stiffness + capacity * mass_table * field_in

def local_diagonal(conduct, capacity, weights, stiff_diag):
    part_x = stiff_diag[:, None, None] * weights[None, :, None] * weights[None, None, :]
    part_z = weights[:, None, None] * stiff_diag[None, :, None] * weights[None, None, :]
    part_y = weights[:, None, None] * weights[None, :, None] * stiff_diag[None, None, :]
    mass_points = weights[:, None, None] * weights[None, :, None] * weights[None, None, :]
    stiff_sum = (part_x + part_z + part_y)[:, :, :, None, None, None]
    return conduct * stiff_sum + capacity * mass_points[:, :, :, None, None, None]

def reciprocal_point_sharing(count_x, count_z, count_y, start_x, start_z, total_x, total_z):
    points = jnp.arange(8, dtype=jnp.int32)

    def along_axis(count_el, start_at, total_el):
        global_index = start_at + jnp.arange(count_el, dtype=jnp.int32)
        low_face = (points[:, None] == 0) & (global_index[None, :] > 0)
        high_face = (points[:, None] == 7) & (global_index[None, :] < total_el - 1)
        return 1.0 + low_face.astype(jnp.float32) + high_face.astype(jnp.float32)
    mult_x = along_axis(count_x, start_x, total_x)[:, None, None, :, None, None]
    mult_z = along_axis(count_z, start_z, total_z)[None, :, None, None, :, None]
    mult_y = along_axis(count_y, 0, count_y)[None, None, :, None, None, :]
    return 1.0 / (mult_x * mult_z * mult_y)

def pair_faces(low_face, high_face, elem_dim):
    stacked = jnp.stack([low_face, high_face], axis=elem_dim + 1)
    new_shape = list(low_face.shape)
    new_shape[elem_dim] = 2 * new_shape[elem_dim]
    return stacked.reshape(new_shape)

def pair_sums(padded, elem_dim, count_el):

    def pair_block(begin_at):
        slab_part = lax.slice_in_dim(padded, begin_at, begin_at + 2 * count_el, axis=elem_dim)
        new_shape = slab_part.shape[:elem_dim] + (count_el, 2) + slab_part.shape[elem_dim + 1:]
        return jnp.sum(slab_part.reshape(new_shape), axis=elem_dim + 1)
    return (pair_block(0), pair_block(2))

def pad_zero(array_in, elem_dim):
    widths = [(0, 0)] * array_in.ndim
    widths[elem_dim] = (1, 1)
    return jnp.pad(array_in, widths)

def assemble(field_in, extend_x, extend_z):
    count_x = field_in.shape[3]
    padded = extend_x(pair_faces(field_in[0], field_in[7], 2))
    low_new, high_new = pair_sums(padded, 2, count_x)
    field_in = field_in.at[0].set(low_new).at[7].set(high_new)
    count_z = field_in.shape[4]
    padded = extend_z(pair_faces(field_in[:, 0], field_in[:, 7], 3))
    low_new, high_new = pair_sums(padded, 3, count_z)
    field_in = field_in.at[:, 0].set(low_new).at[:, 7].set(high_new)
    count_y = field_in.shape[5]
    padded = pad_zero(pair_faces(field_in[:, :, 0], field_in[:, :, 7], 4), 4)
    low_new, high_new = pair_sums(padded, 4, count_y)
    return field_in.at[:, :, 0].set(low_new).at[:, :, 7].set(high_new)

def coarse_terms(conduct_col, capacity_col):
    cond_t = jnp.transpose(conduct_col, (0, 2, 1))
    cap_t = jnp.transpose(capacity_col, (0, 2, 1))
    link_val = 2.0 * cond_t[..., 1:] * cond_t[..., :-1] / (cond_t[..., 1:] + cond_t[..., :-1])
    zero_end = jnp.zeros_like(link_val[..., :1])
    lower_band = jnp.concatenate([zero_end, -link_val], axis=-1)
    upper_band = jnp.concatenate([-link_val, zero_end], axis=-1)
    main_band = 8.0 * cap_t + jnp.concatenate([zero_end, link_val], axis=-1) + jnp.concatenate([link_val, zero_end], axis=-1)
    return (lower_band, main_band, upper_band)

def coarse_solve(bands, restricted_col):
    rhs_t = jnp.transpose(restricted_col, (0, 2, 1))[..., None]
    solved = lax.linalg.tridiagonal_solve(bands[0], bands[1], bands[2], rhs_t)[..., 0]
    return jnp.transpose(solved, (0, 2, 1))

def face_rows(field_in, conduct, diff_mat):
    grad_x = derivative(field_in, diff_mat, 0)
    grad_z = derivative(field_in, diff_mat, 1)
    grad_y = derivative(field_in, diff_mat, 2)
    rest_shape = field_in.shape[3:]
    flux_planes = [conduct * grad_x[0], -conduct * grad_x[7], conduct * grad_z[:, 0], -conduct * grad_z[:, 7], conduct * grad_y[:, :, 0], -conduct * grad_y[:, :, 7]]
    temp_planes = [field_in[0], field_in[7], field_in[:, 0], field_in[:, 7], field_in[:, :, 0], field_in[:, :, 7]]
    flux_all = jnp.stack([plane.reshape((64,) + rest_shape) for plane in flux_planes])
    temp_all = jnp.stack([plane.reshape((64,) + rest_shape) for plane in temp_planes])
    return jnp.concatenate([flux_all, temp_all], axis=1)

def element_coords(device_id, local_id):
    row_pos = device_id // N_HEIGHT
    height_pos = device_id % N_HEIGHT
    coord_x = row_pos * EXD + local_id // (EZD * ELEMENTS_AISLE)
    coord_z = height_pos * EZD + local_id // ELEMENTS_AISLE % EZD
    coord_y = local_id % ELEMENTS_AISLE
    return (coord_x, coord_z, coord_y)

def reference(heat_source_points, conductivity, solid_element_marks, face_owner, face_element, face_side, owner_element):
    weights, diff_mat, mass_table, stiff_diag = operators()
    capacity = jnp.where(solid_element_marks == 1, HEAT_SOLID, HEAT_AIR).astype(jnp.float32)
    reciprocal_sharing = reciprocal_point_sharing(ELEMENTS_ROW_DIR, ELEMENTS_UPWARD, ELEMENTS_AISLE, 0, 0, ELEMENTS_ROW_DIR, ELEMENTS_UPWARD)

    def full_assemble(values_in):
        return assemble(values_in, lambda array_in: pad_zero(array_in, 2), lambda array_in: pad_zero(array_in, 3))
    inv_diag = 1.0 / full_assemble(local_diagonal(conductivity, capacity, weights, stiff_diag))
    bands = coarse_terms(conductivity, capacity)

    def apply_op(values_in):
        return full_assemble(local_apply(values_in, conductivity, capacity, diff_mat, mass_table))

    def precondition(resid):
        restricted = jnp.sum(resid * reciprocal_sharing, axis=(0, 1, 2))
        coarse_val = coarse_solve(bands, restricted)
        return resid * inv_diag + full_assemble(coarse_val[None, None, None] * reciprocal_sharing)

    def inner_product(left_vec, right_vec):
        return jnp.sum(left_vec * right_vec * reciprocal_sharing)
    rhs_vec = full_assemble(mass_table * heat_source_points)
    solution = jnp.zeros_like(rhs_vec)
    residual = rhs_vec
    precond = precondition(residual)
    direction_vec = precond
    rz_now = inner_product(residual, precond)
    for iteration in range(ITERS):
        image_vec = apply_op(direction_vec)
        step_len = rz_now / inner_product(direction_vec, image_vec)
        solution = solution + step_len * direction_vec
        residual = residual - step_len * image_vec
        if iteration + 1 < ITERS:
            precond = precondition(residual)
            rz_next = inner_product(residual, precond)
            direction_vec = precond + rz_next / rz_now * direction_vec
            rz_now = rz_next
    combined = face_rows(solution, conductivity, diff_mat)
    source_dev = (jnp.arange(FACES, dtype=jnp.int32) // F_DEV).astype(jnp.int32)
    src_x, src_z, src_y = element_coords(source_dev, face_element)
    face_payload = combined[face_side, :, src_x, src_z, src_y]
    target_along_x, target_along_z, target_along_y = element_coords(face_owner[:, 0], owner_element)
    load_running_sum = jnp.zeros((ELEMENTS_ROW_DIR, ELEMENTS_UPWARD, ELEMENTS_AISLE, 128), jnp.float32).at[target_along_x, target_along_z, target_along_y].add(face_payload)
    interface_load = jnp.transpose(load_running_sum, (3, 0, 1, 2))
    return (solution, residual, interface_load)
```

```python
import functools

import jax
import jax.numpy as jnp
import numpy as np
from jax import lax
from jax.experimental import pallas as pl
from jax.experimental.pallas import tpu as pltpu
from jax.sharding import PartitionSpec as P

ITERS = 8
HEAT_AIR = 0.02
HEAT_SOLID = 0.08
GLL_INNER = (
    -0.8717401485096066,
    -0.5917001814331423,
    -0.2092992179024789,
    0.2092992179024789,
    0.5917001814331423,
    0.8717401485096066,
)
F32 = jnp.float32
NX, NZ, NY = 8, 16, 128
FIELD = (8, 8, 8, NY)
FACE = (8, 8, NY)
COARSE = (NZ, NX, NY)


def legendre_values(points_in, degree):
    before = points_in * 0.0 + 1.0
    current = points_in * 1.0
    for order_now in range(1, degree):
        following = ((2 * order_now + 1) * points_in * current - order_now * before) / (
            order_now + 1
        )
        before = current
        current = following
    return current


def gll_tables():
    poly_order = 7
    gll_nodes = np.array((-1.0,) + GLL_INNER + (1.0,))
    edge_values = legendre_values(gll_nodes, poly_order)
    gll_weights = 2.0 / (poly_order * (poly_order + 1) * edge_values**2)
    diff_table = np.zeros((8, 8))
    for row_index in range(8):
        for col_index in range(8):
            if row_index != col_index:
                diff_table[row_index, col_index] = edge_values[row_index] / (
                    edge_values[col_index] * (gll_nodes[row_index] - gll_nodes[col_index])
                )
    diff_table[0, 0] = -poly_order * (poly_order + 1) / 4.0
    diff_table[7, 7] = poly_order * (poly_order + 1) / 4.0
    return (gll_weights, diff_table)


W_, D_ = gll_tables()
K_ = D_.T @ np.diag(W_) @ D_
S_ = np.sum(D_**2 * W_[:, None], axis=0)
W = [float(v) for v in W_]
SD = [float(v) for v in S_]
E = 7


def kvec(vals):
    k = lax.broadcasted_iota(jnp.int32, (8, NY), 0)
    out = jnp.full((8, NY), float(vals[0]), F32)
    for n in range(1, 8):
        out = jnp.where(k == n, jnp.float32(float(vals[n])), out)
    return out


def apply1d(v, mat):
    ev = [v[a] + v[7 - a] for a in range(4)]
    od = [v[a] - v[7 - a] for a in range(4)]
    out = [None] * 8
    for i in range(4):
        s = d = None
        for a in range(4):
            cs = float(0.5 * (mat[i, a] + mat[i, 7 - a]))
            cd = float(0.5 * (mat[i, a] - mat[i, 7 - a]))
            s = cs * ev[a] if s is None else s + cs * ev[a]
            d = cd * od[a] if d is None else d + cd * od[a]
        out[i] = s + d
        out[7 - i] = s - d
    return out


def place(pos_ref):
    ix, iz = pos_ref[0], pos_ref[1]
    has = (ix > 0, ix < NX - 1, iz > 0, iz < NZ - 1)
    frac = tuple(jnp.where(h, jnp.float32(0.5), jnp.float32(1.0)) for h in has)
    even = (lax.rem(ix, 2) == 0, lax.rem(iz, 2) == 0)
    return ix, iz, has, frac, even


def own_mult():
    k = lax.broadcasted_iota(jnp.int32, (8, NY), 0)
    y = lax.broadcasted_iota(jnp.int32, (8, NY), 1)
    shared = ((k == 0) & (y > 0)) | ((k == E) & (y < NY - 1))
    return jnp.where(shared, jnp.float32(0.5), jnp.float32(1.0))


def field_sum(get, frac):
    total = None
    for i in range(8):
        mid = get(i, 1)
        for j in range(2, 7):
            mid = mid + get(i, j)
        row = mid + frac[2] * get(i, 0) + frac[3] * get(i, E)
        if i == 0:
            row = frac[0] * row
        elif i == E:
            row = frac[1] * row
        total = row if total is None else total + row
    return total


def assemble_aisle(ref):
    low, high = ref[:, :, 0, :], ref[:, :, E, :]
    y = lax.broadcasted_iota(jnp.int32, FACE, 2)
    ref[:, :, 0, :] = low + jnp.where(y > 0, pltpu.roll(high, 1, 2), 0.0)
    ref[:, :, E, :] = high + jnp.where(y < NY - 1, pltpu.roll(low, NY - 1, 2), 0.0)


def add_faces_x(ref, got, has, even):
    a, b = got[0][...], got[1][...]
    ref[0] = ref[0] + jnp.where(has[0], jnp.where(even[0], b, a), 0.0)
    ref[E] = ref[E] + jnp.where(has[1], jnp.where(even[0], a, b), 0.0)


def add_faces_z(ref, got, has, even):
    a, b = got[0][...], got[1][...]
    ref[:, 0] = ref[:, 0] + jnp.where(has[2], jnp.where(even[1], b, a), 0.0)
    ref[:, E] = ref[:, E] + jnp.where(has[3], jnp.where(even[1], a, b), 0.0)


def put_pair(even, low, high, out):
    out[0][...] = jnp.where(even, high, low)
    out[1][...] = jnp.where(even, low, high)


def local_operator(z_ref, f_ref, nb_ref, even, msgs):
    wk = kvec(W)
    kt, ct = nb_ref[4], nb_ref[13]
    kw, cw = kt * wk, ct * wk
    for kk, rows in enumerate(apply1d([z_ref[:, :, c, :] for c in range(8)], K_)):
        f_ref[:, :, kk, :] = rows
    corner = ((0, 0), (0, E), (E, 0), (E, E))
    xc, yc, zc = {}, {}, {}
    for i, j in corner:
        yc[i, j] = f_ref[i, j]
    for j in range(8):
        v = [z_ref[i, j] for i in range(8)]
        out = apply1d(v, K_)
        kwj = kw * W[j]
        for i in range(8):
            f_ref[i, j] = kwj * out[i] + (W[i] * W[j]) * (kt * f_ref[i, j] + cw * v[i])
        if j in (0, E):
            xc[0, j], xc[E, j] = out[0], out[E]
    for i in range(8):
        out = apply1d([z_ref[i, j] for j in range(8)], K_)
        kwi = kw * W[i]
        for j in range(8):
            f_ref[i, j] = f_ref[i, j] + kwi * out[j]
        if i in (0, E):
            zc[i, 0], zc[i, E] = out[0], out[E]
    w0 = W[0]

    def extra_x(i, j):
        n = 3 if j == 0 else 5
        return nb_ref[n] * (w0 * wk * xc[i, j] + (w0 * w0) * yc[i, j]) + nb_ref[9 + n] * (
            (w0 * w0) * wk * z_ref[i, j]
        )

    def extra_z(i, j):
        n = 1 if i == 0 else 7
        return nb_ref[n] * (w0 * wk * zc[i, j])

    for s in range(8):
        low, high = f_ref[0, s], f_ref[E, s]
        if s in (0, E):
            low, high = low + extra_x(0, s), high + extra_x(E, s)
        msgs[0][s] = jnp.where(even[0], high, low)
        msgs[1][s] = jnp.where(even[0], low, high)
        low, high = f_ref[s, 0], f_ref[s, E]
        if s in (0, E):
            low, high = low + extra_z(s, 0), high + extra_z(s, E)
        msgs[2][s] = jnp.where(even[1], high, low)
        msgs[3][s] = jnp.where(even[1], low, high)


def thomas(cf_ref, rhs):
    dp = []
    for h in range(NZ):
        v = rhs[h] if h == 0 else rhs[h] - cf_ref[h] * dp[h - 1]
        dp.append(v * cf_ref[32 + h])
    for h in range(NZ - 2, -1, -1):
        dp[h] = dp[h] - cf_ref[16 + h] * dp[h + 1]
    return dp


def coarse_dot(a, b):
    acc = None
    for u, v in zip(a, b):
        acc = u * v if acc is None else acc + u * v
    return spread_sum(acc)


def spread_sum(tile):
    row = jnp.broadcast_to(jnp.sum(tile, axis=0, keepdims=True), (8, NY))
    return jnp.broadcast_to(jnp.sum(row, axis=1, keepdims=True), (8, NY))


def shift_pair(v, axis):
    n = v.shape[axis]
    p = lax.broadcasted_iota(jnp.int32, v.shape, axis)
    before = jnp.where(p == 0, v, pltpu.roll(v, 1, axis))
    after = jnp.where(p == n - 1, v, pltpu.roll(v, n - 1, axis))
    return before, after


def spread3(v, before, after):
    return (v, 0.5 * v + 0.25 * (before + after), 0.25 * (before - after))


def gather3(duals, axis):
    m, f, a = duals
    g, h = 0.25 * (f + a), 0.25 * (f - a)
    n = m.shape[axis]
    p = lax.broadcasted_iota(jnp.int32, m.shape, axis)
    up = jnp.where(p == n - 1, h, pltpu.roll(g, n - 1, axis))
    down = jnp.where(p == 0, g, pltpu.roll(h, 1, axis))
    return m + 0.5 * f + up + down


MU = (2.0 - 2.0 * W[0], 2.0 * W[0], 2.0 * W[0])
KS = float(2.0 * (K_[0, 0] + K_[0, 7]))
KA = float(2.0 * (K_[0, 0] - K_[0, 7]))


def stiff3(q):
    d = q[1] - q[0]
    return ((-KS / MU[0]) * d, (KS / MU[1]) * d, (KA / MU[2]) * q[2])


def coarse_operator(d, kc_ref, cc_ref, tmp_ref):
    for h in range(NZ):
        ys = spread3(d[h], *shift_pair(d[h], 1))
        for c in range(3):
            xs = spread3(ys[c], *shift_pair(ys[c], 0))
            for a in range(3):
                tmp_ref[(a * 3 + c) * NZ + h] = xs[a]
    part = []
    for h in range(NZ):
        lo, hi = max(h - 1, 0), min(h + 1, NZ - 1)
        q = {}
        for a in range(3):
            for c in range(3):
                base = (a * 3 + c) * NZ
                zs = spread3(tmp_ref[base + h], tmp_ref[base + lo], tmp_ref[base + hi])
                for b in range(3):
                    q[a, b, c] = zs[b]
        acc = {key: None for key in q}

        def add(key, val):
            acc[key] = val if acc[key] is None else acc[key] + val

        for b in range(3):
            for c in range(3):
                for n, val in enumerate(stiff3([q[a, b, c] for a in range(3)])):
                    add((n, b, c), val)
        for a in range(3):
            for c in range(3):
                for n, val in enumerate(stiff3([q[a, b, c] for b in range(3)])):
                    add((a, n, c), val)
        for a in range(3):
            for b in range(3):
                for n, val in enumerate(stiff3([q[a, b, c] for c in range(3)])):
                    add((a, b, n), val)
        kh, ch = kc_ref[h], cc_ref[h]
        outs = []
        for b in range(3):
            cols = []
            for c in range(3):
                duals = [
                    (MU[a] * MU[b] * MU[c]) * (kh * acc[a, b, c] + ch * q[a, b, c])
                    for a in range(3)
                ]
                cols.append(gather3(duals, 0))
            outs.append(gather3(cols, 1))
        part.append(outs)
    res = []
    for h in range(NZ):
        m, f, _ = part[h]
        v = m + 0.5 * f
        g = lambda n: 0.25 * (part[n][1] + part[n][2])
        l = lambda n: 0.25 * (part[n][1] - part[n][2])
        v = v + (g(h + 1) if h < NZ - 1 else l(h))
        v = v + (l(h - 1) if h > 0 else g(h))
        res.append(v)
    return res


def coarse_row(ref, ix, iz, dx, dz):
    x = jnp.clip(ix + dx, 0, NX - 1)
    z = jnp.clip(iz + dz, 0, NZ - 1)
    return ref[z, pl.ds(x, 1), :]


def aisle_tiles(row, want_stiff):
    c = jnp.broadcast_to(row, (8, NY))
    before, after = shift_pair(c, 1)
    k = lax.broadcasted_iota(jnp.int32, (8, NY), 0)
    low, high = 0.5 * (c + before), 0.5 * (c + after)
    tile = jnp.where(k == 0, low, jnp.where(k == E, high, c))
    if not want_stiff:
        return tile, None
    return tile, kvec(K_[:, 0]) * (low - c) + kvec(K_[:, 7]) * (high - c)


def classes(tiles, reach):
    n = 2 * reach + 1
    m = 2 * n - 3

    def line(vals):
        out = []
        for p in range(m):
            if p % 2 == 0:
                out.append(0.5 * (vals[p // 2] + vals[p // 2 + 1]))
            else:
                out.append(vals[p // 2 + 1])
        return out

    cols = [line(tiles[dx]) for dx in range(n)]
    by_q = [line([cols[dx][q] for dx in range(n)]) for q in range(m)]
    return [[by_q[q][p] for q in range(m)] for p in range(m)]


def cls(i):
    return 0 if i == 0 else (2 if i == E else 1)


def own_prolong(ref, ix, iz):
    tiles = [
        [aisle_tiles(coarse_row(ref, ix, iz, dx, dz), False)[0] for dz in (-1, 0, 1)]
        for dx in (-1, 0, 1)
    ]
    return classes(tiles, 1)


def add_operator_of_prolong(ref, ix, iz, nb_ref, out_ref):
    tv, ty = [], []
    for dx in range(-2, 3):
        pair = [aisle_tiles(coarse_row(ref, ix, iz, dx, dz), True) for dz in range(-2, 3)]
        tv.append([p[0] for p in pair])
        ty.append([p[1] for p in pair])
    v, yv = classes(tv, 2), classes(ty, 2)
    wk = kvec(W)

    def parts(ex, ez):
        p, q = 2 + 2 * ex, 2 + 2 * ez
        n = (ex + 1) * 3 + ez + 1
        kt, ct = nb_ref[n], nb_ref[9 + n]
        kw, cw = kt * wk, ct * wk
        memo = {}

        def once(key, make):
            if key not in memo:
                memo[key] = make()
            return memo[key]

        def along(i, a, b, c):
            return kw * (float(K_[i, 0]) * (a - b) + float(K_[i, 7]) * (c - b))

        def tile(i, j):
            a, b = cls(i), cls(j)
            xt = once(
                ("x", i, b), lambda: along(i, v[p][q + b], v[p + 1][q + b], v[p + 2][q + b])
            )
            zt = once(
                ("z", a, j), lambda: along(j, v[p + a][q], v[p + a][q + 1], v[p + a][q + 2])
            )
            yt = once(("y", a, b), lambda: kt * yv[p + a][q + b] + cw * v[p + a][q + b])
            return W[j] * xt + W[i] * zt + (W[i] * W[j]) * yt

        return tile

    part = {(ex, ez): parts(ex, ez) for ex in (-1, 0, 1) for ez in (-1, 0, 1)}
    for i in range(8):
        for j in range(8):
            acc = out_ref[i, j] + part[0, 0](i, j)
            ex = -1 if i == 0 else (1 if i == E else 0)
            ez = -1 if j == 0 else (1 if j == E else 0)
            if ex:
                acc = acc + part[ex, 0](7 - i, j)
            if ez:
                acc = acc + part[0, ez](i, 7 - j)
            if ex and ez:
                acc = acc + part[ex, ez](7 - i, 7 - j)
            out_ref[i, j] = acc
    return [[v[2 + a][2 + b] for b in range(3)] for a in range(3)]


def make_z(c_ref, ix, iz, r_ref, dinv_ref, z_ref):
    pc = own_prolong(c_ref, ix, iz)
    for i in range(8):
        for j in range(8):
            z_ref[i, j] = r_ref[i, j] * dinv_ref[i, j] + pc[cls(i)][cls(j)]


def coarse_rows_of(got_ref, which):
    return [
        jnp.concatenate([got_ref[r * NZ + h, pl.ds(which, 1), :] for r in range(NX)], axis=0)
        for h in range(NZ)
    ]


def heat_kernel(pos, heat, f, ma, mb):
    _, _, _, _, even = place(pos)
    wk = kvec(W)
    for i in range(8):
        for j in range(8):
            f[i, j] = (W[i] * W[j]) * wk * heat[i, j]
    put_pair(even[0], f[0], f[E], (ma, mb))


def heat_z_kernel(pos, f, ra, rb, out, ma, mb):
    _, _, has, _, even = place(pos)
    out[...] = f[...]
    add_faces_x(out, (ra, rb), has, even)
    put_pair(even[1], out[:, 0], out[:, E], (ma, mb))


def first_rows_kernel(pos, f, ra, rb, kc, marks, owners, out, rows):
    _, _, has, frac, even = place(pos)
    out[...] = f[...]
    add_faces_z(out, (ra, rb), has, even)
    assemble_aisle(out)
    tile = field_sum(lambda i, j: out[i, j], frac) * own_mult()
    restricted = jnp.sum(tile, axis=0, keepdims=True)
    cap = jnp.where(marks[...] == 1, jnp.float32(HEAT_SOLID), jnp.float32(HEAT_AIR))
    block = jnp.concatenate([kc[...], cap, restricted, jnp.zeros((1, NY), F32)], axis=0)
    rows[...] = jnp.broadcast_to(block[None], rows.shape)
    rows[:, 3, :] = owners[...]


def setup_kernel(
    pos, got, r, kc, cc, cf, rc, nb, dinv, z, f, m0, m1, m2, m3, c_tmp
):
    ix, iz, has, frac, even = place(pos)
    k_all, c_all, r_all = (coarse_rows_of(got, n) for n in range(3))
    for h in range(NZ):
        kc[h], cc[h], rc[h] = k_all[h], c_all[h], r_all[h]
    link = [2.0 * k_all[h] * k_all[h + 1] / (k_all[h] + k_all[h + 1]) for h in range(NZ - 1)]
    above = None
    for h in range(NZ):
        main = 8.0 * c_all[h]
        if h > 0:
            main = main + link[h - 1]
        if h < NZ - 1:
            main = main + link[h]
        low = -link[h - 1] if h > 0 else jnp.zeros((NX, NY), F32)
        piv = main if h == 0 else main - low * above
        inv = 1.0 / piv
        above = -link[h] * inv if h < NZ - 1 else jnp.zeros((NX, NY), F32)
        cf[h], cf[16 + h], cf[32 + h] = low, above, inv
    for ex in (-1, 0, 1):
        for ez in (-1, 0, 1):
            n = (ex + 1) * 3 + ez + 1
            there = None
            if ex:
                there = has[0] if ex < 0 else has[1]
            if ez:
                hz = has[2] if ez < 0 else has[3]
                there = hz if there is None else there & hz
            for base, src in ((0, kc), (9, cc)):
                tile = jnp.broadcast_to(coarse_row(src, ix, iz, ex, ez), (8, NY))
                nb[base + n] = tile if there is None else jnp.where(there, tile, 0.0)
    wk, sk = kvec(W), kvec(SD)
    for i in range(8):
        for j in range(8):
            ex = -1 if i == 0 else (1 if i == E else 0)
            ez = -1 if j == 0 else (1 if j == E else 0)
            kt, ct = nb[4], nb[13]
            for n in {4 + 3 * ex, 4 + ez, 4 + 3 * ex + ez} - {4}:
                kt, ct = kt + nb[n], ct + nb[9 + n]
            dinv[i, j] = (
                kt * ((SD[i] * W[j] + W[i] * SD[j]) * wk + (W[i] * W[j]) * sk)
                + ct * ((W[i] * W[j]) * wk)
            )
    assemble_aisle(dinv)
    dinv[...] = 1.0 / dinv[...]
    solved = thomas(cf, r_all)
    for h in range(NZ):
        c_tmp[h] = solved[h]
    make_z(c_tmp, ix, iz, r, dinv, z)
    local_operator(z, f, nb, even, (m0, m1, m2, m3))


def inner_kernel(pos, f, r0, r1, r2, r3, nb, dinv, w1, t, f2, m0, m1, m2, m3):
    _, _, has, _, even = place(pos)
    w1[...] = f[...]
    add_faces_x(w1, (r0, r1), has, even)
    add_faces_z(w1, (r2, r3), has, even)
    assemble_aisle(w1)
    t[...] = w1[...] * dinv[...]
    local_operator(t, f2, nb, even, (m0, m1, m2, m3))


def rows_kernel(first, *refs):
    if first:
        pos, f2, r0, r1, r2, r3, z, r, t, w1, v, rows = refs
    else:
        pos, f2, r0, r1, r2, r3, z, r, t, w1, s1, s2, v, rows = refs
    _, _, has, frac, even = place(pos)
    v[...] = f2[...]
    add_faces_x(v, (r0, r1), has, even)
    add_faces_z(v, (r2, r3), has, even)
    my = own_mult()

    def dot(a, b):
        return field_sum(lambda i, j: a[i, j] * b[i, j], frac)

    tiles = [my * dot(z, r), my * dot(t, r), my * dot(z, w1), my * dot(t, w1), dot(t, v)]
    if not first:
        tiles += [my * dot(z, s1), my * dot(z, s2), my * dot(t, s1), my * dot(t, s2)]
    lines = [jnp.sum(tile, axis=0, keepdims=True) for tile in tiles]
    lines.append(jnp.zeros((16 - len(lines), NY), F32))
    stacked = jnp.concatenate(lines, axis=0)
    totals = jnp.broadcast_to(jnp.sum(stacked, axis=1, keepdims=True), (16, NY))
    lane = lax.broadcasted_iota(jnp.int32, (16, NY), 1)
    at = lax.broadcasted_iota(jnp.int32, (16, NY), 0)
    dots = jnp.sum(jnp.where(lane == at, totals, 0.0), axis=0, keepdims=True)
    g1 = jnp.sum(field_sum(lambda i, j: w1[i, j], frac) * my, axis=0, keepdims=True)
    vt = field_sum(lambda i, j: v[i, j], frac)
    k = lax.broadcasted_iota(jnp.int32, (8, NY), 0)
    y = lax.broadcasted_iota(jnp.int32, (8, NY), 1)
    vlow = jnp.broadcast_to(vt[0:1], (8, NY))
    vhigh = jnp.broadcast_to(vt[7:8], (8, NY))
    vt = vt + jnp.where((k == 0) & (y > 0), pltpu.roll(vhigh, 1, 1), 0.0)
    vt = vt + jnp.where((k == E) & (y < NY - 1), pltpu.roll(vlow, NY - 1, 1), 0.0)
    g2 = jnp.sum(vt * my, axis=0, keepdims=True)
    block = jnp.concatenate([g1, g2, dots, jnp.zeros((1, NY), F32)], axis=0)
    rows[...] = jnp.broadcast_to(block[None], rows.shape)


def step_kernel(first, last, *refs):
    refs = list(refs)
    take = lambda n: [refs.pop(0) for _ in range(n)]
    pos, got, r, z, t, w1, v, dinv, nb, kc, cc, cf, rc = take(13)
    if not first:
        x, p1, p2, s1, s2, rs, wp = take(7)
    xo, ro = take(2)
    if not last:
        p1o, p2o, s1o, s2o, rso, wpo, rco, zo, fo, m0, m1, m2, m3 = take(13)
    ay, c_tmp, tmp = take(3)

    ix, iz, has, frac, even = place(pos)
    total = got[0]
    for d in range(1, NX * NZ):
        total = total + got[d]
    dots = jnp.broadcast_to(total[2:3], (8, NY))
    lane = lax.broadcasted_iota(jnp.int32, (8, NY), 1)

    def pick(n):
        return jnp.broadcast_to(
            jnp.sum(jnp.where(lane == n, dots, 0.0), axis=1, keepdims=True), (8, NY)
        )

    g1, g2 = coarse_rows_of(got, 0), coarse_rows_of(got, 1)
    d = thomas(cf, g1)
    for h in range(NZ):
        c_tmp[h] = d[h]
    q = coarse_operator(d, kc, cc, tmp)
    rcl = [rc[h] for h in range(NZ)]
    b1, b2 = pick(0), pick(1) + coarse_dot(d, rcl)
    w11 = pick(2)
    w12 = pick(3) + coarse_dot(d, g1)
    w22 = pick(4) + 2.0 * coarse_dot(d, g2) + coarse_dot(d, q)
    if not first:
        rs1, rs2 = [rs[h] for h in range(NZ)], [rs[NZ + h] for h in range(NZ)]
        c11, c21 = pick(5), pick(6)
        c12, c22 = pick(7) + coarse_dot(d, rs1), pick(8) + coarse_dot(d, rs2)
        pa, pb, pc = wp[0], wp[1], wp[2]
        inv = -1.0 / (pa * pc - pb * pb)
        e11, e21 = (pc * c11 - pb * c21) * inv, (pa * c21 - pb * c11) * inv
        e12, e22 = (pc * c12 - pb * c22) * inv, (pa * c22 - pb * c12) * inv
        w11 = w11 + c11 * e11 + c21 * e21
        w12 = w12 + c11 * e12 + c21 * e22
        w22 = w22 + c12 * e12 + c22 * e22
    inv = 1.0 / (w11 * w22 - w12 * w12)
    a1 = (w22 * b1 - w12 * b2) * inv
    a2 = (w11 * b2 - w12 * b1) * inv

    ay[...] = v[...]
    pd = add_operator_of_prolong(c_tmp, ix, iz, nb, ay)
    assemble_aisle(ay)
    for i in range(8):
        for j in range(8):
            pn1 = z[i, j]
            pn2 = t[i, j] + pd[cls(i)][cls(j)]
            sn1, sn2 = w1[i, j], ay[i, j]
            if not first:
                u, w = p1[i, j], p2[i, j]
                pn1 = pn1 + e11 * u + e21 * w
                pn2 = pn2 + e12 * u + e22 * w
                u, w = s1[i, j], s2[i, j]
                sn1 = sn1 + e11 * u + e21 * w
                sn2 = sn2 + e12 * u + e22 * w
            up = a1 * pn1 + a2 * pn2
            xo[i, j] = up if first else x[i, j] + up
            ro[i, j] = r[i, j] - (a1 * sn1 + a2 * sn2)
            if not last:
                p1o[i, j], p2o[i, j], s1o[i, j], s2o[i, j] = pn1, pn2, sn1, sn2
    if last:
        return
    wpo[0], wpo[1], wpo[2] = w11, w12, w22
    rnew = []
    for h in range(NZ):
        n1, n2 = g1[h], g2[h] + q[h]
        if not first:
            n1 = n1 + e11 * rs1[h] + e21 * rs2[h]
            n2 = n2 + e12 * rs1[h] + e22 * rs2[h]
        rso[h], rso[NZ + h] = n1, n2
        new = rcl[h] - (a1 * n1 + a2 * n2)
        rco[h] = new
        rnew.append(new)
    solved = thomas(cf, rnew)
    for h in range(NZ):
        c_tmp[h] = solved[h]
    make_z(c_tmp, ix, iz, ro, dinv, zo)
    local_operator(zo, fo, nb, even, (m0, m1, m2, m3))


NT = (((1,), (1,)), ((), ()))
SLOTS = 16


def slots_kernel(own_col, own_row, elem, side, target, table, owners):
    faces = own_row.shape[1]
    before = lax.broadcasted_iota(jnp.int32, (faces, faces), 0) < lax.broadcasted_iota(
        jnp.int32, (faces, faces), 1
    )
    same = (own_col[...] == own_row[...]) & before
    rank = jnp.sum(jnp.where(same, 1.0, 0.0), axis=0, keepdims=True)
    slot = own_row[...].astype(F32) * SLOTS + rank
    vals = jnp.concatenate(
        [
            elem[...].astype(F32) + 1.0,
            side[...].astype(F32),
            jnp.zeros((6, faces), F32),
        ],
        axis=0,
    ).astype(jnp.bfloat16)
    step = 256
    for s in range(0, table.shape[0], step):
        at = lax.broadcasted_iota(jnp.int32, (step, faces), 0).astype(F32) + float(s)
        hot = jnp.where(at == slot, 1.0, 0.0).astype(jnp.bfloat16)
        got = lax.dot_general(hot, vals, NT, preferred_element_type=F32)
        col = got[:, 0:1] - 1.0 + 128.0 * got[:, 1:2]
        lane = lax.broadcasted_iota(jnp.int32, (step, table.shape[1]), 1).astype(F32)
        table[s : s + step] = jnp.where(lane == col, 1.0, 0.0).astype(jnp.bfloat16)
    devices = owners.shape[0]
    dev = lax.broadcasted_iota(jnp.int32, (devices, faces), 0)
    hot = jnp.where(dev == own_row[...], 1.0, 0.0).astype(jnp.bfloat16)
    at = lax.broadcasted_iota(jnp.int32, (128, faces), 0).astype(F32)
    marked = jnp.where(at == rank, target[...].astype(F32) + 1.0, 0.0).astype(jnp.bfloat16)
    owners[...] = lax.dot_general(hot, marked, NT, preferred_element_type=F32) - 1.0


def owners_kernel(got, hot_t):
    devices = got.shape[0]
    lane = lax.broadcasted_iota(jnp.int32, (SLOTS, NY), 1)
    at = lax.broadcasted_iota(jnp.int32, (SLOTS, NY), 0)
    ones = jnp.ones((NY, NY), jnp.bfloat16)
    step = 8
    for d in range(0, devices, step):
        rows = [
            jnp.where(lane == at, jnp.broadcast_to(got[d + n, 3:4, :], (SLOTS, NY)), 0.0)
            for n in range(step)
        ]
        block = jnp.concatenate(rows, axis=0).astype(jnp.bfloat16)
        col = jnp.dot(block, ones, preferred_element_type=F32)
        elem = lax.broadcasted_iota(jnp.int32, col.shape, 1).astype(F32)
        hot = jnp.where(col == elem, 1.0, 0.0)
        hot_t[:, d * SLOTS : (d + step) * SLOTS] = hot.T.astype(jnp.bfloat16)


def split(v):
    high = v.astype(jnp.bfloat16)
    return high, (v - high.astype(F32)).astype(jnp.bfloat16)


def faces_kernel(x, nb, table, send):
    kt = nb[4]

    def weighted(get, row):
        acc = None
        for a in range(8):
            term = float(D_[row, a]) * get(a)
            acc = term if acc is None else acc + term
        return acc

    getters = (lambda a: x[a], lambda a: x[:, a], lambda a: x[:, :, a, :])
    his, los = [], []
    for get in getters:
        for end, sign in ((0, 1.0), (E, -1.0)):
            flux = weighted(get, end) * (sign * kt)[None]
            block = jnp.concatenate(
                [flux.reshape(64, NY), get(end).reshape(64, NY)], axis=0
            )
            h, l = split(block)
            his.append(h)
            los.append(l)
    hi, lo = jnp.concatenate(his, axis=1), jnp.concatenate(los, axis=1)
    step = 512
    for s in range(0, send.shape[0], step):
        hot = table[s : s + step]
        send[s : s + step] = lax.dot_general(
            hot, hi, NT, preferred_element_type=F32
        ) + lax.dot_general(hot, lo, NT, preferred_element_type=F32)


def load_kernel(got, hot_t, out):
    acc = None
    step = 512
    for s in range(0, got.shape[0], step):
        hi, lo = split(got[s : s + step])
        hot = hot_t[:, s : s + step]
        term = jnp.dot(hot, hi, preferred_element_type=F32) + jnp.dot(
            hot, lo, preferred_element_type=F32
        )
        acc = term if acc is None else acc + term
    out[...] = acc.T


def call(body, name, outs, args, scratch=(), flops=2_000_000):
    vmem = pl.BlockSpec(memory_space=pltpu.VMEM)
    return pl.pallas_call(
        body,
        out_shape=[jax.ShapeDtypeStruct(*((o, F32) if not isinstance(o[0], tuple) else o)) for o in outs],
        in_specs=[
            pl.BlockSpec(memory_space=pltpu.SMEM)
            if a.dtype == jnp.int32 and a.shape == (2,)
            else vmem
            for a in args
        ],
        out_specs=[vmem] * len(outs),
        scratch_shapes=[pltpu.VMEM(s, F32) for s in scratch],
        compiler_params=pltpu.CompilerParams(vmem_limit_bytes=24 * 1024 * 1024),
        cost_estimate=pl.CostEstimate(flops=flops, bytes_accessed=1 << 20, transcendentals=0),
        name=name,
    )(*args)


def pair_perms(n):
    first = [(i, i ^ 1) for i in range(n)]
    second = [(i, (i + 1) % n if i % 2 else (i - 1) % n) for i in range(n)]
    return first, second


def swap_x(pair):
    a, b = pair_perms(NX)
    return [lax.ppermute(pair[0], "row", a), lax.ppermute(pair[1], "row", b)]


def swap_z(pair):
    a, b = pair_perms(NZ)
    return [lax.ppermute(pair[0], "height", a), lax.ppermute(pair[1], "height", b)]


def everywhere(rows):
    return lax.all_to_all(rows, ("row", "height"), split_axis=0, concat_axis=0, tiled=True)


def shards(heat, conductivity, marks, face_owner, face_element, face_side, owner_element):
    devices = NX * NZ
    pos = jnp.stack([lax.axis_index("row"), lax.axis_index("height")]).astype(jnp.int32)
    row = lambda a: a.reshape(1, -1)
    faces = face_element.shape[0]
    f, ma, mb = call(heat_kernel, "heat", [FIELD, FACE, FACE], [pos, heat.reshape(FIELD)])
    ra, rb = swap_x((ma, mb))
    table, owners = call(
        slots_kernel,
        "slots",
        [((devices * SLOTS, 6 * NY), jnp.bfloat16), (devices, 128)],
        [face_owner, row(face_owner), row(face_element), row(face_side), row(owner_element)],
    )
    f, ma, mb = call(heat_z_kernel, "heat_z", [FIELD, FACE, FACE], [pos, f, ra, rb])
    ra, rb = swap_z((ma, mb))
    r, rows = call(
        first_rows_kernel,
        "first_rows",
        [FIELD, (devices, 4, NY)],
        [pos, f, ra, rb, row(conductivity), row(marks), owners],
    )
    got0 = everywhere(rows)
    kc, cc, cf, rc, nb, dinv, z, f, *msgs = call(
        setup_kernel,
        "setup",
        [COARSE, COARSE, (48, NX, NY), COARSE, (18, 8, NY), FIELD, FIELD, FIELD] + [FACE] * 4,
        [pos, got0, r],
        scratch=[COARSE],
    )
    (hot_t,) = call(
        owners_kernel, "owners", [((NY, devices * SLOTS), jnp.bfloat16)], [got0]
    )
    state = []
    for outer in range(ITERS // 2):
        first, last = outer == 0, outer == ITERS // 2 - 1
        got = swap_x(msgs[:2]) + swap_z(msgs[2:])
        w1, t, f2, *msgs = call(
            inner_kernel, "inner", [FIELD] * 3 + [FACE] * 4, [pos, f, *got, nb, dinv]
        )
        got = swap_x(msgs[:2]) + swap_z(msgs[2:])
        prev = [] if first else [state[3], state[4]]
        v, rows = call(
            functools.partial(rows_kernel, first),
            "rows",
            [FIELD, (devices, 4, NY)],
            [pos, f2, *got, z, r, t, w1, *prev],
        )
        rows = everywhere(rows)
        outs = [FIELD, FIELD]
        if not last:
            outs += [FIELD] * 4 + [(2 * NZ, NX, NY), (3, 8, NY), COARSE, FIELD, FIELD] + [FACE] * 4
        res = call(
            functools.partial(step_kernel, first, last),
            "step",
            outs,
            [pos, rows, r, z, t, w1, v, dinv, nb, kc, cc, cf, rc, *state],
            scratch=[FIELD, COARSE, (9 * NZ, NX, NY)],
        )
        x, r = res[:2]
        if not last:
            p1, p2, s1, s2, rs, wp, rc, z, f, *msgs = res[2:]
            state = [x, p1, p2, s1, s2, rs, wp]
    (send,) = call(faces_kernel, "faces", [(devices * SLOTS, NY)], [x, nb, table])
    got = everywhere(send.reshape(devices, SLOTS, NY))
    (load,) = call(
        load_kernel, "load", [(NY, NY)], [got.reshape(devices * SLOTS, NY), hot_t]
    )
    shape = (8, 8, 8, 1, 1, NY)
    return (x.reshape(shape), r.reshape(shape), load.reshape(NY, 1, 1, NY))


def solution(mesh):
    in_specs = (
        P(None, None, None, "row", "height", None),
        P("row", "height", None),
        P("row", "height", None),
        P(("row", "height"), None),
        P(("row", "height")),
        P(("row", "height")),
        P(("row", "height")),
    )
    out_specs = (
        P(None, None, None, "row", "height", None),
        P(None, None, None, "row", "height", None),
        P(None, "row", "height", None),
    )
    return jax.shard_map(shards, mesh=mesh, in_specs=in_specs, out_specs=out_specs, check_vma=False)
```

```python
import functools

import jax
import jax.numpy as jnp
import numpy as np
from jax import lax
from jax.experimental import pallas as pl
from jax.experimental.pallas import tpu as pltpu
from jax.sharding import PartitionSpec as P

ITERS = 8
HEAT_AIR = 0.02
HEAT_SOLID = 0.08
GLL_INNER = (
    -0.8717401485096066,
    -0.5917001814331423,
    -0.2092992179024789,
    0.2092992179024789,
    0.5917001814331423,
    0.8717401485096066,
)
F32 = jnp.float32
NX, NZ, NY = 8, 16, 128
FIELD = (8, 8, 8, NY)
FACE = (8, 8, NY)
COARSE = (NZ, NX, NY)


def legendre_values(points_in, degree):
    before = points_in * 0.0 + 1.0
    current = points_in * 1.0
    for order_now in range(1, degree):
        following = ((2 * order_now + 1) * points_in * current - order_now * before) / (
            order_now + 1
        )
        before = current
        current = following
    return current


def gll_tables():
    poly_order = 7
    gll_nodes = np.array((-1.0,) + GLL_INNER + (1.0,))
    edge_values = legendre_values(gll_nodes, poly_order)
    gll_weights = 2.0 / (poly_order * (poly_order + 1) * edge_values**2)
    diff_table = np.zeros((8, 8))
    for row_index in range(8):
        for col_index in range(8):
            if row_index != col_index:
                diff_table[row_index, col_index] = edge_values[row_index] / (
                    edge_values[col_index] * (gll_nodes[row_index] - gll_nodes[col_index])
                )
    diff_table[0, 0] = -poly_order * (poly_order + 1) / 4.0
    diff_table[7, 7] = poly_order * (poly_order + 1) / 4.0
    return (gll_weights, diff_table)


W_, D_ = gll_tables()
K_ = D_.T @ np.diag(W_) @ D_
S_ = np.sum(D_**2 * W_[:, None], axis=0)
W = [float(v) for v in W_]
SD = [float(v) for v in S_]
E = 7


def kvec(vals):
    k = lax.broadcasted_iota(jnp.int32, (8, NY), 0)
    out = jnp.full((8, NY), float(vals[0]), F32)
    for n in range(1, 8):
        out = jnp.where(k == n, jnp.float32(float(vals[n])), out)
    return out


def apply1d(v, mat):
    ev = [v[a] + v[7 - a] for a in range(4)]
    od = [v[a] - v[7 - a] for a in range(4)]
    out = [None] * 8
    for i in range(4):
        s = d = None
        for a in range(4):
            cs = float(0.5 * (mat[i, a] + mat[i, 7 - a]))
            cd = float(0.5 * (mat[i, a] - mat[i, 7 - a]))
            s = cs * ev[a] if s is None else s + cs * ev[a]
            d = cd * od[a] if d is None else d + cd * od[a]
        out[i] = s + d
        out[7 - i] = s - d
    return out


def place(pos_ref):
    ix, iz = pos_ref[0], pos_ref[1]
    has = (ix > 0, ix < NX - 1, iz > 0, iz < NZ - 1)
    frac = tuple(jnp.where(h, jnp.float32(0.5), jnp.float32(1.0)) for h in has)
    even = (lax.rem(ix, 2) == 0, lax.rem(iz, 2) == 0)
    return ix, iz, has, frac, even


def own_mult():
    k = lax.broadcasted_iota(jnp.int32, (8, NY), 0)
    y = lax.broadcasted_iota(jnp.int32, (8, NY), 1)
    shared = ((k == 0) & (y > 0)) | ((k == E) & (y < NY - 1))
    return jnp.where(shared, jnp.float32(0.5), jnp.float32(1.0))


def field_sum(get, frac):
    total = None
    for i in range(8):
        mid = get(i, 1)
        for j in range(2, 7):
            mid = mid + get(i, j)
        row = mid + frac[2] * get(i, 0) + frac[3] * get(i, E)
        if i == 0:
            row = frac[0] * row
        elif i == E:
            row = frac[1] * row
        total = row if total is None else total + row
    return total


def assemble_aisle(ref):
    low, high = ref[:, :, 0, :], ref[:, :, E, :]
    y = lax.broadcasted_iota(jnp.int32, FACE, 2)
    ref[:, :, 0, :] = low + jnp.where(y > 0, pltpu.roll(high, 1, 2), 0.0)
    ref[:, :, E, :] = high + jnp.where(y < NY - 1, pltpu.roll(low, NY - 1, 2), 0.0)


def add_faces_x(ref, got, has, even):
    a, b = got[0][...], got[1][...]
    ref[0] = ref[0] + jnp.where(has[0], jnp.where(even[0], b, a), 0.0)
    ref[E] = ref[E] + jnp.where(has[1], jnp.where(even[0], a, b), 0.0)


def add_faces_z(ref, got, has, even):
    a, b = got[0][...], got[1][...]
    ref[:, 0] = ref[:, 0] + jnp.where(has[2], jnp.where(even[1], b, a), 0.0)
    ref[:, E] = ref[:, E] + jnp.where(has[3], jnp.where(even[1], a, b), 0.0)


def put_pair(even, low, high, out):
    out[0][...] = jnp.where(even, high, low)
    out[1][...] = jnp.where(even, low, high)


def aisle_stiffness(block):
    turned = jnp.swapaxes(block, 0, 1)
    out = apply1d([turned[c] for c in range(8)], K_)
    return jnp.swapaxes(jnp.stack(out, axis=0), 0, 1)


def local_operator(z_ref, f_ref, nb_ref, even, msgs):
    wk = kvec(W)
    kt, ct = nb_ref[4], nb_ref[13]
    kw, cw = kt * wk, ct * wk
    w0 = W[0]
    xc = {}
    for j in range(8):
        out = apply1d([z_ref[i, j] for i in range(8)], K_)
        kwj = kw * W[j]
        res = [kwj * out[i] for i in range(8)]
        for i in range(8):
            f_ref[i, j] = res[i]
        if j in (0, E):
            xc[0, j], xc[E, j] = out[0], out[E]
    for i in range(8):
        block = z_ref[i]
        v = [block[j] for j in range(8)]
        fx = [f_ref[i, j] for j in range(8)]
        zs = apply1d(v, K_)
        ys = aisle_stiffness(block)
        kwi = kw * W[i]
        res = [
            fx[j] + kwi * zs[j] + (W[i] * W[j]) * (kt * ys[j] + cw * v[j]) for j in range(8)
        ]
        for j in range(8):
            f_ref[i, j] = res[j]
        low, high = res[0], res[E]
        if i in (0, E):
            kn = nb_ref[1 if i == 0 else 7] * (w0 * wk)
            low, high = low + kn * zs[0], high + kn * zs[E]
            for j in (0, E):
                n = 3 if j == 0 else 5
                res[j] = (
                    res[j]
                    + nb_ref[n] * (w0 * wk * xc[i, j] + (w0 * w0) * ys[j])
                    + nb_ref[9 + n] * ((w0 * w0) * wk * v[j])
                )
            up, down = (1, 0) if i == 0 else (0, 1)

            @pl.when(even[0])
            def _(res=res, to=up):
                for j in range(8):
                    msgs[to][j] = res[j]

            @pl.when(jnp.logical_not(even[0]))
            def _(res=res, to=down):
                for j in range(8):
                    msgs[to][j] = res[j]

        msgs[2][i] = jnp.where(even[1], high, low)
        msgs[3][i] = jnp.where(even[1], low, high)


def thomas(cf_ref, rhs):
    dp = []
    for h in range(NZ):
        v = rhs[h] if h == 0 else rhs[h] - cf_ref[h] * dp[h - 1]
        dp.append(v * cf_ref[32 + h])
    for h in range(NZ - 2, -1, -1):
        dp[h] = dp[h] - cf_ref[16 + h] * dp[h + 1]
    return dp


def coarse_dot(a, b):
    acc = None
    for u, v in zip(a, b):
        acc = u * v if acc is None else acc + u * v
    return spread_sum(acc)


def spread_sum(tile):
    row = jnp.broadcast_to(jnp.sum(tile, axis=0, keepdims=True), (8, NY))
    return jnp.broadcast_to(jnp.sum(row, axis=1, keepdims=True), (8, NY))


def shift_pair(v, axis):
    n = v.shape[axis]
    p = lax.broadcasted_iota(jnp.int32, v.shape, axis)
    before = jnp.where(p == 0, v, pltpu.roll(v, 1, axis))
    after = jnp.where(p == n - 1, v, pltpu.roll(v, n - 1, axis))
    return before, after


def spread3(v, before, after):
    return (v, 0.5 * v + 0.25 * (before + after), 0.25 * (before - after))


def gather3(duals, axis):
    m, f, a = duals
    g, h = 0.25 * (f + a), 0.25 * (f - a)
    n = m.shape[axis]
    p = lax.broadcasted_iota(jnp.int32, m.shape, axis)
    up = jnp.where(p == n - 1, h, pltpu.roll(g, n - 1, axis))
    down = jnp.where(p == 0, g, pltpu.roll(h, 1, axis))
    return m + 0.5 * f + up + down


MU = (2.0 - 2.0 * W[0], 2.0 * W[0], 2.0 * W[0])
KS = float(2.0 * (K_[0, 0] + K_[0, 7]))
KA = float(2.0 * (K_[0, 0] - K_[0, 7]))


def stiff3(q):
    d = q[1] - q[0]
    return ((-KS / MU[0]) * d, (KS / MU[1]) * d, (KA / MU[2]) * q[2])


def coarse_operator(d, kc_ref, cc_ref, tmp_ref):
    for h in range(NZ):
        ys = spread3(d[h], *shift_pair(d[h], 1))
        for c in range(3):
            xs = spread3(ys[c], *shift_pair(ys[c], 0))
            for a in range(3):
                tmp_ref[(a * 3 + c) * NZ + h] = xs[a]
    part = []
    for h in range(NZ):
        lo, hi = max(h - 1, 0), min(h + 1, NZ - 1)
        q = {}
        for a in range(3):
            for c in range(3):
                base = (a * 3 + c) * NZ
                zs = spread3(tmp_ref[base + h], tmp_ref[base + lo], tmp_ref[base + hi])
                for b in range(3):
                    q[a, b, c] = zs[b]
        acc = {key: None for key in q}

        def add(key, val):
            acc[key] = val if acc[key] is None else acc[key] + val

        for b in range(3):
            for c in range(3):
                for n, val in enumerate(stiff3([q[a, b, c] for a in range(3)])):
                    add((n, b, c), val)
        for a in range(3):
            for c in range(3):
                for n, val in enumerate(stiff3([q[a, b, c] for b in range(3)])):
                    add((a, n, c), val)
        for a in range(3):
            for b in range(3):
                for n, val in enumerate(stiff3([q[a, b, c] for c in range(3)])):
                    add((a, b, n), val)
        kh, ch = kc_ref[h], cc_ref[h]
        outs = []
        for b in range(3):
            cols = []
            for c in range(3):
                duals = [
                    (MU[a] * MU[b] * MU[c]) * (kh * acc[a, b, c] + ch * q[a, b, c])
                    for a in range(3)
                ]
                cols.append(gather3(duals, 0))
            outs.append(gather3(cols, 1))
        part.append(outs)
    res = []
    for h in range(NZ):
        m, f, _ = part[h]
        v = m + 0.5 * f
        g = lambda n: 0.25 * (part[n][1] + part[n][2])
        l = lambda n: 0.25 * (part[n][1] - part[n][2])
        v = v + (g(h + 1) if h < NZ - 1 else l(h))
        v = v + (l(h - 1) if h > 0 else g(h))
        res.append(v)
    return res


def coarse_row(ref, ix, iz, dx, dz):
    x = jnp.clip(ix + dx, 0, NX - 1)
    z = jnp.clip(iz + dz, 0, NZ - 1)
    return ref[z, pl.ds(x, 1), :]


def aisle_tiles(row, want_stiff):
    c = jnp.broadcast_to(row, (8, NY))
    before, after = shift_pair(c, 1)
    k = lax.broadcasted_iota(jnp.int32, (8, NY), 0)
    low, high = 0.5 * (c + before), 0.5 * (c + after)
    tile = jnp.where(k == 0, low, jnp.where(k == E, high, c))
    if not want_stiff:
        return tile, None
    return tile, kvec(K_[:, 0]) * (low - c) + kvec(K_[:, 7]) * (high - c)


def classes(tiles, reach):
    n = 2 * reach + 1
    m = 2 * n - 3

    def line(vals):
        out = []
        for p in range(m):
            if p % 2 == 0:
                out.append(0.5 * (vals[p // 2] + vals[p // 2 + 1]))
            else:
                out.append(vals[p // 2 + 1])
        return out

    cols = [line(tiles[dx]) for dx in range(n)]
    by_q = [line([cols[dx][q] for dx in range(n)]) for q in range(m)]
    return [[by_q[q][p] for q in range(m)] for p in range(m)]


def cls(i):
    return 0 if i == 0 else (2 if i == E else 1)


def own_prolong(ref, ix, iz):
    tiles = [
        [aisle_tiles(coarse_row(ref, ix, iz, dx, dz), False)[0] for dz in (-1, 0, 1)]
        for dx in (-1, 0, 1)
    ]
    return classes(tiles, 1)


def add_operator_of_prolong(ref, ix, iz, nb_ref, out_ref):
    tv, ty = [], []
    for dx in range(-2, 3):
        pair = [aisle_tiles(coarse_row(ref, ix, iz, dx, dz), True) for dz in range(-2, 3)]
        tv.append([p[0] for p in pair])
        ty.append([p[1] for p in pair])
    v, yv = classes(tv, 2), classes(ty, 2)
    wk = kvec(W)

    def parts(ex, ez):
        p, q = 2 + 2 * ex, 2 + 2 * ez
        n = (ex + 1) * 3 + ez + 1
        kt, ct = nb_ref[n], nb_ref[9 + n]
        kw, cw = kt * wk, ct * wk
        memo = {}

        def once(key, make):
            if key not in memo:
                memo[key] = make()
            return memo[key]

        def along(i, a, b, c):
            return kw * (float(K_[i, 0]) * (a - b) + float(K_[i, 7]) * (c - b))

        def tile(i, j):
            a, b = cls(i), cls(j)
            xt = once(
                ("x", i, b), lambda: along(i, v[p][q + b], v[p + 1][q + b], v[p + 2][q + b])
            )
            zt = once(
                ("z", a, j), lambda: along(j, v[p + a][q], v[p + a][q + 1], v[p + a][q + 2])
            )
            yt = once(("y", a, b), lambda: kt * yv[p + a][q + b] + cw * v[p + a][q + b])
            return W[j] * xt + W[i] * zt + (W[i] * W[j]) * yt

        return tile

    part = {(ex, ez): parts(ex, ez) for ex in (-1, 0, 1) for ez in (-1, 0, 1)}
    for i in range(8):
        new = []
        for j in range(8):
            acc = out_ref[i, j] + part[0, 0](i, j)
            ex = -1 if i == 0 else (1 if i == E else 0)
            ez = -1 if j == 0 else (1 if j == E else 0)
            if ex:
                acc = acc + part[ex, 0](7 - i, j)
            if ez:
                acc = acc + part[0, ez](i, 7 - j)
            if ex and ez:
                acc = acc + part[ex, ez](7 - i, 7 - j)
            new.append(acc)
        for j in range(8):
            out_ref[i, j] = new[j]
    return [[v[2 + a][2 + b] for b in range(3)] for a in range(3)]


def make_z(c_ref, ix, iz, r_ref, dinv_ref, z_ref):
    pc = own_prolong(c_ref, ix, iz)
    for i in range(8):
        new = [r_ref[i, j] * dinv_ref[i, j] + pc[cls(i)][cls(j)] for j in range(8)]
        for j in range(8):
            z_ref[i, j] = new[j]


def coarse_rows_of(got_ref, which):
    return [got_ref[pl.ds(4 * h + which, NX, stride=4 * NZ), :] for h in range(NZ)]


def heat_kernel(pos, heat, cond, marks, f, ma, mb, kc, mk, buf, sems):
    copies = [
        pltpu.make_async_copy(src, dst, sems.at[n])
        for n, (src, dst) in enumerate(((heat, buf), (cond, kc), (marks, mk)))
    ]
    for copy in copies:
        copy.start()
    _, _, _, _, even = place(pos)
    wk = kvec(W)
    for copy in copies:
        copy.wait()
    for i in range(8):
        new = [(W[i] * W[j]) * wk * buf[i, j] for j in range(8)]
        for j in range(8):
            f[i, j] = new[j]
    put_pair(even[0], f[0], f[E], (ma, mb))


def heat_z_kernel(pos, f, ra, rb, out, ma, mb):
    _, _, has, _, even = place(pos)
    out[...] = f[...]
    add_faces_x(out, (ra, rb), has, even)
    put_pair(even[1], out[:, 0], out[:, E], (ma, mb))


def first_rows_kernel(pos, f, ra, rb, kc, marks, out, rows):
    _, _, has, frac, even = place(pos)
    out[...] = f[...]
    add_faces_z(out, (ra, rb), has, even)
    assemble_aisle(out)
    tile = field_sum(lambda i, j: out[i, j], frac) * own_mult()
    restricted = jnp.sum(tile, axis=0, keepdims=True)
    cap = jnp.where(marks[...] == 1, jnp.float32(HEAT_SOLID), jnp.float32(HEAT_AIR))
    block = jnp.concatenate([kc[...], cap, restricted, jnp.zeros((1, NY), F32)], axis=0)
    rows[...] = jnp.broadcast_to(block[None], rows.shape)


def setup_kernel(
    pos, got, r, kc, cc, cf, rc, nb, dinv, z, f, m0, m1, m2, m3, c_tmp
):
    ix, iz, has, frac, even = place(pos)
    k_all, c_all, r_all = (coarse_rows_of(got, n) for n in range(3))
    for h in range(NZ):
        kc[h], cc[h], rc[h] = k_all[h], c_all[h], r_all[h]
    link = [2.0 * k_all[h] * k_all[h + 1] / (k_all[h] + k_all[h + 1]) for h in range(NZ - 1)]
    above = None
    for h in range(NZ):
        main = 8.0 * c_all[h]
        if h > 0:
            main = main + link[h - 1]
        if h < NZ - 1:
            main = main + link[h]
        low = -link[h - 1] if h > 0 else jnp.zeros((NX, NY), F32)
        piv = main if h == 0 else main - low * above
        inv = 1.0 / piv
        above = -link[h] * inv if h < NZ - 1 else jnp.zeros((NX, NY), F32)
        cf[h], cf[16 + h], cf[32 + h] = low, above, inv
    for ex in (-1, 0, 1):
        for ez in (-1, 0, 1):
            n = (ex + 1) * 3 + ez + 1
            there = None
            if ex:
                there = has[0] if ex < 0 else has[1]
            if ez:
                hz = has[2] if ez < 0 else has[3]
                there = hz if there is None else there & hz
            for base, src in ((0, kc), (9, cc)):
                tile = jnp.broadcast_to(coarse_row(src, ix, iz, ex, ez), (8, NY))
                nb[base + n] = tile if there is None else jnp.where(there, tile, 0.0)
    wk, sk = kvec(W), kvec(SD)
    for i in range(8):
        for j in range(8):
            ex = -1 if i == 0 else (1 if i == E else 0)
            ez = -1 if j == 0 else (1 if j == E else 0)
            kt, ct = nb[4], nb[13]
            for n in {4 + 3 * ex, 4 + ez, 4 + 3 * ex + ez} - {4}:
                kt, ct = kt + nb[n], ct + nb[9 + n]
            dinv[i, j] = (
                kt * ((SD[i] * W[j] + W[i] * SD[j]) * wk + (W[i] * W[j]) * sk)
                + ct * ((W[i] * W[j]) * wk)
            )
    assemble_aisle(dinv)
    dinv[...] = 1.0 / dinv[...]
    solved = thomas(cf, r_all)
    for h in range(NZ):
        c_tmp[h] = solved[h]
    make_z(c_tmp, ix, iz, r, dinv, z)
    local_operator(z, f, nb, even, (m0, m1, m2, m3))


def inner_kernel(pos, f, r0, r1, r2, r3, nb, dinv, *refs):
    w1, t, f2, m0, m1, m2, m3 = refs[-7:]
    _, _, has, _, even = place(pos)
    w1[...] = f[...]
    add_faces_x(w1, (r0, r1), has, even)
    add_faces_z(w1, (r2, r3), has, even)
    assemble_aisle(w1)
    t[...] = w1[...] * dinv[...]
    local_operator(t, f2, nb, even, (m0, m1, m2, m3))


def dots_kernel(first, *refs):
    if first:
        pos, z, r, t, w1, lines = refs
    else:
        pos, z, r, t, w1, s1, s2, lines = refs
    _, _, _, frac, _ = place(pos)
    my = own_mult()
    zero = jnp.zeros((1, NY), F32)

    def dot(a, b):
        tile = my * field_sum(lambda i, j: a[i, j] * b[i, j], frac)
        return jnp.sum(tile, axis=0, keepdims=True)

    out = [dot(z, r), dot(t, r), dot(z, w1), dot(t, w1), zero]
    out += [zero] * 4 if first else [dot(z, s1), dot(z, s2), dot(t, s1), dot(t, s2)]
    out += [zero] * 6
    out.append(jnp.sum(field_sum(lambda i, j: w1[i, j], frac) * my, axis=0, keepdims=True))
    lines[...] = jnp.concatenate(out, axis=0)


def rows_kernel(first, *refs):
    if first:
        pos, f2, r0, r1, r2, r3, t, lines, owners, v, rows = refs
    else:
        pos, f2, r0, r1, r2, r3, t, lines, v, rows = refs
    _, _, has, frac, even = place(pos)
    v[...] = f2[...]
    add_faces_x(v, (r0, r1), has, even)
    add_faces_z(v, (r2, r3), has, even)
    my = own_mult()
    tv = jnp.sum(field_sum(lambda i, j: t[i, j] * v[i, j], frac), axis=0, keepdims=True)
    lane = lax.broadcasted_iota(jnp.int32, (16, NY), 1)
    at = lax.broadcasted_iota(jnp.int32, (16, NY), 0)
    stacked = jnp.where(at == 4, jnp.broadcast_to(tv, (16, NY)), lines[...])
    totals = jnp.broadcast_to(jnp.sum(stacked, axis=1, keepdims=True), (16, NY))
    dots = jnp.sum(jnp.where(lane == at, totals, 0.0), axis=0, keepdims=True)
    vt = field_sum(lambda i, j: v[i, j], frac)
    k = lax.broadcasted_iota(jnp.int32, (8, NY), 0)
    y = lax.broadcasted_iota(jnp.int32, (8, NY), 1)
    vlow = jnp.broadcast_to(vt[0:1], (8, NY))
    vhigh = jnp.broadcast_to(vt[7:8], (8, NY))
    vt = vt + jnp.where((k == 0) & (y > 0), pltpu.roll(vhigh, 1, 1), 0.0)
    vt = vt + jnp.where((k == E) & (y < NY - 1), pltpu.roll(vlow, NY - 1, 1), 0.0)
    g2 = jnp.sum(vt * my, axis=0, keepdims=True)
    block = jnp.concatenate([lines[15:16], g2, dots, jnp.zeros((1, NY), F32)], axis=0)
    rows[...] = jnp.broadcast_to(block[None], rows.shape)
    if first:
        rows[:, 3, :] = owners[...]


def coefficients(first, got, d, q, rc, rs, wp, cf):
    total = got[0:8]
    for n in range(8, NX * NZ * 4, 8):
        total = total + got[n : n + 8]
    dots = jnp.broadcast_to(total[2:3] + total[6:7], (8, NY))
    lane = lax.broadcasted_iota(jnp.int32, (8, NY), 1)

    def pick(n):
        return jnp.broadcast_to(
            jnp.sum(jnp.where(lane == n, dots, 0.0), axis=1, keepdims=True), (8, NY)
        )

    g1, g2 = coarse_rows_of(got, 0), coarse_rows_of(got, 1)
    b1, b2 = pick(0), pick(1) + coarse_dot(d, [rc[h] for h in range(NZ)])
    w11 = pick(2)
    w12 = pick(3) + coarse_dot(d, g1)
    w22 = pick(4) + 2.0 * coarse_dot(d, g2) + coarse_dot(d, q)
    e = [None] * 4
    if not first:
        rs1, rs2 = [rs[h] for h in range(NZ)], [rs[NZ + h] for h in range(NZ)]
        c11, c21 = pick(5), pick(6)
        c12, c22 = pick(7) + coarse_dot(d, rs1), pick(8) + coarse_dot(d, rs2)
        pa, pb, pc = wp[6], wp[7], wp[8]
        inv = -1.0 / (pa * pc - pb * pb)
        e11, e21 = (pc * c11 - pb * c21) * inv, (pa * c21 - pb * c11) * inv
        e12, e22 = (pc * c12 - pb * c22) * inv, (pa * c22 - pb * c12) * inv
        w11 = w11 + c11 * e11 + c21 * e21
        w12 = w12 + c11 * e12 + c21 * e22
        w22 = w22 + c12 * e12 + c22 * e22
        e = [e11, e21, e12, e22]
    inv = 1.0 / (w11 * w22 - w12 * w12)
    a1 = (w22 * b1 - w12 * b2) * inv
    a2 = (w11 * b2 - w12 * b1) * inv
    return a1, a2, e, (w11, w12, w22), g1, g2


def new_residual(first, a1, a2, x1, x2, r, w1, ay, s1, s2, out):
    for i in range(8):
        new = []
        for j in range(8):
            v = r[i, j] - (a1 * w1[i, j] + a2 * ay[i, j])
            if not first:
                v = v - (x1 * s1[i, j] + x2 * s2[i, j])
            new.append(v)
        for j in range(8):
            out[i, j] = new[j]


def step_kernel(first, *refs):
    refs = list(refs)
    take = lambda n: [refs.pop(0) for _ in range(n)]
    pos, got, r, w1, v, dinv, nb, kc, cc, cf, rc = take(11)
    s1 = s2 = rs = wp = None
    if not first:
        s1, s2, rs, wp = take(4)
    ro, rco, zo, fo, m0, m1, m2, m3, co, ay, pdo, qo = take(12)
    c_tmp, tmp = take(2)
    ix, iz, has, frac, even = place(pos)
    d = thomas(cf, coarse_rows_of(got, 0))
    for h in range(NZ):
        c_tmp[h] = d[h]
    q = coarse_operator(d, kc, cc, tmp)
    a1, a2, e, w, g1, g2 = coefficients(first, got, d, q, rc, rs, wp, cf)
    x1 = x2 = None
    if not first:
        x1, x2 = a1 * e[0] + a2 * e[2], a1 * e[1] + a2 * e[3]
    for n, val in enumerate((a1, a2, *e, *w)):
        if val is not None:
            co[n] = val
        else:
            co[n] = jnp.zeros((8, NY), F32)
    ay[...] = v[...]
    pd = add_operator_of_prolong(c_tmp, ix, iz, nb, ay)
    for n in range(9):
        pdo[n] = pd[n // 3][n % 3]
    assemble_aisle(ay)
    new_residual(first, a1, a2, x1, x2, r, w1, ay, s1, s2, ro)
    rnew = []
    for h in range(NZ):
        qo[h] = q[h]
        new = rc[h] - (a1 * g1[h] + a2 * (g2[h] + q[h]))
        if not first:
            new = new - (x1 * rs[h] + x2 * rs[NZ + h])
        rco[h] = new
        rnew.append(new)
    solved = thomas(cf, rnew)
    for h in range(NZ):
        c_tmp[h] = solved[h]
    make_z(c_tmp, ix, iz, ro, dinv, zo)
    local_operator(zo, fo, nb, even, (m0, m1, m2, m3))


def new_x(first, a1, a2, x1, x2, z, t, pd, p1, p2, x, out):
    for i in range(8):
        new = []
        for j in range(8):
            up = a1 * z[i, j] + a2 * (t[i, j] + pd(i, j))
            if not first:
                up = x[i, j] + (up + (x1 * p1[i, j] + x2 * p2[i, j]))
            new.append(up)
        for j in range(8):
            out[i, j] = new[j]


def late_kernel(first, *refs):
    refs = list(refs)
    take = lambda n: [refs.pop(0) for _ in range(n)]
    got, z, t, w1, ay, co, pdt, q = take(8)
    x = p1 = p2 = s1 = s2 = rs = None
    if not first:
        x, p1, p2, s1, s2, rs = take(6)
    xo, p1o, p2o, s1o, s2o, rso = take(6)
    a1, a2, e11, e21, e12, e22 = (co[n] for n in range(6))
    x1, x2 = a1 * e11 + a2 * e12, a1 * e21 + a2 * e22
    pd = lambda i, j: pdt[3 * cls(i) + cls(j)]
    new_x(first, a1, a2, x1, x2, z, t, pd, p1, p2, x, xo)

    def block(one, two, prev1, prev2, out1, out2):
        for i in range(8):
            new = []
            for j in range(8):
                n1, n2 = one(i, j), two(i, j)
                if not first:
                    u, w = prev1[i, j], prev2[i, j]
                    n1, n2 = n1 + e11 * u + e21 * w, n2 + e12 * u + e22 * w
                new.append((n1, n2))
            for j in range(8):
                out1[i, j], out2[i, j] = new[j]

    block(lambda i, j: z[i, j], lambda i, j: t[i, j] + pd(i, j), p1, p2, p1o, p2o)
    block(lambda i, j: w1[i, j], lambda i, j: ay[i, j], s1, s2, s1o, s2o)
    g1, g2 = coarse_rows_of(got, 0), coarse_rows_of(got, 1)
    for h in range(NZ):
        n1, n2 = g1[h], g2[h] + q[h]
        if not first:
            u, w = rs[h], rs[NZ + h]
            n1, n2 = n1 + e11 * u + e21 * w, n2 + e12 * u + e22 * w
        rso[h], rso[NZ + h] = n1, n2


def last_kernel(pos, got, z, t, nb, kc, cc, cf, rc, x, p1, p2, rs, wp, table, xo, send, co, dc, tmp):
    ix, iz, _, _, _ = place(pos)
    d = thomas(cf, coarse_rows_of(got, 0))
    for h in range(NZ):
        dc[h] = d[h]
    q = coarse_operator(d, kc, cc, tmp)
    a1, a2, e, _, _, _ = coefficients(False, got, d, q, rc, rs, wp, cf)
    x1, x2 = a1 * e[0] + a2 * e[2], a1 * e[1] + a2 * e[3]
    for n, val in enumerate((a1, a2, x1, x2)):
        co[n] = val
    own = own_prolong(dc, ix, iz)
    pd = lambda i, j: own[cls(i)][cls(j)]
    new_x(False, a1, a2, x1, x2, z, t, pd, p1, p2, x, xo)
    put_rows(xo, nb, table, send)


def residual_kernel(pos, co, dc, v, r, w1, s1, s2, nb, ro, ay):
    ix, iz, _, _, _ = place(pos)
    ay[...] = v[...]
    add_operator_of_prolong(dc, ix, iz, nb, ay)
    assemble_aisle(ay)
    new_residual(False, co[0], co[1], co[2], co[3], r, w1, ay, s1, s2, ro)


NT = (((1,), (1,)), ((), ()))
SLOTS = 16


def slots_kernel(own_in, elem_in, side_in, target_in, table, owners, own, elem, side, target, sems):
    pairs = ((own_in, own), (elem_in, elem), (side_in, side), (target_in, target))
    copies = [pltpu.make_async_copy(src, dst, sems.at[n]) for n, (src, dst) in enumerate(pairs)]
    for copy in copies:
        copy.start()
    for copy in copies:
        copy.wait()
    faces = own.shape[1]
    row = own[...].astype(F32)
    col = jnp.broadcast_to(row, (NY, faces)).T
    ranks = []
    for s in range(0, faces, NY):
        f = lax.broadcasted_iota(jnp.int32, (faces, NY), 0)
        g = lax.broadcasted_iota(jnp.int32, (faces, NY), 1) + s
        same = (col == row[:, s : s + NY]) & (f < g)
        ranks.append(jnp.sum(jnp.where(same, 1.0, 0.0), axis=0, keepdims=True))
    rank = jnp.concatenate(ranks, axis=1)
    slot = row * SLOTS + rank
    vals = jnp.concatenate(
        [elem[...].astype(F32) + 1.0, side[...].astype(F32), jnp.zeros((6, faces), F32)], axis=0
    ).astype(jnp.bfloat16)
    step = 256
    for s in range(0, table.shape[0], step):
        at = lax.broadcasted_iota(jnp.int32, (step, faces), 0).astype(F32) + float(s)
        hot = jnp.where(at == slot, 1.0, 0.0).astype(jnp.bfloat16)
        got = lax.dot_general(hot, vals, NT, preferred_element_type=F32)
        pick = got[:, 0:1] - 1.0 + 128.0 * got[:, 1:2]
        lane = lax.broadcasted_iota(jnp.int32, (step, table.shape[1]), 1).astype(F32)
        table[s : s + step] = jnp.where(lane == pick, 1.0, 0.0).astype(jnp.bfloat16)
    devices = owners.shape[0]
    dev = lax.broadcasted_iota(jnp.int32, (devices, faces), 0).astype(F32)
    hot = jnp.where(dev == row, 1.0, 0.0).astype(jnp.bfloat16)
    at = lax.broadcasted_iota(jnp.int32, (128, faces), 0).astype(F32)
    marked = jnp.where(at == rank, target[...].astype(F32) + 1.0, 0.0).astype(jnp.bfloat16)
    owners[...] = lax.dot_general(hot, marked, NT, preferred_element_type=F32) - 1.0


def owners_kernel(got, hot_t):
    devices = got.shape[0] // 4
    lane = lax.broadcasted_iota(jnp.int32, (SLOTS, NY), 1)
    at = lax.broadcasted_iota(jnp.int32, (SLOTS, NY), 0)
    ones = jnp.ones((NY, NY), jnp.bfloat16)
    step = 8
    for d in range(0, devices, step):
        rows = [
            jnp.where(lane == at, jnp.broadcast_to(got[4 * (d + n) + 3 : 4 * (d + n) + 4], (SLOTS, NY)), 0.0)
            for n in range(step)
        ]
        block = jnp.concatenate(rows, axis=0).astype(jnp.bfloat16)
        col = jnp.dot(block, ones, preferred_element_type=F32)
        elem = lax.broadcasted_iota(jnp.int32, col.shape, 1).astype(F32)
        hot = jnp.where(col == elem, 1.0, 0.0)
        hot_t[:, d * SLOTS : (d + step) * SLOTS] = hot.T.astype(jnp.bfloat16)


def split(v):
    high = v.astype(jnp.bfloat16)
    return high, (v - high.astype(F32)).astype(jnp.bfloat16)


def put_rows(x, nb, table, send):
    kt = nb[4]

    def weighted(get, row):
        acc = None
        for a in range(8):
            term = float(D_[row, a]) * get(a)
            acc = term if acc is None else acc + term
        return acc

    getters = (lambda a: x[a], lambda a: x[:, a], lambda a: x[:, :, a, :])
    his, los = [], []
    for get in getters:
        for end, sign in ((0, 1.0), (E, -1.0)):
            flux = weighted(get, end) * (sign * kt)[None]
            block = jnp.concatenate(
                [flux.reshape(64, NY), get(end).reshape(64, NY)], axis=0
            )
            h, l = split(block)
            his.append(h)
            los.append(l)
    both = jnp.concatenate(
        [jnp.concatenate(his, axis=1), jnp.concatenate(los, axis=1)], axis=0
    )
    step = 512
    for s in range(0, send.shape[0], step):
        out = lax.dot_general(table[s : s + step], both, NT, preferred_element_type=F32)
        send[s : s + step] = out[:, :NY] + out[:, NY:]


def load_kernel(got, hot_t, out):
    acc = None
    step = 512
    for s in range(0, got.shape[0], step):
        hi, lo = split(got[s : s + step])
        hot = hot_t[:, s : s + step]
        term = jnp.dot(hot, hi, preferred_element_type=F32) + jnp.dot(
            hot, lo, preferred_element_type=F32
        )
        acc = term if acc is None else acc + term
    out[...] = acc.T


def call(body, name, outs, args, scratch=(), copied=()):
    vmem = pl.BlockSpec(memory_space=pltpu.VMEM)
    shape = lambda o: o if isinstance(o[0], tuple) else (o, F32)

    def spec(n, a):
        if n in copied:
            return pl.BlockSpec(memory_space=pltpu.HBM)
        if a.dtype == jnp.int32 and a.shape == (2,):
            return pl.BlockSpec(memory_space=pltpu.SMEM)
        return vmem

    return pl.pallas_call(
        body,
        out_shape=[jax.ShapeDtypeStruct(*shape(o)) for o in outs],
        in_specs=[spec(n, a) for n, a in enumerate(args)],
        out_specs=[vmem] * len(outs),
        scratch_shapes=[pltpu.VMEM(*shape(s)) if isinstance(s, tuple) else s for s in scratch],
        compiler_params=pltpu.CompilerParams(vmem_limit_bytes=24 * 1024 * 1024),
        cost_estimate=pl.CostEstimate(
            flops=2_000_000, bytes_accessed=1 << 20, transcendentals=0
        ),
        name=name,
    )(*args)


def pair_perms(n):
    first = [(i, i ^ 1) for i in range(n)]
    second = [(i, (i + 1) % n if i % 2 else (i - 1) % n) for i in range(n)]
    return first, second


def swap_x(pair):
    a, b = pair_perms(NX)
    return [lax.ppermute(pair[0], "row", a), lax.ppermute(pair[1], "row", b)]


def swap_z(pair):
    a, b = pair_perms(NZ)
    return [lax.ppermute(pair[0], "height", a), lax.ppermute(pair[1], "height", b)]


def everywhere(rows):
    return lax.all_to_all(rows, ("row", "height"), split_axis=0, concat_axis=0, tiled=True)


def shards(heat, conductivity, marks, face_owner, face_element, face_side, owner_element):
    devices = NX * NZ
    pos = jnp.stack([lax.axis_index("row"), lax.axis_index("height")]).astype(jnp.int32)
    row = lambda a: a.reshape(1, -1)
    line = ((1, NY), F32)
    faces = ((1, face_element.shape[0]), jnp.int32)
    f, ma, mb, cond, marks = call(
        heat_kernel,
        "heat",
        [FIELD, FACE, FACE, line, ((1, NY), jnp.int32)],
        [pos, heat.reshape(FIELD), row(conductivity), row(marks)],
        scratch=[FIELD, pltpu.SemaphoreType.DMA((3,))],
        copied=(1, 2, 3),
    )
    ra, rb = swap_x((ma, mb))
    table, owners = call(
        slots_kernel,
        "slots",
        [((devices * SLOTS, 6 * NY), jnp.bfloat16), (devices, 128)],
        [row(face_owner), row(face_element), row(face_side), row(owner_element)],
        scratch=[faces] * 4 + [pltpu.SemaphoreType.DMA((4,))],
        copied=(0, 1, 2, 3),
    )
    f, ma, mb = call(heat_z_kernel, "heat_z", [FIELD, FACE, FACE], [pos, f, ra, rb])
    ra, rb = swap_z((ma, mb))
    r, rows = call(
        first_rows_kernel,
        "first_rows",
        [FIELD, (devices, 4, NY)],
        [pos, f, ra, rb, cond, marks],
    )
    got0 = everywhere(rows).reshape(devices * 4, NY)
    kc, cc, cf, rc, nb, dinv, z, f, *msgs = call(
        setup_kernel,
        "setup",
        [COARSE, COARSE, (48, NX, NY), COARSE, (18, 8, NY), FIELD, FIELD, FIELD] + [FACE] * 4,
        [pos, got0, r],
        scratch=[COARSE],
    )
    x = p1 = p2 = s1 = s2 = rs = co = None
    for outer in range(ITERS // 2):
        first, last = outer == 0, outer == ITERS // 2 - 1
        got = swap_x(msgs[:2]) + swap_z(msgs[2:])
        w1, t, f2, *msgs = call(
            inner_kernel,
            "inner",
            [FIELD] * 3 + [FACE] * 4,
            [pos, f, *got, nb, dinv] + ([] if first else [rs]),
        )
        got = swap_x(msgs[:2]) + swap_z(msgs[2:])
        (lines,) = call(
            functools.partial(dots_kernel, first),
            "dots",
            [(16, NY)],
            [pos, z, r, t, w1] + ([] if first else [s1, s2]),
        )
        v, rows = call(
            functools.partial(rows_kernel, first),
            "rows",
            [FIELD, (devices, 4, NY)],
            [pos, f2, *got, t, lines] + ([owners] if first else []),
        )
        rows = everywhere(rows).reshape(devices * 4, NY)
        if first:
            (hot_t,) = call(
                owners_kernel, "owners", [((NY, devices * SLOTS), jnp.bfloat16)], [rows]
            )
        if last:
            break
        rn, rcn, zn, f, *msgs, con, ay, pd, q = call(
            functools.partial(step_kernel, first),
            "step",
            [FIELD, COARSE, FIELD, FIELD]
            + [FACE] * 4
            + [(9, 8, NY), FIELD, (9, 8, NY), COARSE],
            [pos, rows, r, w1, v, dinv, nb, kc, cc, cf, rc] + ([] if first else [s1, s2, rs, co]),
            scratch=[COARSE, (9 * NZ, NX, NY)],
        )
        x, p1, p2, s1, s2, rs = call(
            functools.partial(late_kernel, first),
            "late",
            [FIELD] * 5 + [(2 * NZ, NX, NY)],
            [rows, z, t, w1, ay, con, pd, q] + ([] if first else [x, p1, p2, s1, s2, rs]),
        )
        r, rc, z, co = rn, rcn, zn, con
    x, send, coef, d = call(
        last_kernel,
        "last",
        [FIELD, (devices * SLOTS, NY), (4, 8, NY), COARSE],
        [pos, rows, z, t, nb, kc, cc, cf, rc, x, p1, p2, rs, co, table],
        scratch=[(9 * NZ, NX, NY)],
    )
    got = everywhere(send.reshape(devices, SLOTS, NY))
    (r,) = call(
        residual_kernel,
        "residual",
        [FIELD],
        [pos, coef, d, v, r, w1, s1, s2, nb],
        scratch=[FIELD],
    )
    (load,) = call(
        load_kernel, "load", [(NY, NY)], [got.reshape(devices * SLOTS, NY), hot_t]
    )
    shape = (8, 8, 8, 1, 1, NY)
    return (x.reshape(shape), r.reshape(shape), load.reshape(NY, 1, 1, NY))


def solution(mesh):
    in_specs = (
        P(None, None, None, "row", "height", None),
        P("row", "height", None),
        P("row", "height", None),
        P(("row", "height"), None),
        P(("row", "height")),
        P(("row", "height")),
        P(("row", "height")),
    )
    out_specs = (
        P(None, None, None, "row", "height", None),
        P(None, None, None, "row", "height", None),
        P(None, "row", "height", None),
    )
    return jax.shard_map(shards, mesh=mesh, in_specs=in_specs, out_specs=out_specs, check_vma=False)
```

```python
import functools

import jax
import jax.numpy as jnp
import numpy as np
from jax import lax
from jax.experimental import pallas as pl
from jax.experimental.pallas import tpu as pltpu
from jax.sharding import PartitionSpec as P

ITERS = 8
HEAT_AIR = 0.02
HEAT_SOLID = 0.08
GLL_INNER = (
    -0.8717401485096066,
    -0.5917001814331423,
    -0.2092992179024789,
    0.2092992179024789,
    0.5917001814331423,
    0.8717401485096066,
)
F32 = jnp.float32
NX, NZ, NY = 8, 16, 128
FIELD = (8, 8, 8, NY)
FACE = (8, 8, NY)
COARSE = (NZ, NX, NY)


def legendre_values(points_in, degree):
    before = points_in * 0.0 + 1.0
    current = points_in * 1.0
    for order_now in range(1, degree):
        following = ((2 * order_now + 1) * points_in * current - order_now * before) / (
            order_now + 1
        )
        before = current
        current = following
    return current


def gll_tables():
    poly_order = 7
    gll_nodes = np.array((-1.0,) + GLL_INNER + (1.0,))
    edge_values = legendre_values(gll_nodes, poly_order)
    gll_weights = 2.0 / (poly_order * (poly_order + 1) * edge_values**2)
    diff_table = np.zeros((8, 8))
    for row_index in range(8):
        for col_index in range(8):
            if row_index != col_index:
                diff_table[row_index, col_index] = edge_values[row_index] / (
                    edge_values[col_index] * (gll_nodes[row_index] - gll_nodes[col_index])
                )
    diff_table[0, 0] = -poly_order * (poly_order + 1) / 4.0
    diff_table[7, 7] = poly_order * (poly_order + 1) / 4.0
    return (gll_weights, diff_table)


W_, D_ = gll_tables()
K_ = D_.T @ np.diag(W_) @ D_
S_ = np.sum(D_**2 * W_[:, None], axis=0)
W = [float(v) for v in W_]
SD = [float(v) for v in S_]
E = 7


def kvec(vals):
    k = lax.broadcasted_iota(jnp.int32, (8, NY), 0)
    out = jnp.full((8, NY), float(vals[0]), F32)
    for n in range(1, 8):
        out = jnp.where(k == n, jnp.float32(float(vals[n])), out)
    return out


def apply1d(v, mat):
    ev = [v[a] + v[7 - a] for a in range(4)]
    od = [v[a] - v[7 - a] for a in range(4)]
    out = [None] * 8
    for i in range(4):
        s = d = None
        for a in range(4):
            cs = float(0.5 * (mat[i, a] + mat[i, 7 - a]))
            cd = float(0.5 * (mat[i, a] - mat[i, 7 - a]))
            s = cs * ev[a] if s is None else s + cs * ev[a]
            d = cd * od[a] if d is None else d + cd * od[a]
        out[i] = s + d
        out[7 - i] = s - d
    return out


def place(pos_ref):
    ix, iz = pos_ref[0], pos_ref[1]
    has = (ix > 0, ix < NX - 1, iz > 0, iz < NZ - 1)
    frac = tuple(jnp.where(h, jnp.float32(0.5), jnp.float32(1.0)) for h in has)
    even = (lax.rem(ix, 2) == 0, lax.rem(iz, 2) == 0)
    return ix, iz, has, frac, even


def own_mult():
    k = lax.broadcasted_iota(jnp.int32, (8, NY), 0)
    y = lax.broadcasted_iota(jnp.int32, (8, NY), 1)
    shared = ((k == 0) & (y > 0)) | ((k == E) & (y < NY - 1))
    return jnp.where(shared, jnp.float32(0.5), jnp.float32(1.0))


def field_sum(get, frac):
    total = None
    for i in range(8):
        mid = get(i, 1)
        for j in range(2, 7):
            mid = mid + get(i, j)
        row = mid + frac[2] * get(i, 0) + frac[3] * get(i, E)
        if i == 0:
            row = frac[0] * row
        elif i == E:
            row = frac[1] * row
        total = row if total is None else total + row
    return total


def assemble_aisle(ref):
    low, high = ref[:, :, 0, :], ref[:, :, E, :]
    y = lax.broadcasted_iota(jnp.int32, FACE, 2)
    ref[:, :, 0, :] = low + jnp.where(y > 0, pltpu.roll(high, 1, 2), 0.0)
    ref[:, :, E, :] = high + jnp.where(y < NY - 1, pltpu.roll(low, NY - 1, 2), 0.0)


def add_faces_x(ref, got, has, even):
    a, b = got[0][...], got[1][...]
    ref[0] = ref[0] + jnp.where(has[0], jnp.where(even[0], b, a), 0.0)
    ref[E] = ref[E] + jnp.where(has[1], jnp.where(even[0], a, b), 0.0)


def add_faces_z(ref, got, has, even):
    a, b = got[0][...], got[1][...]
    ref[:, 0] = ref[:, 0] + jnp.where(has[2], jnp.where(even[1], b, a), 0.0)
    ref[:, E] = ref[:, E] + jnp.where(has[3], jnp.where(even[1], a, b), 0.0)


def put_pair(even, low, high, out):
    out[0][...] = jnp.where(even, high, low)
    out[1][...] = jnp.where(even, low, high)


def aisle_stiffness(block):
    turned = jnp.swapaxes(block, 0, 1)
    out = apply1d([turned[c] for c in range(8)], K_)
    return jnp.swapaxes(jnp.stack(out, axis=0), 0, 1)


def local_operator(z_ref, f_ref, nb_ref, even, msgs):
    wk = kvec(W)
    kt, ct = nb_ref[4], nb_ref[13]
    kw, cw = kt * wk, ct * wk
    w0 = W[0]
    xc = {}
    for j in range(8):
        out = apply1d([z_ref[i, j] for i in range(8)], K_)
        kwj = kw * W[j]
        res = [kwj * out[i] for i in range(8)]
        for i in range(8):
            f_ref[i, j] = res[i]
        if j in (0, E):
            xc[0, j], xc[E, j] = out[0], out[E]
    for i in range(8):
        block = z_ref[i]
        v = [block[j] for j in range(8)]
        fx = [f_ref[i, j] for j in range(8)]
        zs = apply1d(v, K_)
        ys = aisle_stiffness(block)
        kwi = kw * W[i]
        res = [
            fx[j] + kwi * zs[j] + (W[i] * W[j]) * (kt * ys[j] + cw * v[j]) for j in range(8)
        ]
        for j in range(8):
            f_ref[i, j] = res[j]
        low, high = res[0], res[E]
        if i in (0, E):
            kn = nb_ref[1 if i == 0 else 7] * (w0 * wk)
            low, high = low + kn * zs[0], high + kn * zs[E]
            for j in (0, E):
                n = 3 if j == 0 else 5
                res[j] = (
                    res[j]
                    + nb_ref[n] * (w0 * wk * xc[i, j] + (w0 * w0) * ys[j])
                    + nb_ref[9 + n] * ((w0 * w0) * wk * v[j])
                )
            up, down = (1, 0) if i == 0 else (0, 1)

            @pl.when(even[0])
            def _(res=res, to=up):
                for j in range(8):
                    msgs[to][j] = res[j]

            @pl.when(jnp.logical_not(even[0]))
            def _(res=res, to=down):
                for j in range(8):
                    msgs[to][j] = res[j]

        msgs[2][i] = jnp.where(even[1], high, low)
        msgs[3][i] = jnp.where(even[1], low, high)


def thomas(cf_ref, rhs):
    dp = []
    for h in range(NZ):
        v = rhs[h] if h == 0 else rhs[h] - cf_ref[h] * dp[h - 1]
        dp.append(v * cf_ref[32 + h])
    for h in range(NZ - 2, -1, -1):
        dp[h] = dp[h] - cf_ref[16 + h] * dp[h + 1]
    return dp


def coarse_dot(a, b):
    acc = None
    for u, v in zip(a, b):
        acc = u * v if acc is None else acc + u * v
    return spread_sum(acc)


def spread_sum(tile):
    row = jnp.broadcast_to(jnp.sum(tile, axis=0, keepdims=True), (8, NY))
    return jnp.broadcast_to(jnp.sum(row, axis=1, keepdims=True), (8, NY))


def shift_pair(v, axis):
    n = v.shape[axis]
    p = lax.broadcasted_iota(jnp.int32, v.shape, axis)
    before = jnp.where(p == 0, v, pltpu.roll(v, 1, axis))
    after = jnp.where(p == n - 1, v, pltpu.roll(v, n - 1, axis))
    return before, after


MID, FACE_MU = 2.0 - 2.0 * W[0], 2.0 * W[0]
SYM_F = (MID / (2.0 * FACE_MU)) ** 0.5
SYM_M = -((FACE_MU / (2.0 * MID)) ** 0.5)
A0, B0 = (MID + FACE_MU / 2.0) / 2.0**0.5, FACE_MU / (4.0 * 2.0**0.5)
A1, B1 = -SYM_F * FACE_MU / 2.0, SYM_F * FACE_MU / 4.0
C2 = FACE_MU**0.5 / 4.0
LAM = (
    0.0,
    float(2.0 * (K_[0, 0] + K_[0, 7])) * (SYM_F - SYM_M) ** 2,
    float(2.0 * (K_[0, 0] - K_[0, 7])) / FACE_MU,
)


def spread3(v, before, after):
    both = before + after
    return (A0 * v + B0 * both, A1 * v + B1 * both, C2 * (before - after))


def back3(duals):
    t, u = B0 * duals[0] + B1 * duals[1], C2 * duals[2]
    return A0 * duals[0] + A1 * duals[1], t + u, t - u


def gather3(duals, axis):
    own, g, h = back3(duals)
    n = own.shape[axis]
    p = lax.broadcasted_iota(jnp.int32, own.shape, axis)
    up = jnp.where(p == n - 1, h, pltpu.roll(g, n - 1, axis))
    down = jnp.where(p == 0, g, pltpu.roll(h, 1, axis))
    return own + (up + down)


def coarse_operator(d, kc_ref, cc_ref, tmp_ref):
    for h in range(NZ):
        ys = spread3(d[h], *shift_pair(d[h], 1))
        for c in range(3):
            xs = spread3(ys[c], *shift_pair(ys[c], 0))
            for a in range(3):
                tmp_ref[(a * 3 + c) * NZ + h] = xs[a]
    keys = [(a, c) for a in range(3) for c in range(3)]
    res, kept, after = [], {}, {}

    def finish(vals):
        return gather3([gather3([vals[a, c] for a in range(3)], 0) for c in range(3)], 1)

    for h in range(NZ):
        lo, hi = max(h - 1, 0), min(h + 1, NZ - 1)
        kh, ch = kc_ref[h], cc_ref[h]
        factor, final = {}, {}
        for a, c in keys:
            base = (a * 3 + c) * NZ
            zs = spread3(tmp_ref[base + h], tmp_ref[base + lo], tmp_ref[base + hi])
            duals = []
            for b in range(3):
                kind = tuple(sorted((a, b, c)))
                if kind not in factor:
                    lam = sum(LAM[n] for n in kind)
                    factor[kind] = kh * lam + ch if lam else ch
                duals.append(factor[kind] * zs[b])
            own, g, hh = back3(duals)
            if h > 0:
                final[a, c] = kept[a, c] + g
                own = own + after[a, c]
            else:
                own = own + g
            if h == NZ - 1:
                own = own + hh
            kept[a, c], after[a, c] = own, hh
        if h > 0:
            res.append(finish(final))
    res.append(finish(kept))
    return res


def coarse_row(ref, ix, iz, dx, dz):
    x = jnp.clip(ix + dx, 0, NX - 1)
    z = jnp.clip(iz + dz, 0, NZ - 1)
    return ref[z, pl.ds(x, 1), :]


def aisle_tiles(row, want_stiff):
    c = jnp.broadcast_to(row, (8, NY))
    before, after = shift_pair(c, 1)
    k = lax.broadcasted_iota(jnp.int32, (8, NY), 0)
    low, high = 0.5 * (c + before), 0.5 * (c + after)
    tile = jnp.where(k == 0, low, jnp.where(k == E, high, c))
    if not want_stiff:
        return tile, None
    return tile, kvec(K_[:, 0]) * (low - c) + kvec(K_[:, 7]) * (high - c)


def classes(tiles, reach):
    n = 2 * reach + 1
    m = 2 * n - 3

    def line(vals):
        out = []
        for p in range(m):
            if p % 2 == 0:
                out.append(0.5 * (vals[p // 2] + vals[p // 2 + 1]))
            else:
                out.append(vals[p // 2 + 1])
        return out

    cols = [line(tiles[dx]) for dx in range(n)]
    by_q = [line([cols[dx][q] for dx in range(n)]) for q in range(m)]
    return [[by_q[q][p] for q in range(m)] for p in range(m)]


def cls(i):
    return 0 if i == 0 else (2 if i == E else 1)


def own_prolong(ref, ix, iz):
    tiles = [
        [aisle_tiles(coarse_row(ref, ix, iz, dx, dz), False)[0] for dz in (-1, 0, 1)]
        for dx in (-1, 0, 1)
    ]
    return classes(tiles, 1)


def add_operator_of_prolong(ref, ix, iz, nb_ref, out_ref):
    tv, ty = [], []
    for dx in range(-2, 3):
        pair = [aisle_tiles(coarse_row(ref, ix, iz, dx, dz), True) for dz in range(-2, 3)]
        tv.append([p[0] for p in pair])
        ty.append([p[1] for p in pair])
    v, yv = classes(tv, 2), classes(ty, 2)
    wk = kvec(W)

    def parts(ex, ez):
        p, q = 2 + 2 * ex, 2 + 2 * ez
        n = (ex + 1) * 3 + ez + 1
        kt, ct = nb_ref[n], nb_ref[9 + n]
        kw, cw = kt * wk, ct * wk
        memo = {}

        def once(key, make):
            if key not in memo:
                memo[key] = make()
            return memo[key]

        def along(i, a, b, c):
            return kw * (float(K_[i, 0]) * (a - b) + float(K_[i, 7]) * (c - b))

        def tile(i, j):
            a, b = cls(i), cls(j)
            xt = once(
                ("x", i, b), lambda: along(i, v[p][q + b], v[p + 1][q + b], v[p + 2][q + b])
            )
            zt = once(
                ("z", a, j), lambda: along(j, v[p + a][q], v[p + a][q + 1], v[p + a][q + 2])
            )
            yt = once(("y", a, b), lambda: kt * yv[p + a][q + b] + cw * v[p + a][q + b])
            return W[j] * xt + W[i] * zt + (W[i] * W[j]) * yt

        return tile

    part = {(ex, ez): parts(ex, ez) for ex in (-1, 0, 1) for ez in (-1, 0, 1)}
    for i in range(8):
        new = []
        for j in range(8):
            acc = out_ref[i, j] + part[0, 0](i, j)
            ex = -1 if i == 0 else (1 if i == E else 0)
            ez = -1 if j == 0 else (1 if j == E else 0)
            if ex:
                acc = acc + part[ex, 0](7 - i, j)
            if ez:
                acc = acc + part[0, ez](i, 7 - j)
            if ex and ez:
                acc = acc + part[ex, ez](7 - i, 7 - j)
            new.append(acc)
        for j in range(8):
            out_ref[i, j] = new[j]
    return [[v[2 + a][2 + b] for b in range(3)] for a in range(3)]


def make_z(c_ref, ix, iz, r_ref, dinv_ref, z_ref):
    pc = own_prolong(c_ref, ix, iz)
    for i in range(8):
        new = [r_ref[i, j] * dinv_ref[i, j] + pc[cls(i)][cls(j)] for j in range(8)]
        for j in range(8):
            z_ref[i, j] = new[j]


def coarse_rows_of(got_ref, which):
    return [got_ref[pl.ds(4 * h + which, NX, stride=4 * NZ), :] for h in range(NZ)]


def heat_kernel(pos, heat, f, ma, mb):
    _, _, _, _, even = place(pos)
    wk = kvec(W)
    for i in range(8):
        new = [(W[i] * W[j]) * wk * heat[i, j] for j in range(8)]
        for j in range(8):
            f[i, j] = new[j]
    put_pair(even[0], f[0], f[E], (ma, mb))


def heat_z_kernel(pos, f, ra, rb, out, ma, mb):
    _, _, has, _, even = place(pos)
    out[...] = f[...]
    add_faces_x(out, (ra, rb), has, even)
    put_pair(even[1], out[:, 0], out[:, E], (ma, mb))


def first_rows_kernel(pos, f, ra, rb, both, out, rows):
    _, _, has, frac, even = place(pos)
    out[...] = f[...]
    add_faces_z(out, (ra, rb), has, even)
    assemble_aisle(out)
    tile = field_sum(lambda i, j: out[i, j], frac) * own_mult()
    restricted = jnp.sum(tile, axis=0, keepdims=True)
    cap = jnp.where(both[1:2] == 1.0, jnp.float32(HEAT_SOLID), jnp.float32(HEAT_AIR))
    block = jnp.concatenate([both[0:1], cap, restricted, jnp.zeros((1, NY), F32)], axis=0)
    rows[...] = jnp.broadcast_to(block[None], rows.shape)


def setup_kernel(
    pos, got, r, kc, cc, cf, rc, nb, dinv, z, f, m0, m1, m2, m3, c_tmp
):
    ix, iz, has, frac, even = place(pos)
    k_all, c_all, r_all = (coarse_rows_of(got, n) for n in range(3))
    for h in range(NZ):
        kc[h], cc[h], rc[h] = k_all[h], c_all[h], r_all[h]
    link = [2.0 * k_all[h] * k_all[h + 1] / (k_all[h] + k_all[h + 1]) for h in range(NZ - 1)]
    above = None
    for h in range(NZ):
        main = 8.0 * c_all[h]
        if h > 0:
            main = main + link[h - 1]
        if h < NZ - 1:
            main = main + link[h]
        low = -link[h - 1] if h > 0 else jnp.zeros((NX, NY), F32)
        piv = main if h == 0 else main - low * above
        inv = 1.0 / piv
        above = -link[h] * inv if h < NZ - 1 else jnp.zeros((NX, NY), F32)
        cf[h], cf[16 + h], cf[32 + h] = low, above, inv
    for ex in (-1, 0, 1):
        for ez in (-1, 0, 1):
            n = (ex + 1) * 3 + ez + 1
            there = None
            if ex:
                there = has[0] if ex < 0 else has[1]
            if ez:
                hz = has[2] if ez < 0 else has[3]
                there = hz if there is None else there & hz
            for base, src in ((0, kc), (9, cc)):
                tile = jnp.broadcast_to(coarse_row(src, ix, iz, ex, ez), (8, NY))
                nb[base + n] = tile if there is None else jnp.where(there, tile, 0.0)
    wk, sk = kvec(W), kvec(SD)
    for i in range(8):
        for j in range(8):
            ex = -1 if i == 0 else (1 if i == E else 0)
            ez = -1 if j == 0 else (1 if j == E else 0)
            kt, ct = nb[4], nb[13]
            for n in {4 + 3 * ex, 4 + ez, 4 + 3 * ex + ez} - {4}:
                kt, ct = kt + nb[n], ct + nb[9 + n]
            dinv[i, j] = (
                kt * ((SD[i] * W[j] + W[i] * SD[j]) * wk + (W[i] * W[j]) * sk)
                + ct * ((W[i] * W[j]) * wk)
            )
    assemble_aisle(dinv)
    dinv[...] = 1.0 / dinv[...]
    solved = thomas(cf, r_all)
    for h in range(NZ):
        c_tmp[h] = solved[h]
    make_z(c_tmp, ix, iz, r, dinv, z)
    local_operator(z, f, nb, even, (m0, m1, m2, m3))


def inner_kernel(pos, f, r0, r1, r2, r3, nb, dinv, *refs):
    w1, t, f2, m0, m1, m2, m3 = refs[-7:]
    _, _, has, _, even = place(pos)
    w1[...] = f[...]
    add_faces_x(w1, (r0, r1), has, even)
    add_faces_z(w1, (r2, r3), has, even)
    assemble_aisle(w1)
    t[...] = w1[...] * dinv[...]
    local_operator(t, f2, nb, even, (m0, m1, m2, m3))


def dots_kernel(first, *refs):
    if first:
        pos, z, r, t, w1, lines = refs
    else:
        pos, z, r, t, w1, s1, s2, lines = refs
    _, _, _, frac, _ = place(pos)
    my = own_mult()
    zero = jnp.zeros((1, NY), F32)

    def dot(a, b):
        tile = my * field_sum(lambda i, j: a[i, j] * b[i, j], frac)
        return jnp.sum(tile, axis=0, keepdims=True)

    out = [dot(z, r), dot(t, r), dot(z, w1), dot(t, w1), zero]
    out += [zero] * 4 if first else [dot(z, s1), dot(z, s2), dot(t, s1), dot(t, s2)]
    out += [zero] * 6
    out.append(jnp.sum(field_sum(lambda i, j: w1[i, j], frac) * my, axis=0, keepdims=True))
    lines[...] = jnp.concatenate(out, axis=0)


def rows_kernel(first, *refs):
    if first:
        pos, f2, r0, r1, r2, r3, t, lines, owners, v, rows = refs
    else:
        pos, f2, r0, r1, r2, r3, t, lines, v, rows = refs
    _, _, has, frac, even = place(pos)
    v[...] = f2[...]
    add_faces_x(v, (r0, r1), has, even)
    add_faces_z(v, (r2, r3), has, even)
    my = own_mult()
    tv = jnp.sum(field_sum(lambda i, j: t[i, j] * v[i, j], frac), axis=0, keepdims=True)
    lane = lax.broadcasted_iota(jnp.int32, (16, NY), 1)
    at = lax.broadcasted_iota(jnp.int32, (16, NY), 0)
    stacked = jnp.where(at == 4, jnp.broadcast_to(tv, (16, NY)), lines[...])
    totals = jnp.broadcast_to(jnp.sum(stacked, axis=1, keepdims=True), (16, NY))
    dots = jnp.sum(jnp.where(lane == at, totals, 0.0), axis=0, keepdims=True)
    vt = field_sum(lambda i, j: v[i, j], frac)
    k = lax.broadcasted_iota(jnp.int32, (8, NY), 0)
    y = lax.broadcasted_iota(jnp.int32, (8, NY), 1)
    vlow = jnp.broadcast_to(vt[0:1], (8, NY))
    vhigh = jnp.broadcast_to(vt[7:8], (8, NY))
    vt = vt + jnp.where((k == 0) & (y > 0), pltpu.roll(vhigh, 1, 1), 0.0)
    vt = vt + jnp.where((k == E) & (y < NY - 1), pltpu.roll(vlow, NY - 1, 1), 0.0)
    g2 = jnp.sum(vt * my, axis=0, keepdims=True)
    block = jnp.concatenate([lines[15:16], g2, dots, jnp.zeros((1, NY), F32)], axis=0)
    rows[...] = jnp.broadcast_to(block[None], rows.shape)
    if first:
        rows[:, 3, :] = owners[...]


def coefficients(first, got, d, q, rc, rs, wp, cf):
    total = got[0:8]
    for n in range(8, NX * NZ * 4, 8):
        total = total + got[n : n + 8]
    dots = jnp.broadcast_to(total[2:3] + total[6:7], (8, NY))
    lane = lax.broadcasted_iota(jnp.int32, (8, NY), 1)

    def pick(n):
        return jnp.broadcast_to(
            jnp.sum(jnp.where(lane == n, dots, 0.0), axis=1, keepdims=True), (8, NY)
        )

    g1, g2 = coarse_rows_of(got, 0), coarse_rows_of(got, 1)
    b1, b2 = pick(0), pick(1) + coarse_dot(d, [rc[h] for h in range(NZ)])
    w11 = pick(2)
    w12 = pick(3) + coarse_dot(d, g1)
    w22 = pick(4) + 2.0 * coarse_dot(d, g2) + coarse_dot(d, q)
    e = [None] * 4
    if not first:
        rs1, rs2 = [rs[h] for h in range(NZ)], [rs[NZ + h] for h in range(NZ)]
        c11, c21 = pick(5), pick(6)
        c12, c22 = pick(7) + coarse_dot(d, rs1), pick(8) + coarse_dot(d, rs2)
        pa, pb, pc = wp[6], wp[7], wp[8]
        inv = -1.0 / (pa * pc - pb * pb)
        e11, e21 = (pc * c11 - pb * c21) * inv, (pa * c21 - pb * c11) * inv
        e12, e22 = (pc * c12 - pb * c22) * inv, (pa * c22 - pb * c12) * inv
        w11 = w11 + c11 * e11 + c21 * e21
        w12 = w12 + c11 * e12 + c21 * e22
        w22 = w22 + c12 * e12 + c22 * e22
        e = [e11, e21, e12, e22]
    inv = 1.0 / (w11 * w22 - w12 * w12)
    a1 = (w22 * b1 - w12 * b2) * inv
    a2 = (w11 * b2 - w12 * b1) * inv
    return a1, a2, e, (w11, w12, w22), g1, g2


def new_residual(first, a1, a2, x1, x2, r, w1, ay, s1, s2, out):
    for i in range(8):
        new = []
        for j in range(8):
            v = r[i, j] - (a1 * w1[i, j] + a2 * ay[i, j])
            if not first:
                v = v - (x1 * s1[i, j] + x2 * s2[i, j])
            new.append(v)
        for j in range(8):
            out[i, j] = new[j]


def step_kernel(first, *refs):
    refs = list(refs)
    take = lambda n: [refs.pop(0) for _ in range(n)]
    pos, got, r, w1, v, dinv, nb, kc, cc, cf, rc = take(11)
    s1 = s2 = rs = wp = None
    if not first:
        s1, s2, rs, wp = take(4)
    ro, rco, zo, fo, m0, m1, m2, m3, co, ay, pdo, qo = take(12)
    c_tmp, tmp = take(2)
    ix, iz, has, frac, even = place(pos)
    d = thomas(cf, coarse_rows_of(got, 0))
    for h in range(NZ):
        c_tmp[h] = d[h]
    q = coarse_operator(d, kc, cc, tmp)
    a1, a2, e, w, g1, g2 = coefficients(first, got, d, q, rc, rs, wp, cf)
    x1 = x2 = None
    if not first:
        x1, x2 = a1 * e[0] + a2 * e[2], a1 * e[1] + a2 * e[3]
    for n, val in enumerate((a1, a2, *e, *w)):
        if val is not None:
            co[n] = val
        else:
            co[n] = jnp.zeros((8, NY), F32)
    ay[...] = v[...]
    pd = add_operator_of_prolong(c_tmp, ix, iz, nb, ay)
    for n in range(9):
        pdo[n] = pd[n // 3][n % 3]
    assemble_aisle(ay)
    new_residual(first, a1, a2, x1, x2, r, w1, ay, s1, s2, ro)
    rnew = []
    for h in range(NZ):
        qo[h] = q[h]
        new = rc[h] - (a1 * g1[h] + a2 * (g2[h] + q[h]))
        if not first:
            new = new - (x1 * rs[h] + x2 * rs[NZ + h])
        rco[h] = new
        rnew.append(new)
    solved = thomas(cf, rnew)
    for h in range(NZ):
        c_tmp[h] = solved[h]
    make_z(c_tmp, ix, iz, ro, dinv, zo)
    local_operator(zo, fo, nb, even, (m0, m1, m2, m3))


def new_x(first, a1, a2, x1, x2, z, t, pd, p1, p2, x, out):
    for i in range(8):
        new = []
        for j in range(8):
            up = a1 * z[i, j] + a2 * (t[i, j] + pd(i, j))
            if not first:
                up = x[i, j] + (up + (x1 * p1[i, j] + x2 * p2[i, j]))
            new.append(up)
        for j in range(8):
            out[i, j] = new[j]


def late_kernel(first, *refs):
    refs = list(refs)
    take = lambda n: [refs.pop(0) for _ in range(n)]
    got, z, t, w1, ay, co, pdt, q = take(8)
    x = p1 = p2 = s1 = s2 = rs = None
    if not first:
        x, p1, p2, s1, s2, rs = take(6)
    xo, p1o, p2o, s1o, s2o, rso = take(6)
    a1, a2, e11, e21, e12, e22 = (co[n] for n in range(6))
    x1, x2 = a1 * e11 + a2 * e12, a1 * e21 + a2 * e22
    pd = lambda i, j: pdt[3 * cls(i) + cls(j)]
    new_x(first, a1, a2, x1, x2, z, t, pd, p1, p2, x, xo)

    def block(one, two, prev1, prev2, out1, out2):
        for i in range(8):
            new = []
            for j in range(8):
                n1, n2 = one(i, j), two(i, j)
                if not first:
                    u, w = prev1[i, j], prev2[i, j]
                    n1, n2 = n1 + e11 * u + e21 * w, n2 + e12 * u + e22 * w
                new.append((n1, n2))
            for j in range(8):
                out1[i, j], out2[i, j] = new[j]

    block(lambda i, j: z[i, j], lambda i, j: t[i, j] + pd(i, j), p1, p2, p1o, p2o)
    block(lambda i, j: w1[i, j], lambda i, j: ay[i, j], s1, s2, s1o, s2o)
    g1, g2 = coarse_rows_of(got, 0), coarse_rows_of(got, 1)
    for h in range(NZ):
        n1, n2 = g1[h], g2[h] + q[h]
        if not first:
            u, w = rs[h], rs[NZ + h]
            n1, n2 = n1 + e11 * u + e21 * w, n2 + e12 * u + e22 * w
        rso[h], rso[NZ + h] = n1, n2


def last_kernel(pos, got, z, t, nb, kc, cc, cf, rc, x, p1, p2, rs, wp, table, xo, send, co, dc, tmp):
    ix, iz, _, _, _ = place(pos)
    d = thomas(cf, coarse_rows_of(got, 0))
    for h in range(NZ):
        dc[h] = d[h]
    q = coarse_operator(d, kc, cc, tmp)
    a1, a2, e, _, _, _ = coefficients(False, got, d, q, rc, rs, wp, cf)
    x1, x2 = a1 * e[0] + a2 * e[2], a1 * e[1] + a2 * e[3]
    for n, val in enumerate((a1, a2, x1, x2)):
        co[n] = val
    own = own_prolong(dc, ix, iz)
    pd = lambda i, j: own[cls(i)][cls(j)]
    new_x(False, a1, a2, x1, x2, z, t, pd, p1, p2, x, xo)
    put_rows(xo, nb, table, send)


def residual_kernel(pos, co, dc, v, r, w1, s1, s2, nb, ro, ay):
    ix, iz, _, _, _ = place(pos)
    ay[...] = v[...]
    add_operator_of_prolong(dc, ix, iz, nb, ay)
    assemble_aisle(ay)
    new_residual(False, co[0], co[1], co[2], co[3], r, w1, ay, s1, s2, ro)


NT = (((1,), (1,)), ((), ()))
SLOTS = 16


def slots_kernel(ints, table, owners):
    own, elem, side, target = (ints[n : n + 1] for n in range(4))
    faces = own.shape[1]
    row = own.astype(F32)
    col = jnp.broadcast_to(row, (NY, faces)).T
    ranks = []
    for s in range(0, faces, NY):
        f = lax.broadcasted_iota(jnp.int32, (faces, NY), 0)
        g = lax.broadcasted_iota(jnp.int32, (faces, NY), 1) + s
        same = (col == row[:, s : s + NY]) & (f < g)
        ranks.append(jnp.sum(jnp.where(same, 1.0, 0.0), axis=0, keepdims=True))
    rank = jnp.concatenate(ranks, axis=1)
    slot = row * SLOTS + rank
    vals = jnp.concatenate(
        [elem.astype(F32) + 1.0, side.astype(F32), jnp.zeros((6, faces), F32)], axis=0
    ).astype(jnp.bfloat16)
    step = 256
    for s in range(0, table.shape[0], step):
        at = lax.broadcasted_iota(jnp.int32, (step, faces), 0).astype(F32) + float(s)
        hot = jnp.where(at == slot, 1.0, 0.0).astype(jnp.bfloat16)
        got = lax.dot_general(hot, vals, NT, preferred_element_type=F32)
        pick = got[:, 0:1] - 1.0 + 128.0 * got[:, 1:2]
        lane = lax.broadcasted_iota(jnp.int32, (step, table.shape[1]), 1).astype(F32)
        table[s : s + step] = jnp.where(lane == pick, 1.0, 0.0).astype(jnp.bfloat16)
    devices = owners.shape[0]
    dev = lax.broadcasted_iota(jnp.int32, (devices, faces), 0).astype(F32)
    hot = jnp.where(dev == row, 1.0, 0.0).astype(jnp.bfloat16)
    at = lax.broadcasted_iota(jnp.int32, (128, faces), 0).astype(F32)
    marked = jnp.where(at == rank, target.astype(F32) + 1.0, 0.0).astype(jnp.bfloat16)
    owners[...] = lax.dot_general(hot, marked, NT, preferred_element_type=F32) - 1.0


def owners_kernel(got, hot_t):
    devices = got.shape[0] // 4
    lane = lax.broadcasted_iota(jnp.int32, (SLOTS, NY), 1)
    at = lax.broadcasted_iota(jnp.int32, (SLOTS, NY), 0)
    ones = jnp.ones((NY, NY), jnp.bfloat16)
    step = 8
    for d in range(0, devices, step):
        rows = [
            jnp.where(lane == at, jnp.broadcast_to(got[4 * (d + n) + 3 : 4 * (d + n) + 4], (SLOTS, NY)), 0.0)
            for n in range(step)
        ]
        block = jnp.concatenate(rows, axis=0).astype(jnp.bfloat16)
        col = jnp.dot(block, ones, preferred_element_type=F32)
        elem = lax.broadcasted_iota(jnp.int32, col.shape, 1).astype(F32)
        hot = jnp.where(col == elem, 1.0, 0.0)
        hot_t[:, d * SLOTS : (d + step) * SLOTS] = hot.T.astype(jnp.bfloat16)


def split(v):
    high = v.astype(jnp.bfloat16)
    return high, (v - high.astype(F32)).astype(jnp.bfloat16)


def put_rows(x, nb, table, send):
    kt = nb[4]

    def weighted(get, row):
        acc = None
        for a in range(8):
            term = float(D_[row, a]) * get(a)
            acc = term if acc is None else acc + term
        return acc

    getters = (lambda a: x[a], lambda a: x[:, a], lambda a: x[:, :, a, :])
    his, los = [], []
    for get in getters:
        for end, sign in ((0, 1.0), (E, -1.0)):
            flux = weighted(get, end) * (sign * kt)[None]
            block = jnp.concatenate(
                [flux.reshape(64, NY), get(end).reshape(64, NY)], axis=0
            )
            h, l = split(block)
            his.append(h)
            los.append(l)
    both = jnp.concatenate(
        [jnp.concatenate(his, axis=1), jnp.concatenate(los, axis=1)], axis=0
    )
    step = 512
    for s in range(0, send.shape[0], step):
        out = lax.dot_general(table[s : s + step], both, NT, preferred_element_type=F32)
        send[s : s + step] = out[:, :NY] + out[:, NY:]


def load_kernel(got, hot_t, out):
    acc = None
    step = 512
    for s in range(0, got.shape[0], step):
        hi, lo = split(got[s : s + step])
        hot = hot_t[:, s : s + step]
        term = jnp.dot(hot, hi, preferred_element_type=F32) + jnp.dot(
            hot, lo, preferred_element_type=F32
        )
        acc = term if acc is None else acc + term
    out[...] = acc.T


def call(body, name, outs, args, scratch=()):
    vmem = pl.BlockSpec(memory_space=pltpu.VMEM)
    smem = pl.BlockSpec(memory_space=pltpu.SMEM)
    shape = lambda o: o if isinstance(o[0], tuple) else (o, F32)
    scalars = lambda a: a.dtype == jnp.int32 and a.shape == (2,)
    return pl.pallas_call(
        body,
        out_shape=[jax.ShapeDtypeStruct(*shape(o)) for o in outs],
        in_specs=[smem if scalars(a) else vmem for a in args],
        out_specs=[vmem] * len(outs),
        scratch_shapes=[pltpu.VMEM(s, F32) for s in scratch],
        compiler_params=pltpu.CompilerParams(vmem_limit_bytes=24 * 1024 * 1024),
        cost_estimate=pl.CostEstimate(
            flops=2_000_000, bytes_accessed=1 << 20, transcendentals=0
        ),
        name=name,
    )(*args)


def pairs(axis, second):
    out = []
    for x in range(NX):
        for z in range(NZ):
            here = [x, z]
            n, last = here[axis], (NX, NZ)[axis] - 1
            if not second:
                here[axis] = n ^ 1
            elif n in (0, last):
                here[1 - axis] ^= 1
            else:
                here[axis] = n + 1 if n % 2 else n - 1
            out.append((x * NZ + z, here[0] * NZ + here[1]))
    return out


def swap(pair, axis):
    return [lax.ppermute(v, ("row", "height"), pairs(axis, n == 1)) for n, v in enumerate(pair)]


def swap_x(pair):
    return swap(pair, 0)


def swap_z(pair):
    return swap(pair, 1)


def everywhere(rows):
    return lax.all_to_all(rows, ("row", "height"), split_axis=0, concat_axis=0, tiled=True)


def shards(heat, conductivity, marks, face_owner, face_element, face_side, owner_element):
    devices = NX * NZ
    pos = jnp.stack([lax.axis_index("row"), lax.axis_index("height")]).astype(jnp.int32)
    f, ma, mb = call(heat_kernel, "heat", [FIELD, FACE, FACE], [pos, heat.reshape(FIELD)])
    ra, rb = swap_x((ma, mb))
    both = jnp.stack([conductivity.reshape(-1), marks.reshape(-1).astype(F32)])
    ints = jnp.stack([face_owner.reshape(-1), face_element, face_side, owner_element])
    table, owners = call(
        slots_kernel,
        "slots",
        [((devices * SLOTS, 6 * NY), jnp.bfloat16), (devices, 128)],
        [ints],
    )
    f, ma, mb = call(heat_z_kernel, "heat_z", [FIELD, FACE, FACE], [pos, f, ra, rb])
    ra, rb = swap_z((ma, mb))
    r, rows = call(
        first_rows_kernel,
        "first_rows",
        [FIELD, (devices, 4, NY)],
        [pos, f, ra, rb, both],
    )
    got0 = everywhere(rows).reshape(devices * 4, NY)
    kc, cc, cf, rc, nb, dinv, z, f, *msgs = call(
        setup_kernel,
        "setup",
        [COARSE, COARSE, (48, NX, NY), COARSE, (18, 8, NY), FIELD, FIELD, FIELD] + [FACE] * 4,
        [pos, got0, r],
        scratch=[COARSE],
    )
    x = p1 = p2 = s1 = s2 = rs = co = None
    for outer in range(ITERS // 2):
        first, last = outer == 0, outer == ITERS // 2 - 1
        got = swap_x(msgs[:2]) + swap_z(msgs[2:])
        w1, t, f2, *msgs = call(
            inner_kernel,
            "inner",
            [FIELD] * 3 + [FACE] * 4,
            [pos, f, *got, nb, dinv] + ([] if first else [rs]),
        )
        got = swap_x(msgs[:2]) + swap_z(msgs[2:])
        (lines,) = call(
            functools.partial(dots_kernel, first),
            "dots",
            [(16, NY)],
            [pos, z, r, t, w1] + ([] if first else [s1, s2]),
        )
        v, rows = call(
            functools.partial(rows_kernel, first),
            "rows",
            [FIELD, (devices, 4, NY)],
            [pos, f2, *got, t, lines] + ([owners] if first else []),
        )
        rows = everywhere(rows).reshape(devices * 4, NY)
        if first:
            (hot_t,) = call(
                owners_kernel, "owners", [((NY, devices * SLOTS), jnp.bfloat16)], [rows]
            )
        if last:
            break
        rn, rcn, zn, f, *msgs, con, ay, pd, q = call(
            functools.partial(step_kernel, first),
            "step",
            [FIELD, COARSE, FIELD, FIELD]
            + [FACE] * 4
            + [(9, 8, NY), FIELD, (9, 8, NY), COARSE],
            [pos, rows, r, w1, v, dinv, nb, kc, cc, cf, rc] + ([] if first else [s1, s2, rs, co]),
            scratch=[COARSE, (9 * NZ, NX, NY)],
        )
        x, p1, p2, s1, s2, rs = call(
            functools.partial(late_kernel, first),
            "late",
            [FIELD] * 5 + [(2 * NZ, NX, NY)],
            [rows, z, t, w1, ay, con, pd, q] + ([] if first else [x, p1, p2, s1, s2, rs]),
        )
        r, rc, z, co = rn, rcn, zn, con
    x, send, coef, d = call(
        last_kernel,
        "last",
        [FIELD, (devices * SLOTS, NY), (4, 8, NY), COARSE],
        [pos, rows, z, t, nb, kc, cc, cf, rc, x, p1, p2, rs, co, table],
        scratch=[(9 * NZ, NX, NY)],
    )
    got = everywhere(send.reshape(devices, SLOTS, NY))
    (r,) = call(
        residual_kernel,
        "residual",
        [FIELD],
        [pos, coef, d, v, r, w1, s1, s2, nb],
        scratch=[FIELD],
    )
    (load,) = call(
        load_kernel, "load", [(NY, NY)], [got.reshape(devices * SLOTS, NY), hot_t]
    )
    shape = (8, 8, 8, 1, 1, NY)
    return (x.reshape(shape), r.reshape(shape), load.reshape(NY, 1, 1, NY))


def solution(mesh):
    in_specs = (
        P(None, None, None, "row", "height", None),
        P("row", "height", None),
        P("row", "height", None),
        P(("row", "height"), None),
        P(("row", "height")),
        P(("row", "height")),
        P(("row", "height")),
    )
    out_specs = (
        P(None, None, None, "row", "height", None),
        P(None, None, None, "row", "height", None),
        P(None, "row", "height", None),
    )
    return jax.shard_map(shards, mesh=mesh, in_specs=in_specs, out_specs=out_specs, check_vma=False)
```

```python
import functools

import jax
import jax.numpy as jnp
import numpy as np
from jax import lax
from jax.experimental import pallas as pl
from jax.experimental.pallas import tpu as pltpu
from jax.sharding import PartitionSpec as P

ITERS = 8
HEAT_AIR = 0.02
HEAT_SOLID = 0.08
GLL_INNER = (
    -0.8717401485096066,
    -0.5917001814331423,
    -0.2092992179024789,
    0.2092992179024789,
    0.5917001814331423,
    0.8717401485096066,
)
F32 = jnp.float32
NX, NZ, NY = 8, 16, 128
FIELD = (8, 8, 8, NY)
FACE = (8, 8, NY)
COARSE = (NZ, NX, NY)


def legendre_values(points_in, degree):
    before = points_in * 0.0 + 1.0
    current = points_in * 1.0
    for order_now in range(1, degree):
        following = ((2 * order_now + 1) * points_in * current - order_now * before) / (
            order_now + 1
        )
        before = current
        current = following
    return current


def gll_tables():
    poly_order = 7
    gll_nodes = np.array((-1.0,) + GLL_INNER + (1.0,))
    edge_values = legendre_values(gll_nodes, poly_order)
    gll_weights = 2.0 / (poly_order * (poly_order + 1) * edge_values**2)
    diff_table = np.zeros((8, 8))
    for row_index in range(8):
        for col_index in range(8):
            if row_index != col_index:
                diff_table[row_index, col_index] = edge_values[row_index] / (
                    edge_values[col_index] * (gll_nodes[row_index] - gll_nodes[col_index])
                )
    diff_table[0, 0] = -poly_order * (poly_order + 1) / 4.0
    diff_table[7, 7] = poly_order * (poly_order + 1) / 4.0
    return (gll_weights, diff_table)


W_, D_ = gll_tables()
K_ = D_.T @ np.diag(W_) @ D_
S_ = np.sum(D_**2 * W_[:, None], axis=0)
W = [float(v) for v in W_]
SD = [float(v) for v in S_]
E = 7


def kvec(vals):
    k = lax.broadcasted_iota(jnp.int32, (8, NY), 0)
    out = jnp.full((8, NY), float(vals[0]), F32)
    for n in range(1, 8):
        out = jnp.where(k == n, jnp.float32(float(vals[n])), out)
    return out


def apply1d(v, mat):
    ev = [v[a] + v[7 - a] for a in range(4)]
    od = [v[a] - v[7 - a] for a in range(4)]
    out = [None] * 8
    for i in range(4):
        s = d = None
        for a in range(4):
            cs = float(0.5 * (mat[i, a] + mat[i, 7 - a]))
            cd = float(0.5 * (mat[i, a] - mat[i, 7 - a]))
            s = cs * ev[a] if s is None else s + cs * ev[a]
            d = cd * od[a] if d is None else d + cd * od[a]
        out[i] = s + d
        out[7 - i] = s - d
    return out


def place(pos_ref):
    ix, iz = pos_ref[0], pos_ref[1]
    has = (ix > 0, ix < NX - 1, iz > 0, iz < NZ - 1)
    frac = tuple(jnp.where(h, jnp.float32(0.5), jnp.float32(1.0)) for h in has)
    even = (lax.rem(ix, 2) == 0, lax.rem(iz, 2) == 0)
    return ix, iz, has, frac, even


def own_mult():
    k = lax.broadcasted_iota(jnp.int32, (8, NY), 0)
    y = lax.broadcasted_iota(jnp.int32, (8, NY), 1)
    shared = ((k == 0) & (y > 0)) | ((k == E) & (y < NY - 1))
    return jnp.where(shared, jnp.float32(0.5), jnp.float32(1.0))


def field_sum(get, frac):
    total = None
    for i in range(8):
        mid = get(i, 1)
        for j in range(2, 7):
            mid = mid + get(i, j)
        row = mid + frac[2] * get(i, 0) + frac[3] * get(i, E)
        if i == 0:
            row = frac[0] * row
        elif i == E:
            row = frac[1] * row
        total = row if total is None else total + row
    return total


def assemble_aisle(ref):
    low, high = ref[:, :, 0, :], ref[:, :, E, :]
    y = lax.broadcasted_iota(jnp.int32, FACE, 2)
    ref[:, :, 0, :] = low + jnp.where(y > 0, pltpu.roll(high, 1, 2), 0.0)
    ref[:, :, E, :] = high + jnp.where(y < NY - 1, pltpu.roll(low, NY - 1, 2), 0.0)


def add_faces_x(ref, got, has, even):
    a, b = got[0][...], got[1][...]
    ref[0] = ref[0] + jnp.where(has[0], jnp.where(even[0], b, a), 0.0)
    ref[E] = ref[E] + jnp.where(has[1], jnp.where(even[0], a, b), 0.0)


def add_faces_z(ref, got, has, even):
    a, b = got[0][...], got[1][...]
    ref[:, 0] = ref[:, 0] + jnp.where(has[2], jnp.where(even[1], b, a), 0.0)
    ref[:, E] = ref[:, E] + jnp.where(has[3], jnp.where(even[1], a, b), 0.0)


def put_pair(even, low, high, out):
    out[0][...] = jnp.where(even, high, low)
    out[1][...] = jnp.where(even, low, high)


def aisle_stiffness(block):
    turned = jnp.swapaxes(block, 0, 1)
    out = apply1d([turned[c] for c in range(8)], K_)
    return jnp.swapaxes(jnp.stack(out, axis=0), 0, 1)


def apply_ends(v, mat):
    s = d = None
    for a in range(4):
        p = float(0.5 * (mat[0, a] + mat[0, 7 - a])) * (v[a] + v[7 - a])
        m = float(0.5 * (mat[0, a] - mat[0, 7 - a])) * (v[a] - v[7 - a])
        s, d = (p, m) if s is None else (s + p, d + m)
    return s + d, s - d


def local_operator(z_ref, nb_ref, f_ref):
    wk = kvec(W)
    kt, ct = nb_ref[4], nb_ref[13]
    kw, cw = kt * wk, ct * wk
    for j in range(8):
        out = apply1d([z_ref[i, j] for i in range(8)], K_)
        kwj = kw * W[j]
        res = [kwj * out[i] for i in range(8)]
        for i in range(8):
            f_ref[i, j] = res[i]
    for i in range(8):
        block = z_ref[i]
        fx = [f_ref[i, j] for j in range(8)]
        zs = apply1d([block[j] for j in range(8)], K_)
        ys = aisle_stiffness(block)
        kwi = kw * W[i]
        res = [
            fx[j] + kwi * zs[j] + (W[i] * W[j]) * (kt * ys[j] + cw * block[j]) for j in range(8)
        ]
        for j in range(8):
            f_ref[i, j] = res[j]


def face_messages(z_ref, nb_ref, even, msgs):
    wk = kvec(W)
    kt, ct = nb_ref[4], nb_ref[13]
    kw, cw = kt * wk, ct * wk
    w0 = W[0]
    w00 = w0 * w0
    ends = [apply_ends([z_ref[i, j] for i in range(8)], K_) for j in range(8)]
    for n, i in enumerate((0, E)):
        block = z_ref[i]
        zs, ys = apply1d([block[j] for j in range(8)], K_), aisle_stiffness(block)
        res = [
            kw * (W[j] * ends[j][n] + w0 * zs[j]) + (w0 * W[j]) * (kt * ys[j] + cw * block[j])
            for j in range(8)
        ]
        for j, m in ((0, 3), (E, 5)):
            res[j] = (
                res[j]
                + nb_ref[m] * (w0 * wk * ends[j][n] + w00 * ys[j])
                + nb_ref[9 + m] * (w00 * wk * block[j])
            )
        up, down = (1, 0) if i == 0 else (0, 1)

        @pl.when(even[0])
        def _(res=res, to=up):
            for j in range(8):
                msgs[to][j] = res[j]

        @pl.when(jnp.logical_not(even[0]))
        def _(res=res, to=down):
            for j in range(8):
                msgs[to][j] = res[j]

    ends = [apply_ends([z_ref[i, j] for j in range(8)], K_) for i in range(8)]
    for n, j in enumerate((0, E)):
        block = z_ref[:, j]
        xs, ys = apply1d([block[i] for i in range(8)], K_), aisle_stiffness(block)
        res = [
            kw * (w0 * xs[i] + W[i] * ends[i][n]) + (W[i] * w0) * (kt * ys[i] + cw * block[i])
            for i in range(8)
        ]
        for i, m in ((0, 1), (E, 7)):
            res[i] = res[i] + nb_ref[m] * (w0 * wk * ends[i][n])
        up, down = (3, 2) if j == 0 else (2, 3)

        @pl.when(even[1])
        def _(res=res, to=up):
            for i in range(8):
                msgs[to][i] = res[i]

        @pl.when(jnp.logical_not(even[1]))
        def _(res=res, to=down):
            for i in range(8):
                msgs[to][i] = res[i]


def thomas(cf_ref, rhs):
    dp = []
    for h in range(NZ):
        v = rhs[h] if h == 0 else rhs[h] - cf_ref[h] * dp[h - 1]
        dp.append(v * cf_ref[32 + h])
    for h in range(NZ - 2, -1, -1):
        dp[h] = dp[h] - cf_ref[16 + h] * dp[h + 1]
    return dp


def coarse_dot(a, b):
    acc = None
    for u, v in zip(a, b):
        acc = u * v if acc is None else acc + u * v
    return spread_sum(acc)


def spread_sum(tile):
    row = jnp.broadcast_to(jnp.sum(tile, axis=0, keepdims=True), (8, NY))
    return jnp.broadcast_to(jnp.sum(row, axis=1, keepdims=True), (8, NY))


def shift_pair(v, axis):
    n = v.shape[axis]
    p = lax.broadcasted_iota(jnp.int32, v.shape, axis)
    before = jnp.where(p == 0, v, pltpu.roll(v, 1, axis))
    after = jnp.where(p == n - 1, v, pltpu.roll(v, n - 1, axis))
    return before, after


MID, FACE_MU = 2.0 - 2.0 * W[0], 2.0 * W[0]
SYM_F = (MID / (2.0 * FACE_MU)) ** 0.5
SYM_M = -((FACE_MU / (2.0 * MID)) ** 0.5)
A0, B0 = (MID + FACE_MU / 2.0) / 2.0**0.5, FACE_MU / (4.0 * 2.0**0.5)
A1, B1 = -SYM_F * FACE_MU / 2.0, SYM_F * FACE_MU / 4.0
C2 = FACE_MU**0.5 / 4.0
LAM = (
    0.0,
    float(2.0 * (K_[0, 0] + K_[0, 7])) * (SYM_F - SYM_M) ** 2,
    float(2.0 * (K_[0, 0] - K_[0, 7])) / FACE_MU,
)


def spread3(v, before, after):
    both = before + after
    return (A0 * v + B0 * both, A1 * v + B1 * both, C2 * (before - after))


def back3(duals):
    t, u = B0 * duals[0] + B1 * duals[1], C2 * duals[2]
    return A0 * duals[0] + A1 * duals[1], t + u, t - u


def gather3(duals, axis):
    own, g, h = back3(duals)
    n = own.shape[axis]
    p = lax.broadcasted_iota(jnp.int32, own.shape, axis)
    up = jnp.where(p == n - 1, h, pltpu.roll(g, n - 1, axis))
    down = jnp.where(p == 0, g, pltpu.roll(h, 1, axis))
    return own + (up + down)


def coarse_operator(d, kc_ref, cc_ref, tmp_ref):
    for h in range(NZ):
        ys = spread3(d[h], *shift_pair(d[h], 1))
        for c in range(3):
            xs = spread3(ys[c], *shift_pair(ys[c], 0))
            for a in range(3):
                tmp_ref[(a * 3 + c) * NZ + h] = xs[a]
    keys = [(a, c) for a in range(3) for c in range(3)]
    res, kept, after = [], {}, {}

    def finish(vals):
        return gather3([gather3([vals[a, c] for a in range(3)], 0) for c in range(3)], 1)

    for h in range(NZ):
        lo, hi = max(h - 1, 0), min(h + 1, NZ - 1)
        kh, ch = kc_ref[h], cc_ref[h]
        factor, final = {}, {}
        for a, c in keys:
            base = (a * 3 + c) * NZ
            zs = spread3(tmp_ref[base + h], tmp_ref[base + lo], tmp_ref[base + hi])
            duals = []
            for b in range(3):
                kind = tuple(sorted((a, b, c)))
                if kind not in factor:
                    lam = sum(LAM[n] for n in kind)
                    factor[kind] = kh * lam + ch if lam else ch
                duals.append(factor[kind] * zs[b])
            own, g, hh = back3(duals)
            if h > 0:
                final[a, c] = kept[a, c] + g
                own = own + after[a, c]
            else:
                own = own + g
            if h == NZ - 1:
                own = own + hh
            kept[a, c], after[a, c] = own, hh
        if h > 0:
            res.append(finish(final))
    res.append(finish(kept))
    return res


def coarse_row(ref, ix, iz, dx, dz):
    x = jnp.clip(ix + dx, 0, NX - 1)
    z = jnp.clip(iz + dz, 0, NZ - 1)
    return ref[z, pl.ds(x, 1), :]


def aisle_tiles(row, want_stiff):
    c = jnp.broadcast_to(row, (8, NY))
    before, after = shift_pair(c, 1)
    k = lax.broadcasted_iota(jnp.int32, (8, NY), 0)
    low, high = 0.5 * (c + before), 0.5 * (c + after)
    tile = jnp.where(k == 0, low, jnp.where(k == E, high, c))
    if not want_stiff:
        return tile, None
    return tile, kvec(K_[:, 0]) * (low - c) + kvec(K_[:, 7]) * (high - c)


def classes(tiles, reach):
    n = 2 * reach + 1
    m = 2 * n - 3

    def line(vals):
        out = []
        for p in range(m):
            if p % 2 == 0:
                out.append(0.5 * (vals[p // 2] + vals[p // 2 + 1]))
            else:
                out.append(vals[p // 2 + 1])
        return out

    cols = [line(tiles[dx]) for dx in range(n)]
    by_q = [line([cols[dx][q] for dx in range(n)]) for q in range(m)]
    return [[by_q[q][p] for q in range(m)] for p in range(m)]


def cls(i):
    return 0 if i == 0 else (2 if i == E else 1)


def own_prolong(ref, ix, iz):
    tiles = [
        [aisle_tiles(coarse_row(ref, ix, iz, dx, dz), False)[0] for dz in (-1, 0, 1)]
        for dx in (-1, 0, 1)
    ]
    return classes(tiles, 1)


def add_operator_of_prolong(ref, ix, iz, nb_ref, out_ref):
    tv, ty = [], []
    for dx in range(-2, 3):
        pair = [aisle_tiles(coarse_row(ref, ix, iz, dx, dz), True) for dz in range(-2, 3)]
        tv.append([p[0] for p in pair])
        ty.append([p[1] for p in pair])
    v, yv = classes(tv, 2), classes(ty, 2)
    wk = kvec(W)

    def parts(ex, ez):
        p, q = 2 + 2 * ex, 2 + 2 * ez
        n = (ex + 1) * 3 + ez + 1
        kt, ct = nb_ref[n], nb_ref[9 + n]
        kw, cw = kt * wk, ct * wk
        memo = {}

        def once(key, make):
            if key not in memo:
                memo[key] = make()
            return memo[key]

        def along(i, a, b, c):
            return kw * (float(K_[i, 0]) * (a - b) + float(K_[i, 7]) * (c - b))

        def tile(i, j):
            a, b = cls(i), cls(j)
            xt = once(
                ("x", i, b), lambda: along(i, v[p][q + b], v[p + 1][q + b], v[p + 2][q + b])
            )
            zt = once(
                ("z", a, j), lambda: along(j, v[p + a][q], v[p + a][q + 1], v[p + a][q + 2])
            )
            yt = once(("y", a, b), lambda: kt * yv[p + a][q + b] + cw * v[p + a][q + b])
            return W[j] * xt + W[i] * zt + (W[i] * W[j]) * yt

        return tile

    part = {(ex, ez): parts(ex, ez) for ex in (-1, 0, 1) for ez in (-1, 0, 1)}
    for i in range(8):
        new = []
        for j in range(8):
            acc = out_ref[i, j] + part[0, 0](i, j)
            ex = -1 if i == 0 else (1 if i == E else 0)
            ez = -1 if j == 0 else (1 if j == E else 0)
            if ex:
                acc = acc + part[ex, 0](7 - i, j)
            if ez:
                acc = acc + part[0, ez](i, 7 - j)
            if ex and ez:
                acc = acc + part[ex, ez](7 - i, 7 - j)
            new.append(acc)
        for j in range(8):
            out_ref[i, j] = new[j]
    return [[v[2 + a][2 + b] for b in range(3)] for a in range(3)]


def make_z(c_ref, ix, iz, r_ref, dinv_ref, z_ref):
    pc = own_prolong(c_ref, ix, iz)
    for i in range(8):
        new = [r_ref[i, j] * dinv_ref[i, j] + pc[cls(i)][cls(j)] for j in range(8)]
        for j in range(8):
            z_ref[i, j] = new[j]


def coarse_rows_of(got_ref, which):
    return [got_ref[pl.ds(4 * h + which, NX, stride=4 * NZ), :] for h in range(NZ)]


def heat_kernel(pos, heat, f, ma, mb):
    _, _, _, _, even = place(pos)
    wk = kvec(W)
    for i in range(8):
        new = [(W[i] * W[j]) * wk * heat[i, j] for j in range(8)]
        for j in range(8):
            f[i, j] = new[j]
    put_pair(even[0], f[0], f[E], (ma, mb))


def heat_z_kernel(pos, f, rb, ra, out, ma, mb):
    _, _, has, _, even = place(pos)
    out[...] = f[...]
    add_faces_x(out, (ra, rb), has, even)
    put_pair(even[1], out[:, 0], out[:, E], (ma, mb))


def first_rows_kernel(pos, f, rb, ra, both, out, rows):
    _, _, has, frac, even = place(pos)
    out[...] = f[...]
    add_faces_z(out, (ra, rb), has, even)
    assemble_aisle(out)
    tile = field_sum(lambda i, j: out[i, j], frac) * own_mult()
    restricted = jnp.sum(tile, axis=0, keepdims=True)
    cap = jnp.where(both[1:2] == 1.0, jnp.float32(HEAT_SOLID), jnp.float32(HEAT_AIR))
    block = jnp.concatenate([both[0:1], cap, restricted, jnp.zeros((1, NY), F32)], axis=0)
    rows[...] = jnp.broadcast_to(block[None], rows.shape)


def setup_kernel(
    pos, got, r, kc, cc, cf, rc, nb, dinv, z, m0, m1, m2, m3, c_tmp
):
    ix, iz, has, frac, even = place(pos)
    k_all, c_all, r_all = (coarse_rows_of(got, n) for n in range(3))
    for h in range(NZ):
        kc[h], cc[h], rc[h] = k_all[h], c_all[h], r_all[h]
    link = [2.0 * k_all[h] * k_all[h + 1] / (k_all[h] + k_all[h + 1]) for h in range(NZ - 1)]
    above = None
    for h in range(NZ):
        main = 8.0 * c_all[h]
        if h > 0:
            main = main + link[h - 1]
        if h < NZ - 1:
            main = main + link[h]
        low = -link[h - 1] if h > 0 else jnp.zeros((NX, NY), F32)
        piv = main if h == 0 else main - low * above
        inv = 1.0 / piv
        above = -link[h] * inv if h < NZ - 1 else jnp.zeros((NX, NY), F32)
        cf[h], cf[16 + h], cf[32 + h] = low, above, inv
    for ex in (-1, 0, 1):
        for ez in (-1, 0, 1):
            n = (ex + 1) * 3 + ez + 1
            there = None
            if ex:
                there = has[0] if ex < 0 else has[1]
            if ez:
                hz = has[2] if ez < 0 else has[3]
                there = hz if there is None else there & hz
            for base, src in ((0, kc), (9, cc)):
                tile = jnp.broadcast_to(coarse_row(src, ix, iz, ex, ez), (8, NY))
                nb[base + n] = tile if there is None else jnp.where(there, tile, 0.0)
    wk, sk = kvec(W), kvec(SD)
    for i in range(8):
        for j in range(8):
            ex = -1 if i == 0 else (1 if i == E else 0)
            ez = -1 if j == 0 else (1 if j == E else 0)
            kt, ct = nb[4], nb[13]
            for n in {4 + 3 * ex, 4 + ez, 4 + 3 * ex + ez} - {4}:
                kt, ct = kt + nb[n], ct + nb[9 + n]
            dinv[i, j] = (
                kt * ((SD[i] * W[j] + W[i] * SD[j]) * wk + (W[i] * W[j]) * sk)
                + ct * ((W[i] * W[j]) * wk)
            )
    assemble_aisle(dinv)
    dinv[...] = 1.0 / dinv[...]
    solved = thomas(cf, r_all)
    for h in range(NZ):
        c_tmp[h] = solved[h]
    make_z(c_tmp, ix, iz, r, dinv, z)
    face_messages(z, nb, even, (m0, m1, m2, m3))


def inner_kernel(pos, f, r3, r1, r2, r0, nb, dinv, *refs):
    w1, t, m0, m1, m2, m3 = refs[-6:]
    _, _, has, _, even = place(pos)
    w1[...] = f[...]
    add_faces_x(w1, (r0, r1), has, even)
    add_faces_z(w1, (r2, r3), has, even)
    assemble_aisle(w1)
    t[...] = w1[...] * dinv[...]
    face_messages(t, nb, even, (m0, m1, m2, m3))


def dots_kernel(first, *refs):
    if first:
        pos, z, r, t, w1, lines = refs
    else:
        pos, z, r, t, w1, s1, s2, lines = refs
    _, _, _, frac, _ = place(pos)
    my = own_mult()
    zero = jnp.zeros((1, NY), F32)

    def dot(a, b):
        tile = my * field_sum(lambda i, j: a[i, j] * b[i, j], frac)
        return jnp.sum(tile, axis=0, keepdims=True)

    out = [dot(z, r), dot(t, r), dot(z, w1), dot(t, w1), zero]
    out += [zero] * 4 if first else [dot(z, s1), dot(z, s2), dot(t, s1), dot(t, s2)]
    out += [zero] * 6
    out.append(jnp.sum(field_sum(lambda i, j: w1[i, j], frac) * my, axis=0, keepdims=True))
    lines[...] = jnp.concatenate(out, axis=0)


def rows_kernel(first, *refs):
    if first:
        pos, f2, r3, r1, r2, r0, t, lines, owners, v, rows = refs
    else:
        pos, f2, r3, r1, r2, r0, t, lines, v, rows = refs
    _, _, has, frac, even = place(pos)
    v[...] = f2[...]
    add_faces_x(v, (r0, r1), has, even)
    add_faces_z(v, (r2, r3), has, even)
    my = own_mult()
    tv = jnp.sum(field_sum(lambda i, j: t[i, j] * v[i, j], frac), axis=0, keepdims=True)
    lane = lax.broadcasted_iota(jnp.int32, (16, NY), 1)
    at = lax.broadcasted_iota(jnp.int32, (16, NY), 0)
    stacked = jnp.where(at == 4, jnp.broadcast_to(tv, (16, NY)), lines[...])
    totals = jnp.broadcast_to(jnp.sum(stacked, axis=1, keepdims=True), (16, NY))
    dots = jnp.sum(jnp.where(lane == at, totals, 0.0), axis=0, keepdims=True)
    vt = field_sum(lambda i, j: v[i, j], frac)
    k = lax.broadcasted_iota(jnp.int32, (8, NY), 0)
    y = lax.broadcasted_iota(jnp.int32, (8, NY), 1)
    vlow = jnp.broadcast_to(vt[0:1], (8, NY))
    vhigh = jnp.broadcast_to(vt[7:8], (8, NY))
    vt = vt + jnp.where((k == 0) & (y > 0), pltpu.roll(vhigh, 1, 1), 0.0)
    vt = vt + jnp.where((k == E) & (y < NY - 1), pltpu.roll(vlow, NY - 1, 1), 0.0)
    g2 = jnp.sum(vt * my, axis=0, keepdims=True)
    block = jnp.concatenate([lines[15:16], g2, dots, jnp.zeros((1, NY), F32)], axis=0)
    rows[...] = jnp.broadcast_to(block[None], rows.shape)
    if first:
        rows[:, 3, :] = owners[...]


def coefficients(first, got, d, q, rc, rs, wp, cf):
    total = got[0:8]
    for n in range(8, NX * NZ * 4, 8):
        total = total + got[n : n + 8]
    dots = jnp.broadcast_to(total[2:3] + total[6:7], (8, NY))
    lane = lax.broadcasted_iota(jnp.int32, (8, NY), 1)

    def pick(n):
        return jnp.broadcast_to(
            jnp.sum(jnp.where(lane == n, dots, 0.0), axis=1, keepdims=True), (8, NY)
        )

    g1, g2 = coarse_rows_of(got, 0), coarse_rows_of(got, 1)
    b1, b2 = pick(0), pick(1) + coarse_dot(d, [rc[h] for h in range(NZ)])
    w11 = pick(2)
    w12 = pick(3) + coarse_dot(d, g1)
    w22 = pick(4) + 2.0 * coarse_dot(d, g2) + coarse_dot(d, q)
    e = [None] * 4
    if not first:
        rs1, rs2 = [rs[h] for h in range(NZ)], [rs[NZ + h] for h in range(NZ)]
        c11, c21 = pick(5), pick(6)
        c12, c22 = pick(7) + coarse_dot(d, rs1), pick(8) + coarse_dot(d, rs2)
        pa, pb, pc = wp[6], wp[7], wp[8]
        inv = -1.0 / (pa * pc - pb * pb)
        e11, e21 = (pc * c11 - pb * c21) * inv, (pa * c21 - pb * c11) * inv
        e12, e22 = (pc * c12 - pb * c22) * inv, (pa * c22 - pb * c12) * inv
        w11 = w11 + c11 * e11 + c21 * e21
        w12 = w12 + c11 * e12 + c21 * e22
        w22 = w22 + c12 * e12 + c22 * e22
        e = [e11, e21, e12, e22]
    inv = 1.0 / (w11 * w22 - w12 * w12)
    a1 = (w22 * b1 - w12 * b2) * inv
    a2 = (w11 * b2 - w12 * b1) * inv
    return a1, a2, e, (w11, w12, w22), g1, g2


def new_residual(first, a1, a2, x1, x2, r, w1, ay, s1, s2, out):
    for i in range(8):
        new = []
        for j in range(8):
            v = r[i, j] - (a1 * w1[i, j] + a2 * ay[i, j])
            if not first:
                v = v - (x1 * s1[i, j] + x2 * s2[i, j])
            new.append(v)
        for j in range(8):
            out[i, j] = new[j]


def step_kernel(first, *refs):
    refs = list(refs)
    take = lambda n: [refs.pop(0) for _ in range(n)]
    pos, got, r, w1, v, dinv, nb, kc, cc, cf, rc = take(11)
    s1 = s2 = rs = wp = None
    if not first:
        s1, s2, rs, wp = take(4)
    ro, rco, zo, m0, m1, m2, m3, co, ay, pdo, qo = take(11)
    c_tmp, tmp = take(2)
    ix, iz, has, frac, even = place(pos)
    d = thomas(cf, coarse_rows_of(got, 0))
    for h in range(NZ):
        c_tmp[h] = d[h]
    q = coarse_operator(d, kc, cc, tmp)
    a1, a2, e, w, g1, g2 = coefficients(first, got, d, q, rc, rs, wp, cf)
    x1 = x2 = None
    if not first:
        x1, x2 = a1 * e[0] + a2 * e[2], a1 * e[1] + a2 * e[3]
    for n, val in enumerate((a1, a2, *e, *w)):
        if val is not None:
            co[n] = val
        else:
            co[n] = jnp.zeros((8, NY), F32)
    ay[...] = v[...]
    pd = add_operator_of_prolong(c_tmp, ix, iz, nb, ay)
    for n in range(9):
        pdo[n] = pd[n // 3][n % 3]
    assemble_aisle(ay)
    new_residual(first, a1, a2, x1, x2, r, w1, ay, s1, s2, ro)
    rnew = []
    for h in range(NZ):
        qo[h] = q[h]
        new = rc[h] - (a1 * g1[h] + a2 * (g2[h] + q[h]))
        if not first:
            new = new - (x1 * rs[h] + x2 * rs[NZ + h])
        rco[h] = new
        rnew.append(new)
    solved = thomas(cf, rnew)
    for h in range(NZ):
        c_tmp[h] = solved[h]
    make_z(c_tmp, ix, iz, ro, dinv, zo)
    face_messages(zo, nb, even, (m0, m1, m2, m3))


def new_x(first, a1, a2, x1, x2, z, t, pd, p1, p2, x, out):
    for i in range(8):
        new = []
        for j in range(8):
            up = a1 * z[i, j] + a2 * (t[i, j] + pd(i, j))
            if not first:
                up = x[i, j] + (up + (x1 * p1[i, j] + x2 * p2[i, j]))
            new.append(up)
        for j in range(8):
            out[i, j] = new[j]


def late_kernel(first, *refs):
    refs = list(refs)
    take = lambda n: [refs.pop(0) for _ in range(n)]
    got, z, t, w1, ay, co, pdt, q = take(8)
    x = p1 = p2 = s1 = s2 = rs = None
    if not first:
        x, p1, p2, s1, s2, rs = take(6)
    xo, p1o, p2o, s1o, s2o, rso = take(6)
    a1, a2, e11, e21, e12, e22 = (co[n] for n in range(6))
    x1, x2 = a1 * e11 + a2 * e12, a1 * e21 + a2 * e22
    pd = lambda i, j: pdt[3 * cls(i) + cls(j)]
    new_x(first, a1, a2, x1, x2, z, t, pd, p1, p2, x, xo)

    def block(one, two, prev1, prev2, out1, out2):
        for i in range(8):
            new = []
            for j in range(8):
                n1, n2 = one(i, j), two(i, j)
                if not first:
                    u, w = prev1[i, j], prev2[i, j]
                    n1, n2 = n1 + e11 * u + e21 * w, n2 + e12 * u + e22 * w
                new.append((n1, n2))
            for j in range(8):
                out1[i, j], out2[i, j] = new[j]

    block(lambda i, j: z[i, j], lambda i, j: t[i, j] + pd(i, j), p1, p2, p1o, p2o)
    block(lambda i, j: w1[i, j], lambda i, j: ay[i, j], s1, s2, s1o, s2o)
    g1, g2 = coarse_rows_of(got, 0), coarse_rows_of(got, 1)
    for h in range(NZ):
        n1, n2 = g1[h], g2[h] + q[h]
        if not first:
            u, w = rs[h], rs[NZ + h]
            n1, n2 = n1 + e11 * u + e21 * w, n2 + e12 * u + e22 * w
        rso[h], rso[NZ + h] = n1, n2


def last_kernel(pos, got, z, t, nb, kc, cc, cf, rc, x, p1, p2, rs, wp, table, xo, send, co, dc, tmp):
    ix, iz, _, _, _ = place(pos)
    d = thomas(cf, coarse_rows_of(got, 0))
    for h in range(NZ):
        dc[h] = d[h]
    q = coarse_operator(d, kc, cc, tmp)
    a1, a2, e, _, _, _ = coefficients(False, got, d, q, rc, rs, wp, cf)
    x1, x2 = a1 * e[0] + a2 * e[2], a1 * e[1] + a2 * e[3]
    for n, val in enumerate((a1, a2, x1, x2)):
        co[n] = val
    own = own_prolong(dc, ix, iz)
    pd = lambda i, j: own[cls(i)][cls(j)]
    new_x(False, a1, a2, x1, x2, z, t, pd, p1, p2, x, xo)
    put_rows(xo, nb, table, send)


def residual_kernel(pos, co, dc, v, r, w1, s1, s2, nb, ro, ay):
    ix, iz, _, _, _ = place(pos)
    ay[...] = v[...]
    add_operator_of_prolong(dc, ix, iz, nb, ay)
    assemble_aisle(ay)
    new_residual(False, co[0], co[1], co[2], co[3], r, w1, ay, s1, s2, ro)


NT = (((1,), (1,)), ((), ()))
SLOTS = 16


def slots_kernel(ints, table, owners):
    own, elem, side, target = (ints[n : n + 1] for n in range(4))
    faces = own.shape[1]
    row = own.astype(F32)
    col = jnp.broadcast_to(row, (NY, faces)).T
    ranks = []
    for s in range(0, faces, NY):
        f = lax.broadcasted_iota(jnp.int32, (faces, NY), 0)
        g = lax.broadcasted_iota(jnp.int32, (faces, NY), 1) + s
        same = (col == row[:, s : s + NY]) & (f < g)
        ranks.append(jnp.sum(jnp.where(same, 1.0, 0.0), axis=0, keepdims=True))
    rank = jnp.concatenate(ranks, axis=1)
    slot = row * SLOTS + rank
    vals = jnp.concatenate(
        [elem.astype(F32) + 1.0, side.astype(F32), jnp.zeros((6, faces), F32)], axis=0
    ).astype(jnp.bfloat16)
    step = 256
    for s in range(0, table.shape[0], step):
        at = lax.broadcasted_iota(jnp.int32, (step, faces), 0).astype(F32) + float(s)
        hot = jnp.where(at == slot, 1.0, 0.0).astype(jnp.bfloat16)
        got = lax.dot_general(hot, vals, NT, preferred_element_type=F32)
        pick = got[:, 0:1] - 1.0 + 128.0 * got[:, 1:2]
        lane = lax.broadcasted_iota(jnp.int32, (step, table.shape[1]), 1).astype(F32)
        table[s : s + step] = jnp.where(lane == pick, 1.0, 0.0).astype(jnp.bfloat16)
    devices = owners.shape[0]
    dev = lax.broadcasted_iota(jnp.int32, (devices, faces), 0).astype(F32)
    hot = jnp.where(dev == row, 1.0, 0.0).astype(jnp.bfloat16)
    at = lax.broadcasted_iota(jnp.int32, (128, faces), 0).astype(F32)
    marked = jnp.where(at == rank, target.astype(F32) + 1.0, 0.0).astype(jnp.bfloat16)
    owners[...] = lax.dot_general(hot, marked, NT, preferred_element_type=F32) - 1.0


def owners_kernel(got, hot_t):
    devices = got.shape[0] // 4
    lane = lax.broadcasted_iota(jnp.int32, (SLOTS, NY), 1)
    at = lax.broadcasted_iota(jnp.int32, (SLOTS, NY), 0)
    ones = jnp.ones((NY, NY), jnp.bfloat16)
    step = 8
    for d in range(0, devices, step):
        rows = [
            jnp.where(lane == at, jnp.broadcast_to(got[4 * (d + n) + 3 : 4 * (d + n) + 4], (SLOTS, NY)), 0.0)
            for n in range(step)
        ]
        block = jnp.concatenate(rows, axis=0).astype(jnp.bfloat16)
        col = jnp.dot(block, ones, preferred_element_type=F32)
        elem = lax.broadcasted_iota(jnp.int32, col.shape, 1).astype(F32)
        hot = jnp.where(col == elem, 1.0, 0.0)
        hot_t[:, d * SLOTS : (d + step) * SLOTS] = hot.T.astype(jnp.bfloat16)


def split(v):
    high = v.astype(jnp.bfloat16)
    return high, (v - high.astype(F32)).astype(jnp.bfloat16)


def put_rows(x, nb, table, send):
    kt = nb[4]

    def weighted(get, row):
        acc = None
        for a in range(8):
            term = float(D_[row, a]) * get(a)
            acc = term if acc is None else acc + term
        return acc

    getters = (lambda a: x[a], lambda a: x[:, a], lambda a: x[:, :, a, :])
    his, los = [], []
    for get in getters:
        for end, sign in ((0, 1.0), (E, -1.0)):
            flux = weighted(get, end) * (sign * kt)[None]
            block = jnp.concatenate(
                [flux.reshape(64, NY), get(end).reshape(64, NY)], axis=0
            )
            h, l = split(block)
            his.append(h)
            los.append(l)
    both = jnp.concatenate(
        [jnp.concatenate(his, axis=1), jnp.concatenate(los, axis=1)], axis=0
    )
    step = 512
    for s in range(0, send.shape[0], step):
        out = lax.dot_general(table[s : s + step], both, NT, preferred_element_type=F32)
        send[s : s + step] = out[:, :NY] + out[:, NY:]


def load_kernel(got, hot_t, out):
    acc = None
    step = 512
    for s in range(0, got.shape[0], step):
        both = jnp.concatenate(split(got[s : s + step]), axis=1)
        term = jnp.dot(hot_t[:, s : s + step], both, preferred_element_type=F32)
        acc = term if acc is None else acc + term
    out[...] = (acc[:, :NY] + acc[:, NY:]).T


def call(body, name, outs, args, scratch=()):
    vmem = pl.BlockSpec(memory_space=pltpu.VMEM)
    smem = pl.BlockSpec(memory_space=pltpu.SMEM)
    shape = lambda o: o if isinstance(o[0], tuple) else (o, F32)
    scalars = lambda a: a.dtype == jnp.int32 and a.shape == (2,)
    return pl.pallas_call(
        body,
        out_shape=[jax.ShapeDtypeStruct(*shape(o)) for o in outs],
        in_specs=[smem if scalars(a) else vmem for a in args],
        out_specs=[vmem] * len(outs),
        scratch_shapes=[pltpu.VMEM(s, F32) for s in scratch],
        compiler_params=pltpu.CompilerParams(vmem_limit_bytes=24 * 1024 * 1024),
        cost_estimate=pl.CostEstimate(
            flops=2_000_000, bytes_accessed=1 << 20, transcendentals=0
        ),
        name=name,
    )(*args)


def pairs(axis, second):
    out = []
    for x in range(NX):
        for z in range(NZ):
            here = [x, z]
            n, last = here[axis], (NX, NZ)[axis] - 1
            if not second:
                here[axis] = n ^ 1
            elif n in (0, last):
                here[1 - axis] ^= 1
            else:
                here[axis] = n + 1 if n % 2 else n - 1
            out.append((x * NZ + z, here[0] * NZ + here[1]))
    return out


def swap(pair, axis):
    return [lax.ppermute(v, ("row", "height"), pairs(axis, n == 1)) for n, v in enumerate(pair)]


def swap_x(pair):
    return swap(pair, 0)


def swap_z(pair):
    return swap(pair, 1)


def halo(msgs):
    got = swap_x(msgs[:2]) + swap_z(msgs[2:])
    return [got[n] for n in (3, 1, 2, 0)]


def everywhere(rows):
    return lax.all_to_all(rows, ("row", "height"), split_axis=0, concat_axis=0, tiled=True)


def shards(heat, conductivity, marks, face_owner, face_element, face_side, owner_element):
    devices = NX * NZ
    pos = jnp.stack([lax.axis_index("row"), lax.axis_index("height")]).astype(jnp.int32)
    f, ma, mb = call(heat_kernel, "heat", [FIELD, FACE, FACE], [pos, heat.reshape(FIELD)])
    ra, rb = swap_x((ma, mb))
    both = jnp.stack([conductivity.reshape(-1), marks.reshape(-1).astype(F32)])
    ints = jnp.stack([face_owner.reshape(-1), face_element, face_side, owner_element])
    table, owners = call(
        slots_kernel,
        "slots",
        [((devices * SLOTS, 6 * NY), jnp.bfloat16), (devices, 128)],
        [ints],
    )
    f, ma, mb = call(heat_z_kernel, "heat_z", [FIELD, FACE, FACE], [pos, f, rb, ra])
    ra, rb = swap_z((ma, mb))
    r, rows = call(
        first_rows_kernel,
        "first_rows",
        [FIELD, (devices, 4, NY)],
        [pos, f, rb, ra, both],
    )
    got0 = everywhere(rows).reshape(devices * 4, NY)
    kc, cc, cf, rc, nb, dinv, z, *msgs = call(
        setup_kernel,
        "setup",
        [COARSE, COARSE, (48, NX, NY), COARSE, (18, 8, NY), FIELD, FIELD] + [FACE] * 4,
        [pos, got0, r],
        scratch=[COARSE],
    )
    x = p1 = p2 = s1 = s2 = rs = co = None
    for outer in range(ITERS // 2):
        first, last = outer == 0, outer == ITERS // 2 - 1
        got = halo(msgs)
        (f,) = call(local_operator, "apply", [FIELD], [z, nb])
        w1, t, *msgs = call(
            inner_kernel,
            "inner",
            [FIELD] * 2 + [FACE] * 4,
            [pos, f, *got, nb, dinv] + ([] if first else [rs]),
        )
        got = halo(msgs)
        (f2,) = call(local_operator, "apply", [FIELD], [t, nb])
        (lines,) = call(
            functools.partial(dots_kernel, first),
            "dots",
            [(16, NY)],
            [pos, z, r, t, w1] + ([] if first else [s1, s2]),
        )
        v, rows = call(
            functools.partial(rows_kernel, first),
            "rows",
            [FIELD, (devices, 4, NY)],
            [pos, f2, *got, t, lines] + ([owners] if first else []),
        )
        rows = everywhere(rows).reshape(devices * 4, NY)
        if first:
            (hot_t,) = call(
                owners_kernel, "owners", [((NY, devices * SLOTS), jnp.bfloat16)], [rows]
            )
        if last:
            break
        rn, rcn, zn, *msgs, con, ay, pd, q = call(
            functools.partial(step_kernel, first),
            "step",
            [FIELD, COARSE, FIELD]
            + [FACE] * 4
            + [(9, 8, NY), FIELD, (9, 8, NY), COARSE],
            [pos, rows, r, w1, v, dinv, nb, kc, cc, cf, rc] + ([] if first else [s1, s2, rs, co]),
            scratch=[COARSE, (9 * NZ, NX, NY)],
        )
        x, p1, p2, s1, s2, rs = call(
            functools.partial(late_kernel, first),
            "late",
            [FIELD] * 5 + [(2 * NZ, NX, NY)],
            [rows, z, t, w1, ay, con, pd, q] + ([] if first else [x, p1, p2, s1, s2, rs]),
        )
        r, rc, z, co = rn, rcn, zn, con
    x, send, coef, d = call(
        last_kernel,
        "last",
        [FIELD, (devices * SLOTS, NY), (4, 8, NY), COARSE],
        [pos, rows, z, t, nb, kc, cc, cf, rc, x, p1, p2, rs, co, table],
        scratch=[(9 * NZ, NX, NY)],
    )
    got = everywhere(send.reshape(devices, SLOTS, NY))
    (r,) = call(
        residual_kernel,
        "residual",
        [FIELD],
        [pos, coef, d, v, r, w1, s1, s2, nb],
        scratch=[FIELD],
    )
    (load,) = call(
        load_kernel, "load", [(NY, NY)], [got.reshape(devices * SLOTS, NY), hot_t]
    )
    shape = (8, 8, 8, 1, 1, NY)
    return (x.reshape(shape), r.reshape(shape), load.reshape(NY, 1, 1, NY))


def solution(mesh):
    in_specs = (
        P(None, None, None, "row", "height", None),
        P("row", "height", None),
        P("row", "height", None),
        P(("row", "height"), None),
        P(("row", "height")),
        P(("row", "height")),
        P(("row", "height")),
    )
    out_specs = (
        P(None, None, None, "row", "height", None),
        P(None, None, None, "row", "height", None),
        P(None, "row", "height", None),
    )
    return jax.shard_map(shards, mesh=mesh, in_specs=in_specs, out_specs=out_specs, check_vma=False)
```

```python
import functools

import jax
import jax.numpy as jnp
import numpy as np
from jax import lax
from jax.experimental import pallas as pl
from jax.experimental.pallas import tpu as pltpu
from jax.sharding import PartitionSpec as P

ITERS = 8
HEAT_AIR = 0.02
HEAT_SOLID = 0.08
GLL_INNER = (
    -0.8717401485096066,
    -0.5917001814331423,
    -0.2092992179024789,
    0.2092992179024789,
    0.5917001814331423,
    0.8717401485096066,
)
F32 = jnp.float32
NX, NZ, NY = 8, 16, 128
FIELD = (8, 8, 8, NY)
FACE = (8, 8, NY)
COARSE = (NZ, NX, NY)


def legendre_values(points_in, degree):
    before = points_in * 0.0 + 1.0
    current = points_in * 1.0
    for order_now in range(1, degree):
        following = ((2 * order_now + 1) * points_in * current - order_now * before) / (
            order_now + 1
        )
        before = current
        current = following
    return current


def gll_tables():
    poly_order = 7
    gll_nodes = np.array((-1.0,) + GLL_INNER + (1.0,))
    edge_values = legendre_values(gll_nodes, poly_order)
    gll_weights = 2.0 / (poly_order * (poly_order + 1) * edge_values**2)
    diff_table = np.zeros((8, 8))
    for row_index in range(8):
        for col_index in range(8):
            if row_index != col_index:
                diff_table[row_index, col_index] = edge_values[row_index] / (
                    edge_values[col_index] * (gll_nodes[row_index] - gll_nodes[col_index])
                )
    diff_table[0, 0] = -poly_order * (poly_order + 1) / 4.0
    diff_table[7, 7] = poly_order * (poly_order + 1) / 4.0
    return (gll_weights, diff_table)


W_, D_ = gll_tables()
K_ = D_.T @ np.diag(W_) @ D_
S_ = np.sum(D_**2 * W_[:, None], axis=0)
W = [float(v) for v in W_]
SD = [float(v) for v in S_]
E = 7


def kvec(vals):
    k = lax.broadcasted_iota(jnp.int32, (8, NY), 0)
    out = jnp.full((8, NY), float(vals[0]), F32)
    for n in range(1, 8):
        out = jnp.where(k == n, jnp.float32(float(vals[n])), out)
    return out


def apply1d(v, mat):
    ev = [v[a] + v[7 - a] for a in range(4)]
    od = [v[a] - v[7 - a] for a in range(4)]
    out = [None] * 8
    for i in range(4):
        s = d = None
        for a in range(4):
            cs = float(0.5 * (mat[i, a] + mat[i, 7 - a]))
            cd = float(0.5 * (mat[i, a] - mat[i, 7 - a]))
            s = cs * ev[a] if s is None else s + cs * ev[a]
            d = cd * od[a] if d is None else d + cd * od[a]
        out[i] = s + d
        out[7 - i] = s - d
    return out


def place(pos_ref):
    ix, iz = pos_ref[0], pos_ref[1]
    has = (ix > 0, ix < NX - 1, iz > 0, iz < NZ - 1)
    frac = tuple(jnp.where(h, jnp.float32(0.5), jnp.float32(1.0)) for h in has)
    even = (lax.rem(ix, 2) == 0, lax.rem(iz, 2) == 0)
    return ix, iz, has, frac, even


def own_mult():
    k = lax.broadcasted_iota(jnp.int32, (8, NY), 0)
    y = lax.broadcasted_iota(jnp.int32, (8, NY), 1)
    shared = ((k == 0) & (y > 0)) | ((k == E) & (y < NY - 1))
    return jnp.where(shared, jnp.float32(0.5), jnp.float32(1.0))


def field_sum(get, frac):
    total = None
    for i in range(8):
        mid = get(i, 1)
        for j in range(2, 7):
            mid = mid + get(i, j)
        row = mid + frac[2] * get(i, 0) + frac[3] * get(i, E)
        if i == 0:
            row = frac[0] * row
        elif i == E:
            row = frac[1] * row
        total = row if total is None else total + row
    return total


def assemble_aisle(ref):
    low, high = ref[:, :, 0, :], ref[:, :, E, :]
    y = lax.broadcasted_iota(jnp.int32, FACE, 2)
    ref[:, :, 0, :] = low + jnp.where(y > 0, pltpu.roll(high, 1, 2), 0.0)
    ref[:, :, E, :] = high + jnp.where(y < NY - 1, pltpu.roll(low, NY - 1, 2), 0.0)


def add_faces_x(ref, got, has, even):
    a, b = got[0][...], got[1][...]
    ref[0] = ref[0] + jnp.where(has[0], jnp.where(even[0], b, a), 0.0)
    ref[E] = ref[E] + jnp.where(has[1], jnp.where(even[0], a, b), 0.0)


def add_faces_z(ref, got, has, even):
    a, b = got[0][...], got[1][...]
    ref[:, 0] = ref[:, 0] + jnp.where(has[2], jnp.where(even[1], b, a), 0.0)
    ref[:, E] = ref[:, E] + jnp.where(has[3], jnp.where(even[1], a, b), 0.0)


def put_pair(even, low, high, out):
    out[0][...] = jnp.where(even, high, low)
    out[1][...] = jnp.where(even, low, high)


def aisle_stiffness(block):
    turned = jnp.swapaxes(block, 0, 1)
    out = apply1d([turned[c] for c in range(8)], K_)
    return jnp.swapaxes(jnp.stack(out, axis=0), 0, 1)


def apply_ends(v, mat):
    s = d = None
    for a in range(4):
        p = float(0.5 * (mat[0, a] + mat[0, 7 - a])) * (v[a] + v[7 - a])
        m = float(0.5 * (mat[0, a] - mat[0, 7 - a])) * (v[a] - v[7 - a])
        s, d = (p, m) if s is None else (s + p, d + m)
    return s + d, s - d


def local_operator(z_ref, nb_ref, f_ref):
    wk = kvec(W)
    kt, ct = nb_ref[4], nb_ref[13]
    kw, cw = kt * wk, ct * wk
    for j in range(8):
        out = apply1d([z_ref[i, j] for i in range(8)], K_)
        kwj = kw * W[j]
        res = [kwj * out[i] for i in range(8)]
        for i in range(8):
            f_ref[i, j] = res[i]
    for i in range(8):
        block = z_ref[i]
        fx = [f_ref[i, j] for j in range(8)]
        zs = apply1d([block[j] for j in range(8)], K_)
        ys = aisle_stiffness(block)
        kwi = kw * W[i]
        res = [
            fx[j] + kwi * zs[j] + (W[i] * W[j]) * (kt * ys[j] + cw * block[j]) for j in range(8)
        ]
        for j in range(8):
            f_ref[i, j] = res[j]


def face_messages(z_ref, nb_ref, even, msgs):
    wk = kvec(W)
    kt, ct = nb_ref[4], nb_ref[13]
    kw, cw = kt * wk, ct * wk
    w0 = W[0]
    w00 = w0 * w0
    ends = [apply_ends([z_ref[i, j] for i in range(8)], K_) for j in range(8)]
    for n, i in enumerate((0, E)):
        block = z_ref[i]
        zs, ys = apply1d([block[j] for j in range(8)], K_), aisle_stiffness(block)
        res = [
            kw * (W[j] * ends[j][n] + w0 * zs[j]) + (w0 * W[j]) * (kt * ys[j] + cw * block[j])
            for j in range(8)
        ]
        for j, m in ((0, 3), (E, 5)):
            res[j] = (
                res[j]
                + nb_ref[m] * (w0 * wk * ends[j][n] + w00 * ys[j])
                + nb_ref[9 + m] * (w00 * wk * block[j])
            )
        up, down = (1, 0) if i == 0 else (0, 1)

        @pl.when(even[0])
        def _(res=res, to=up):
            for j in range(8):
                msgs[to][j] = res[j]

        @pl.when(jnp.logical_not(even[0]))
        def _(res=res, to=down):
            for j in range(8):
                msgs[to][j] = res[j]

    ends = [apply_ends([z_ref[i, j] for j in range(8)], K_) for i in range(8)]
    for n, j in enumerate((0, E)):
        block = z_ref[:, j]
        xs, ys = apply1d([block[i] for i in range(8)], K_), aisle_stiffness(block)
        res = [
            kw * (w0 * xs[i] + W[i] * ends[i][n]) + (W[i] * w0) * (kt * ys[i] + cw * block[i])
            for i in range(8)
        ]
        for i, m in ((0, 1), (E, 7)):
            res[i] = res[i] + nb_ref[m] * (w0 * wk * ends[i][n])
        up, down = (3, 2) if j == 0 else (2, 3)

        @pl.when(even[1])
        def _(res=res, to=up):
            for i in range(8):
                msgs[to][i] = res[i]

        @pl.when(jnp.logical_not(even[1]))
        def _(res=res, to=down):
            for i in range(8):
                msgs[to][i] = res[i]


def thomas(cf_ref, rhs):
    dp = []
    for h in range(NZ):
        v = rhs[h] if h == 0 else rhs[h] - cf_ref[h] * dp[h - 1]
        dp.append(v * cf_ref[32 + h])
    for h in range(NZ - 2, -1, -1):
        dp[h] = dp[h] - cf_ref[16 + h] * dp[h + 1]
    return dp


def coarse_dot(a, b):
    acc = None
    for u, v in zip(a, b):
        acc = u * v if acc is None else acc + u * v
    return spread_sum(acc)


def spread_sum(tile):
    row = jnp.broadcast_to(jnp.sum(tile, axis=0, keepdims=True), (8, NY))
    return jnp.broadcast_to(jnp.sum(row, axis=1, keepdims=True), (8, NY))


def shift_pair(v, axis):
    n = v.shape[axis]
    p = lax.broadcasted_iota(jnp.int32, v.shape, axis)
    before = jnp.where(p == 0, v, pltpu.roll(v, 1, axis))
    after = jnp.where(p == n - 1, v, pltpu.roll(v, n - 1, axis))
    return before, after


MID, FACE_MU = 2.0 - 2.0 * W[0], 2.0 * W[0]
SYM_F = (MID / (2.0 * FACE_MU)) ** 0.5
SYM_M = -((FACE_MU / (2.0 * MID)) ** 0.5)
A0, B0 = (MID + FACE_MU / 2.0) / 2.0**0.5, FACE_MU / (4.0 * 2.0**0.5)
A1, B1 = -SYM_F * FACE_MU / 2.0, SYM_F * FACE_MU / 4.0
C2 = FACE_MU**0.5 / 4.0
LAM = (
    0.0,
    float(2.0 * (K_[0, 0] + K_[0, 7])) * (SYM_F - SYM_M) ** 2,
    float(2.0 * (K_[0, 0] - K_[0, 7])) / FACE_MU,
)


def spread3(v, before, after):
    both = before + after
    return (A0 * v + B0 * both, A1 * v + B1 * both, C2 * (before - after))


def back3(duals):
    t, u = B0 * duals[0] + B1 * duals[1], C2 * duals[2]
    return A0 * duals[0] + A1 * duals[1], t + u, t - u


def gather3(duals, axis):
    own, g, h = back3(duals)
    n = own.shape[axis]
    p = lax.broadcasted_iota(jnp.int32, own.shape, axis)
    up = jnp.where(p == n - 1, h, pltpu.roll(g, n - 1, axis))
    down = jnp.where(p == 0, g, pltpu.roll(h, 1, axis))
    return own + (up + down)


def coarse_operator(d, kc_ref, cc_ref, tmp_ref):
    for h in range(NZ):
        ys = spread3(d[h], *shift_pair(d[h], 1))
        for c in range(3):
            xs = spread3(ys[c], *shift_pair(ys[c], 0))
            for a in range(3):
                tmp_ref[(a * 3 + c) * NZ + h] = xs[a]
    keys = [(a, c) for a in range(3) for c in range(3)]
    res, kept, after = [], {}, {}

    def finish(vals):
        return gather3([gather3([vals[a, c] for a in range(3)], 0) for c in range(3)], 1)

    for h in range(NZ):
        lo, hi = max(h - 1, 0), min(h + 1, NZ - 1)
        kh, ch = kc_ref[h], cc_ref[h]
        factor, final = {}, {}
        for a, c in keys:
            base = (a * 3 + c) * NZ
            zs = spread3(tmp_ref[base + h], tmp_ref[base + lo], tmp_ref[base + hi])
            duals = []
            for b in range(3):
                kind = tuple(sorted((a, b, c)))
                if kind not in factor:
                    lam = sum(LAM[n] for n in kind)
                    factor[kind] = kh * lam + ch if lam else ch
                duals.append(factor[kind] * zs[b])
            own, g, hh = back3(duals)
            if h > 0:
                final[a, c] = kept[a, c] + g
                own = own + after[a, c]
            else:
                own = own + g
            if h == NZ - 1:
                own = own + hh
            kept[a, c], after[a, c] = own, hh
        if h > 0:
            res.append(finish(final))
    res.append(finish(kept))
    return res


def coarse_row(ref, ix, iz, dx, dz):
    x = jnp.clip(ix + dx, 0, NX - 1)
    z = jnp.clip(iz + dz, 0, NZ - 1)
    return ref[z, pl.ds(x, 1), :]


def aisle_tiles(row, want_stiff):
    c = jnp.broadcast_to(row, (8, NY))
    before, after = shift_pair(c, 1)
    k = lax.broadcasted_iota(jnp.int32, (8, NY), 0)
    low, high = 0.5 * (c + before), 0.5 * (c + after)
    tile = jnp.where(k == 0, low, jnp.where(k == E, high, c))
    if not want_stiff:
        return tile, None
    return tile, kvec(K_[:, 0]) * (low - c) + kvec(K_[:, 7]) * (high - c)


def classes(tiles, reach):
    n = 2 * reach + 1
    m = 2 * n - 3

    def line(vals):
        out = []
        for p in range(m):
            if p % 2 == 0:
                out.append(0.5 * (vals[p // 2] + vals[p // 2 + 1]))
            else:
                out.append(vals[p // 2 + 1])
        return out

    cols = [line(tiles[dx]) for dx in range(n)]
    by_q = [line([cols[dx][q] for dx in range(n)]) for q in range(m)]
    return [[by_q[q][p] for q in range(m)] for p in range(m)]


def cls(i):
    return 0 if i == 0 else (2 if i == E else 1)


def own_prolong(ref, ix, iz):
    tiles = [
        [aisle_tiles(coarse_row(ref, ix, iz, dx, dz), False)[0] for dz in (-1, 0, 1)]
        for dx in (-1, 0, 1)
    ]
    return classes(tiles, 1)


def add_operator_of_prolong(ref, ix, iz, nb_ref, out_ref):
    tv, ty = [], []
    for dx in range(-2, 3):
        pair = [aisle_tiles(coarse_row(ref, ix, iz, dx, dz), True) for dz in range(-2, 3)]
        tv.append([p[0] for p in pair])
        ty.append([p[1] for p in pair])
    v, yv = classes(tv, 2), classes(ty, 2)
    wk = kvec(W)

    def parts(ex, ez):
        p, q = 2 + 2 * ex, 2 + 2 * ez
        n = (ex + 1) * 3 + ez + 1
        kt, ct = nb_ref[n], nb_ref[9 + n]
        kw, cw = kt * wk, ct * wk
        memo = {}

        def once(key, make):
            if key not in memo:
                memo[key] = make()
            return memo[key]

        def along(i, a, b, c):
            return kw * (float(K_[i, 0]) * (a - b) + float(K_[i, 7]) * (c - b))

        def tile(i, j):
            a, b = cls(i), cls(j)
            xt = once(
                ("x", i, b), lambda: along(i, v[p][q + b], v[p + 1][q + b], v[p + 2][q + b])
            )
            zt = once(
                ("z", a, j), lambda: along(j, v[p + a][q], v[p + a][q + 1], v[p + a][q + 2])
            )
            yt = once(("y", a, b), lambda: kt * yv[p + a][q + b] + cw * v[p + a][q + b])
            return W[j] * xt + W[i] * zt + (W[i] * W[j]) * yt

        return tile

    part = {(ex, ez): parts(ex, ez) for ex in (-1, 0, 1) for ez in (-1, 0, 1)}
    for i in range(8):
        new = []
        for j in range(8):
            acc = out_ref[i, j] + part[0, 0](i, j)
            ex = -1 if i == 0 else (1 if i == E else 0)
            ez = -1 if j == 0 else (1 if j == E else 0)
            if ex:
                acc = acc + part[ex, 0](7 - i, j)
            if ez:
                acc = acc + part[0, ez](i, 7 - j)
            if ex and ez:
                acc = acc + part[ex, ez](7 - i, 7 - j)
            new.append(acc)
        for j in range(8):
            out_ref[i, j] = new[j]
    return [[v[2 + a][2 + b] for b in range(3)] for a in range(3)]


def make_z(c_ref, ix, iz, r_ref, dinv_ref, z_ref):
    pc = own_prolong(c_ref, ix, iz)
    for i in range(8):
        new = [r_ref[i, j] * dinv_ref[i, j] + pc[cls(i)][cls(j)] for j in range(8)]
        for j in range(8):
            z_ref[i, j] = new[j]


def coarse_rows_of(got_ref, which):
    return [got_ref[pl.ds(4 * h + which, NX, stride=4 * NZ), :] for h in range(NZ)]


def heat_kernel(pos, heat, f, ma, mb):
    _, _, _, _, even = place(pos)
    wk = kvec(W)
    for i in range(8):
        new = [(W[i] * W[j]) * wk * heat[i, j] for j in range(8)]
        for j in range(8):
            f[i, j] = new[j]
    put_pair(even[0], f[0], f[E], (ma, mb))


def heat_z_kernel(pos, f, rb, ra, out, ma, mb):
    _, _, has, _, even = place(pos)
    out[...] = f[...]
    add_faces_x(out, (ra, rb), has, even)
    put_pair(even[1], out[:, 0], out[:, E], (ma, mb))


def first_rows_kernel(pos, f, rb, ra, both, out, rows):
    _, _, has, frac, even = place(pos)
    out[...] = f[...]
    add_faces_z(out, (ra, rb), has, even)
    assemble_aisle(out)
    tile = field_sum(lambda i, j: out[i, j], frac) * own_mult()
    restricted = jnp.sum(tile, axis=0, keepdims=True)
    cap = jnp.where(both[1:2] == 1.0, jnp.float32(HEAT_SOLID), jnp.float32(HEAT_AIR))
    block = jnp.concatenate([both[0:1], cap, restricted, jnp.zeros((1, NY), F32)], axis=0)
    rows[...] = jnp.broadcast_to(block[None], rows.shape)


def setup_kernel(
    pos, got, r, kc, cc, cf, rc, nb, dinv, z, m0, m1, m2, m3, c_tmp
):
    ix, iz, has, frac, even = place(pos)
    k_all, c_all, r_all = (coarse_rows_of(got, n) for n in range(3))
    for h in range(NZ):
        kc[h], cc[h], rc[h] = k_all[h], c_all[h], r_all[h]
    link = [2.0 * k_all[h] * k_all[h + 1] / (k_all[h] + k_all[h + 1]) for h in range(NZ - 1)]
    above = None
    for h in range(NZ):
        main = 8.0 * c_all[h]
        if h > 0:
            main = main + link[h - 1]
        if h < NZ - 1:
            main = main + link[h]
        low = -link[h - 1] if h > 0 else jnp.zeros((NX, NY), F32)
        piv = main if h == 0 else main - low * above
        inv = 1.0 / piv
        above = -link[h] * inv if h < NZ - 1 else jnp.zeros((NX, NY), F32)
        cf[h], cf[16 + h], cf[32 + h] = low, above, inv
    for ex in (-1, 0, 1):
        for ez in (-1, 0, 1):
            n = (ex + 1) * 3 + ez + 1
            there = None
            if ex:
                there = has[0] if ex < 0 else has[1]
            if ez:
                hz = has[2] if ez < 0 else has[3]
                there = hz if there is None else there & hz
            for base, src in ((0, kc), (9, cc)):
                tile = jnp.broadcast_to(coarse_row(src, ix, iz, ex, ez), (8, NY))
                nb[base + n] = tile if there is None else jnp.where(there, tile, 0.0)
    wk, sk = kvec(W), kvec(SD)
    for i in range(8):
        for j in range(8):
            ex = -1 if i == 0 else (1 if i == E else 0)
            ez = -1 if j == 0 else (1 if j == E else 0)
            kt, ct = nb[4], nb[13]
            for n in {4 + 3 * ex, 4 + ez, 4 + 3 * ex + ez} - {4}:
                kt, ct = kt + nb[n], ct + nb[9 + n]
            dinv[i, j] = (
                kt * ((SD[i] * W[j] + W[i] * SD[j]) * wk + (W[i] * W[j]) * sk)
                + ct * ((W[i] * W[j]) * wk)
            )
    assemble_aisle(dinv)
    dinv[...] = 1.0 / dinv[...]
    solved = thomas(cf, r_all)
    for h in range(NZ):
        c_tmp[h] = solved[h]
    make_z(c_tmp, ix, iz, r, dinv, z)
    face_messages(z, nb, even, (m0, m1, m2, m3))


def inner_kernel(pos, f, r3, r1, r2, r0, nb, dinv, *refs):
    w1, t, m0, m1, m2, m3 = refs[-6:]
    _, _, has, _, even = place(pos)
    w1[...] = f[...]
    add_faces_x(w1, (r0, r1), has, even)
    add_faces_z(w1, (r2, r3), has, even)
    assemble_aisle(w1)
    t[...] = w1[...] * dinv[...]
    face_messages(t, nb, even, (m0, m1, m2, m3))


def dots_kernel(first, *refs):
    if first:
        pos, z, r, t, w1, lines = refs
    else:
        pos, z, r, t, w1, s1, s2, lines = refs
    _, _, _, frac, _ = place(pos)
    my = own_mult()
    zero = jnp.zeros((1, NY), F32)

    def dot(a, b):
        tile = my * field_sum(lambda i, j: a[i, j] * b[i, j], frac)
        return jnp.sum(tile, axis=0, keepdims=True)

    out = [dot(z, r), dot(t, r), dot(z, w1), dot(t, w1), zero]
    out += [zero] * 4 if first else [dot(z, s1), dot(z, s2), dot(t, s1), dot(t, s2)]
    out += [zero] * 6
    out.append(jnp.sum(field_sum(lambda i, j: w1[i, j], frac) * my, axis=0, keepdims=True))
    lines[...] = jnp.concatenate(out, axis=0)


def rows_kernel(first, *refs):
    if first:
        pos, f2, r2, r0, r3, r1, t, lines, owners, v, rows = refs
    else:
        pos, f2, r3, r1, r2, r0, t, lines, v, rows = refs
    _, _, has, frac, even = place(pos)
    v[...] = f2[...]
    add_faces_x(v, (r0, r1), has, even)
    add_faces_z(v, (r2, r3), has, even)
    my = own_mult()
    tv = jnp.sum(field_sum(lambda i, j: t[i, j] * v[i, j], frac), axis=0, keepdims=True)
    lane = lax.broadcasted_iota(jnp.int32, (16, NY), 1)
    at = lax.broadcasted_iota(jnp.int32, (16, NY), 0)
    stacked = jnp.where(at == 4, jnp.broadcast_to(tv, (16, NY)), lines[...])
    totals = jnp.broadcast_to(jnp.sum(stacked, axis=1, keepdims=True), (16, NY))
    dots = jnp.sum(jnp.where(lane == at, totals, 0.0), axis=0, keepdims=True)
    vt = field_sum(lambda i, j: v[i, j], frac)
    k = lax.broadcasted_iota(jnp.int32, (8, NY), 0)
    y = lax.broadcasted_iota(jnp.int32, (8, NY), 1)
    vlow = jnp.broadcast_to(vt[0:1], (8, NY))
    vhigh = jnp.broadcast_to(vt[7:8], (8, NY))
    vt = vt + jnp.where((k == 0) & (y > 0), pltpu.roll(vhigh, 1, 1), 0.0)
    vt = vt + jnp.where((k == E) & (y < NY - 1), pltpu.roll(vlow, NY - 1, 1), 0.0)
    g2 = jnp.sum(vt * my, axis=0, keepdims=True)
    block = jnp.concatenate([lines[15:16], g2, dots, jnp.zeros((1, NY), F32)], axis=0)
    rows[...] = jnp.broadcast_to(block[None], rows.shape)
    if first:
        rows[:, 3, :] = owners[...]


def coefficients(first, got, d, q, rc, rs, wp, cf):
    total = got[0:8]
    for n in range(8, NX * NZ * 4, 8):
        total = total + got[n : n + 8]
    dots = jnp.broadcast_to(total[2:3] + total[6:7], (8, NY))
    lane = lax.broadcasted_iota(jnp.int32, (8, NY), 1)

    def pick(n):
        return jnp.broadcast_to(
            jnp.sum(jnp.where(lane == n, dots, 0.0), axis=1, keepdims=True), (8, NY)
        )

    g1, g2 = coarse_rows_of(got, 0), coarse_rows_of(got, 1)
    b1, b2 = pick(0), pick(1) + coarse_dot(d, [rc[h] for h in range(NZ)])
    w11 = pick(2)
    w12 = pick(3) + coarse_dot(d, g1)
    w22 = pick(4) + 2.0 * coarse_dot(d, g2) + coarse_dot(d, q)
    e = [None] * 4
    if not first:
        rs1, rs2 = [rs[h] for h in range(NZ)], [rs[NZ + h] for h in range(NZ)]
        c11, c21 = pick(5), pick(6)
        c12, c22 = pick(7) + coarse_dot(d, rs1), pick(8) + coarse_dot(d, rs2)
        pa, pb, pc = wp[6], wp[7], wp[8]
        inv = -1.0 / (pa * pc - pb * pb)
        e11, e21 = (pc * c11 - pb * c21) * inv, (pa * c21 - pb * c11) * inv
        e12, e22 = (pc * c12 - pb * c22) * inv, (pa * c22 - pb * c12) * inv
        w11 = w11 + c11 * e11 + c21 * e21
        w12 = w12 + c11 * e12 + c21 * e22
        w22 = w22 + c12 * e12 + c22 * e22
        e = [e11, e21, e12, e22]
    inv = 1.0 / (w11 * w22 - w12 * w12)
    a1 = (w22 * b1 - w12 * b2) * inv
    a2 = (w11 * b2 - w12 * b1) * inv
    return a1, a2, e, (w11, w12, w22), g1, g2


def new_residual(first, a1, a2, x1, x2, r, w1, ay, s1, s2, out):
    for i in range(8):
        new = []
        for j in range(8):
            v = r[i, j] - (a1 * w1[i, j] + a2 * ay[i, j])
            if not first:
                v = v - (x1 * s1[i, j] + x2 * s2[i, j])
            new.append(v)
        for j in range(8):
            out[i, j] = new[j]


def step_kernel(first, *refs):
    refs = list(refs)
    take = lambda n: [refs.pop(0) for _ in range(n)]
    pos, got, r, w1, v, dinv, nb, kc, cc, cf, rc = take(11)
    s1 = s2 = rs = wp = None
    if not first:
        s1, s2, rs, wp = take(4)
    ro, rco, zo, m0, m1, m2, m3, co, ay, pdo, qo = take(11)
    c_tmp, tmp = take(2)
    ix, iz, has, frac, even = place(pos)
    d = thomas(cf, coarse_rows_of(got, 0))
    for h in range(NZ):
        c_tmp[h] = d[h]
    q = coarse_operator(d, kc, cc, tmp)
    a1, a2, e, w, g1, g2 = coefficients(first, got, d, q, rc, rs, wp, cf)
    x1 = x2 = None
    if not first:
        x1, x2 = a1 * e[0] + a2 * e[2], a1 * e[1] + a2 * e[3]
    for n, val in enumerate((a1, a2, *e, *w)):
        if val is not None:
            co[n] = val
        else:
            co[n] = jnp.zeros((8, NY), F32)
    ay[...] = v[...]
    pd = add_operator_of_prolong(c_tmp, ix, iz, nb, ay)
    for n in range(9):
        pdo[n] = pd[n // 3][n % 3]
    assemble_aisle(ay)
    new_residual(first, a1, a2, x1, x2, r, w1, ay, s1, s2, ro)
    rnew = []
    for h in range(NZ):
        qo[h] = q[h]
        new = rc[h] - (a1 * g1[h] + a2 * (g2[h] + q[h]))
        if not first:
            new = new - (x1 * rs[h] + x2 * rs[NZ + h])
        rco[h] = new
        rnew.append(new)
    solved = thomas(cf, rnew)
    for h in range(NZ):
        c_tmp[h] = solved[h]
    make_z(c_tmp, ix, iz, ro, dinv, zo)
    face_messages(zo, nb, even, (m0, m1, m2, m3))


def new_x(first, a1, a2, x1, x2, z, t, pd, p1, p2, x, out):
    for i in range(8):
        new = []
        for j in range(8):
            up = a1 * z[i, j] + a2 * (t[i, j] + pd(i, j))
            if not first:
                up = x[i, j] + (up + (x1 * p1[i, j] + x2 * p2[i, j]))
            new.append(up)
        for j in range(8):
            out[i, j] = new[j]


def late_kernel(first, *refs):
    refs = list(refs)
    take = lambda n: [refs.pop(0) for _ in range(n)]
    got, z, t, w1, ay, co, pdt, q = take(8)
    x = p1 = p2 = s1 = s2 = rs = None
    if not first:
        x, p1, p2, s1, s2, rs = take(6)
    xo, p1o, p2o, s1o, s2o, rso = take(6)
    a1, a2, e11, e21, e12, e22 = (co[n] for n in range(6))
    x1, x2 = a1 * e11 + a2 * e12, a1 * e21 + a2 * e22
    pd = lambda i, j: pdt[3 * cls(i) + cls(j)]
    new_x(first, a1, a2, x1, x2, z, t, pd, p1, p2, x, xo)

    def block(one, two, prev1, prev2, out1, out2):
        for i in range(8):
            new = []
            for j in range(8):
                n1, n2 = one(i, j), two(i, j)
                if not first:
                    u, w = prev1[i, j], prev2[i, j]
                    n1, n2 = n1 + e11 * u + e21 * w, n2 + e12 * u + e22 * w
                new.append((n1, n2))
            for j in range(8):
                out1[i, j], out2[i, j] = new[j]

    block(lambda i, j: z[i, j], lambda i, j: t[i, j] + pd(i, j), p1, p2, p1o, p2o)
    block(lambda i, j: w1[i, j], lambda i, j: ay[i, j], s1, s2, s1o, s2o)
    g1, g2 = coarse_rows_of(got, 0), coarse_rows_of(got, 1)
    for h in range(NZ):
        n1, n2 = g1[h], g2[h] + q[h]
        if not first:
            u, w = rs[h], rs[NZ + h]
            n1, n2 = n1 + e11 * u + e21 * w, n2 + e12 * u + e22 * w
        rso[h], rso[NZ + h] = n1, n2


def last_kernel(pos, got, z, t, nb, kc, cc, cf, rc, x, p1, p2, rs, wp, table, xo, send, co, dc, tmp):
    ix, iz, _, _, _ = place(pos)
    d = thomas(cf, coarse_rows_of(got, 0))
    for h in range(NZ):
        dc[h] = d[h]
    q = coarse_operator(d, kc, cc, tmp)
    a1, a2, e, _, _, _ = coefficients(False, got, d, q, rc, rs, wp, cf)
    x1, x2 = a1 * e[0] + a2 * e[2], a1 * e[1] + a2 * e[3]
    for n, val in enumerate((a1, a2, x1, x2)):
        co[n] = val
    own = own_prolong(dc, ix, iz)
    pd = lambda i, j: own[cls(i)][cls(j)]
    new_x(False, a1, a2, x1, x2, z, t, pd, p1, p2, x, xo)
    put_rows(xo, nb, table, send)


def residual_kernel(pos, co, dc, v, r, w1, s1, s2, nb, ro, ay):
    ix, iz, _, _, _ = place(pos)
    ay[...] = v[...]
    add_operator_of_prolong(dc, ix, iz, nb, ay)
    assemble_aisle(ay)
    new_residual(False, co[0], co[1], co[2], co[3], r, w1, ay, s1, s2, ro)


NT = (((1,), (1,)), ((), ()))
SLOTS = 16


def slots_kernel(ints, table, owners):
    own, elem, side, target = (ints[n : n + 1] for n in range(4))
    faces = own.shape[1]
    row = own.astype(F32)
    col = jnp.broadcast_to(row, (NY, faces)).T
    ranks = []
    for s in range(0, faces, NY):
        f = lax.broadcasted_iota(jnp.int32, (faces, NY), 0)
        g = lax.broadcasted_iota(jnp.int32, (faces, NY), 1) + s
        same = (col == row[:, s : s + NY]) & (f < g)
        ranks.append(jnp.sum(jnp.where(same, 1.0, 0.0), axis=0, keepdims=True))
    rank = jnp.concatenate(ranks, axis=1)
    slot = row * SLOTS + rank
    vals = jnp.concatenate(
        [elem.astype(F32) + 1.0, side.astype(F32), jnp.zeros((6, faces), F32)], axis=0
    ).astype(jnp.bfloat16)
    step = 256
    for s in range(0, table.shape[0], step):
        at = lax.broadcasted_iota(jnp.int32, (step, faces), 0).astype(F32) + float(s)
        hot = jnp.where(at == slot, 1.0, 0.0).astype(jnp.bfloat16)
        got = lax.dot_general(hot, vals, NT, preferred_element_type=F32)
        pick = got[:, 0:1] - 1.0 + 128.0 * got[:, 1:2]
        lane = lax.broadcasted_iota(jnp.int32, (step, table.shape[1]), 1).astype(F32)
        table[s : s + step] = jnp.where(lane == pick, 1.0, 0.0).astype(jnp.bfloat16)
    devices = owners.shape[0]
    dev = lax.broadcasted_iota(jnp.int32, (devices, faces), 0).astype(F32)
    hot = jnp.where(dev == row, 1.0, 0.0).astype(jnp.bfloat16)
    at = lax.broadcasted_iota(jnp.int32, (128, faces), 0).astype(F32)
    marked = jnp.where(at == rank, target.astype(F32) + 1.0, 0.0).astype(jnp.bfloat16)
    owners[...] = lax.dot_general(hot, marked, NT, preferred_element_type=F32) - 1.0


def owners_kernel(got, hot_t):
    devices = got.shape[0] // 4
    lane = lax.broadcasted_iota(jnp.int32, (SLOTS, NY), 1)
    at = lax.broadcasted_iota(jnp.int32, (SLOTS, NY), 0)
    ones = jnp.ones((NY, NY), jnp.bfloat16)
    step = 8
    for d in range(0, devices, step):
        rows = [
            jnp.where(lane == at, jnp.broadcast_to(got[4 * (d + n) + 3 : 4 * (d + n) + 4], (SLOTS, NY)), 0.0)
            for n in range(step)
        ]
        block = jnp.concatenate(rows, axis=0).astype(jnp.bfloat16)
        col = jnp.dot(block, ones, preferred_element_type=F32)
        elem = lax.broadcasted_iota(jnp.int32, col.shape, 1).astype(F32)
        hot = jnp.where(col == elem, 1.0, 0.0)
        hot_t[:, d * SLOTS : (d + step) * SLOTS] = hot.T.astype(jnp.bfloat16)


def split(v):
    high = v.astype(jnp.bfloat16)
    return high, (v - high.astype(F32)).astype(jnp.bfloat16)


def put_rows(x, nb, table, send):
    kt = nb[4]

    def weighted(get, row):
        acc = None
        for a in range(8):
            term = float(D_[row, a]) * get(a)
            acc = term if acc is None else acc + term
        return acc

    getters = (lambda a: x[a], lambda a: x[:, a], lambda a: x[:, :, a, :])
    his, los = [], []
    for get in getters:
        for end, sign in ((0, 1.0), (E, -1.0)):
            flux = weighted(get, end) * (sign * kt)[None]
            block = jnp.concatenate(
                [flux.reshape(64, NY), get(end).reshape(64, NY)], axis=0
            )
            h, l = split(block)
            his.append(h)
            los.append(l)
    both = jnp.concatenate(
        [jnp.concatenate(his, axis=1), jnp.concatenate(los, axis=1)], axis=0
    )
    step = 512
    for s in range(0, send.shape[0], step):
        out = lax.dot_general(table[s : s + step], both, NT, preferred_element_type=F32)
        send[s : s + step] = out[:, :NY] + out[:, NY:]


def load_kernel(got, hot_t, out):
    acc = None
    step = 512
    for s in range(0, got.shape[0], step):
        both = jnp.concatenate(split(got[s : s + step]), axis=1)
        term = jnp.dot(hot_t[:, s : s + step], both, preferred_element_type=F32)
        acc = term if acc is None else acc + term
    out[...] = (acc[:, :NY] + acc[:, NY:]).T


def call(body, name, outs, args, scratch=()):
    vmem = pl.BlockSpec(memory_space=pltpu.VMEM)
    smem = pl.BlockSpec(memory_space=pltpu.SMEM)
    shape = lambda o: o if isinstance(o[0], tuple) else (o, F32)
    scalars = lambda a: a.dtype == jnp.int32 and a.shape == (2,)
    return pl.pallas_call(
        body,
        out_shape=[jax.ShapeDtypeStruct(*shape(o)) for o in outs],
        in_specs=[smem if scalars(a) else vmem for a in args],
        out_specs=[vmem] * len(outs),
        scratch_shapes=[pltpu.VMEM(s, F32) for s in scratch],
        compiler_params=pltpu.CompilerParams(vmem_limit_bytes=24 * 1024 * 1024),
        cost_estimate=pl.CostEstimate(
            flops=2_000_000, bytes_accessed=1 << 20, transcendentals=0
        ),
        name=name,
    )(*args)


def pairs(axis, second):
    out = []
    for x in range(NX):
        for z in range(NZ):
            here = [x, z]
            n, last = here[axis], (NX, NZ)[axis] - 1
            if not second:
                here[axis] = n ^ 1
            elif n in (0, last):
                here[1 - axis] ^= 1
            else:
                here[axis] = n + 1 if n % 2 else n - 1
            out.append((x * NZ + z, here[0] * NZ + here[1]))
    return out


def swap(pair, axis):
    return [lax.ppermute(v, ("row", "height"), pairs(axis, n == 1)) for n, v in enumerate(pair)]


def swap_x(pair):
    return swap(pair, 0)


def swap_z(pair):
    return swap(pair, 1)


def halo(msgs, order=(3, 1, 2, 0)):
    got = swap_x(msgs[:2]) + swap_z(msgs[2:])
    return [got[n] for n in order]


def everywhere(rows):
    return lax.all_to_all(rows, ("row", "height"), split_axis=0, concat_axis=0, tiled=True)


def shards(heat, conductivity, marks, face_owner, face_element, face_side, owner_element):
    devices = NX * NZ
    pos = jnp.stack([lax.axis_index("row"), lax.axis_index("height")]).astype(jnp.int32)
    f, ma, mb = call(heat_kernel, "heat", [FIELD, FACE, FACE], [pos, heat.reshape(FIELD)])
    ra, rb = swap_x((ma, mb))
    both = jnp.stack([conductivity.reshape(-1), marks.reshape(-1).astype(F32)])
    ints = jnp.stack([face_owner.reshape(-1), face_element, face_side, owner_element])
    table, owners = call(
        slots_kernel,
        "slots",
        [((devices * SLOTS, 6 * NY), jnp.bfloat16), (devices, 128)],
        [ints],
    )
    f, ma, mb = call(heat_z_kernel, "heat_z", [FIELD, FACE, FACE], [pos, f, rb, ra])
    ra, rb = swap_z((ma, mb))
    r, rows = call(
        first_rows_kernel,
        "first_rows",
        [FIELD, (devices, 4, NY)],
        [pos, f, rb, ra, both],
    )
    got0 = everywhere(rows).reshape(devices * 4, NY)
    kc, cc, cf, rc, nb, dinv, z, *msgs = call(
        setup_kernel,
        "setup",
        [COARSE, COARSE, (48, NX, NY), COARSE, (18, 8, NY), FIELD, FIELD] + [FACE] * 4,
        [pos, got0, r],
        scratch=[COARSE],
    )
    x = p1 = p2 = s1 = s2 = rs = co = None
    for outer in range(ITERS // 2):
        first, last = outer == 0, outer == ITERS // 2 - 1
        got = halo(msgs)
        (f,) = call(local_operator, "apply", [FIELD], [z, nb])
        w1, t, *msgs = call(
            inner_kernel,
            "inner",
            [FIELD] * 2 + [FACE] * 4,
            [pos, f, *got, nb, dinv] + ([] if first else [rs]),
        )
        got = halo(msgs, (2, 0, 3, 1)) if first else halo(msgs)
        (f2,) = call(local_operator, "apply", [FIELD], [t, nb])
        (lines,) = call(
            functools.partial(dots_kernel, first),
            "dots",
            [(16, NY)],
            [pos, z, r, t, w1] + ([] if first else [s1, s2]),
        )
        v, rows = call(
            functools.partial(rows_kernel, first),
            "rows",
            [FIELD, (devices, 4, NY)],
            [pos, f2, *got, t, lines] + ([owners] if first else []),
        )
        rows = everywhere(rows).reshape(devices * 4, NY)
        if first:
            (hot_t,) = call(
                owners_kernel, "owners", [((NY, devices * SLOTS), jnp.bfloat16)], [rows]
            )
        if last:
            break
        rn, rcn, zn, *msgs, con, ay, pd, q = call(
            functools.partial(step_kernel, first),
            "step",
            [FIELD, COARSE, FIELD]
            + [FACE] * 4
            + [(9, 8, NY), FIELD, (9, 8, NY), COARSE],
            [pos, rows, r, w1, v, dinv, nb, kc, cc, cf, rc] + ([] if first else [s1, s2, rs, co]),
            scratch=[COARSE, (9 * NZ, NX, NY)],
        )
        x, p1, p2, s1, s2, rs = call(
            functools.partial(late_kernel, first),
            "late",
            [FIELD] * 5 + [(2 * NZ, NX, NY)],
            [rows, z, t, w1, ay, con, pd, q] + ([] if first else [x, p1, p2, s1, s2, rs]),
        )
        r, rc, z, co = rn, rcn, zn, con
    x, send, coef, d = call(
        last_kernel,
        "last",
        [FIELD, (devices * SLOTS, NY), (4, 8, NY), COARSE],
        [pos, rows, z, t, nb, kc, cc, cf, rc, x, p1, p2, rs, co, table],
        scratch=[(9 * NZ, NX, NY)],
    )
    got = everywhere(send.reshape(devices, SLOTS, NY))
    (r,) = call(
        residual_kernel,
        "residual",
        [FIELD],
        [pos, coef, d, v, r, w1, s1, s2, nb],
        scratch=[FIELD],
    )
    (load,) = call(
        load_kernel, "load", [(NY, NY)], [got.reshape(devices * SLOTS, NY), hot_t]
    )
    shape = (8, 8, 8, 1, 1, NY)
    return (x.reshape(shape), r.reshape(shape), load.reshape(NY, 1, 1, NY))


def solution(mesh):
    in_specs = (
        P(None, None, None, "row", "height", None),
        P("row", "height", None),
        P("row", "height", None),
        P(("row", "height"), None),
        P(("row", "height")),
        P(("row", "height")),
        P(("row", "height")),
    )
    out_specs = (
        P(None, None, None, "row", "height", None),
        P(None, None, None, "row", "height", None),
        P(None, "row", "height", None),
    )
    return jax.shard_map(shards, mesh=mesh, in_specs=in_specs, out_specs=out_specs, check_vma=False)
```
